128 devices in a mesh: wide: 64 (over z, y, x), narrow: 2 (over core).
Axes of the slice: x: 4, y: 4, z: 4, core: 2. Of those that a mesh axis runs over, the one named last changes fastest.
Arguments:
- grid_state: bfloat16 [262144, 100], P(('wide', 'narrow')), may hold values from -6 to 6
- latent_init: bfloat16 [32768, 1024], P(('wide', 'narrow')), may hold values from -6 to 6
- enc_src: int32 [32768, 16], P(('wide', 'narrow')), may hold values from 0 to 4095, as said below
- enc_count: int32 [32768], P(('wide', 'narrow')), may hold values from 4 to 16
- dec_src: int32 [262144, 3], P(('wide', 'narrow')), may hold values from 0 to 32767, as said below
- w_in: bfloat16 [100, 1024], replicated, may hold values from -0.625 to 0.625
- enc_w: bfloat16 [4, 1024, 1024], replicated, may hold values from -0.1875 to 0.1875
- proc_w: bfloat16 [4, 1024, 1024], replicated, may hold values from -0.1875 to 0.1875
- dec_w: bfloat16 [4, 1024, 1024], replicated, may hold values from -0.1875 to 0.1875
- w_out: bfloat16 [1024, 100], replicated, may hold values from -0.1875 to 0.1875
- logit_scale: float32 [3, 16], replicated, may hold values from 0.5 to 3
Outputs:
- tendency: bfloat16 [262144, 100], P(('wide', 'narrow'))
The draws below stay inside these ranges and needn't reach their ends.
Inputs may be any that keep to these rules, and one draw needn't show every extreme that they name: Row i, with d = i // 256, names grid point d * 2048 - 1024 + enc_src[i, e], which always lies in the grid; slots at or past enc_count[i] are padding. `dec_src`: row g, with d = g // 2048, names latent nodes from d * 256 - 128 to (d + 1) * 256 + 127, clipped to the latent nodes.
All inputs are finite; a program needn't handle non-finite values.
Results may differ from the reference program's by a relative error of at most 0.025.
Values may be sent and summed in bfloat16 or wider, within the bound.
No kernel may reach another device: no remote copies, remote signals or barrier semaphores. Data moves between devices by JAX's collectives and lax.ppermute only.
A program may use at most 256 MiB of HBM per device.

```python
import math
import jax
import jax.numpy as jnp
from jax import lax

H = 1024
HEADS = 16
CH = 100
K_ENC = 16
K_DEC = 3
WIN = 512
BG = 1024
BL = 128
RATIO = 8
LAT_DEV = 256
GRID_DEV = 2048
LAT = 32768
GRID = 262144


def draw_enc_src(key, part):
    key = jax.random.fold_in(key, 11)
    node = jnp.arange(LAT, dtype=jnp.int32)
    center = node * RATIO
    offset = jax.random.randint(key, (LAT, K_ENC), -BG, BG + RATIO, dtype=jnp.int32)
    local = node % LAT_DEV
    first = jnp.where(local == 0, -BG, jnp.where(local == LAT_DEV - 1, BG + RATIO - 1, offset[:, 0]))
    offset = offset.at[:, 0].set(first.astype(jnp.int32))
    absolute = jnp.clip(center[:, None] + offset, 0, GRID - 1).astype(jnp.int32)
    base = node // LAT_DEV * GRID_DEV - BG
    return (absolute - base[:, None]).astype(jnp.int32)


def draw_enc_count(key, part):
    key = jax.random.fold_in(key, 12)
    count = jax.random.randint(key, (LAT,), K_ENC // 4, K_ENC + 1, dtype=jnp.int32)
    local = jnp.arange(LAT, dtype=jnp.int32) % LAT_DEV
    count = jnp.where(local == 0, K_ENC, jnp.where(local == 1, K_ENC // 4, count))
    return count.astype(jnp.int32)


def draw_dec_src(key, part):
    key = jax.random.fold_in(key, 13)
    point = jnp.arange(GRID, dtype=jnp.int32)
    center = point // RATIO
    offset = jax.random.randint(key, (GRID, K_DEC), -BL, BL + 1, dtype=jnp.int32)
    local = point % GRID_DEV
    first = jnp.where(local == 0, -BL, jnp.where(local == GRID_DEV - 1, BL, offset[:, 0]))
    offset = offset.at[:, 0].set(first.astype(jnp.int32))
    return jnp.clip(center[:, None] + offset, 0, LAT - 1).astype(jnp.int32)


def draw_logit_scale(key, part):
    key = jax.random.fold_in(key, 14)
    lowest, highest = (0.5, 2.0)
    return jnp.exp(jax.random.uniform(key, (3, HEADS), jnp.float32, math.log(lowest), math.log(highest)))


def level_of(stream_key, extent, shards, smallest, high):
    gain = 1.0
    for axis_at, parts in shards:
        steps = jax.random.uniform(jax.random.fold_in(jax.random.fold_in(stream_key, 6), axis_at), (parts,), jnp.float32, smallest / len(shards), high / len(shards))
        gain = gain * jnp.repeat(jnp.exp(steps), extent[axis_at] // parts).reshape((-1,) + (1,) * (len(extent) - 1 - axis_at))
    return gain


def noise(stream_key, shape, scale, bound, split=(), kind=jnp.bfloat16):
    level = level_of(stream_key, shape, split, -0.22, 0.18) if split else 1.0
    array = jax.random.normal(stream_key, shape, jnp.float32) * scale * level
    return jnp.minimum(jnp.maximum(array, -bound), bound).astype(kind)


def setup_inputs(seed: int = 0) -> dict:
    key_list = jax.random.split(jax.random.key(seed), 12)
    return {
        "grid_state": noise(key_list[0], (GRID, CH), 1.0, 6.0, ((0, 128),)),
        "latent_init": noise(key_list[1], (LAT, H), 1.0, 6.0, ((0, 128),)),
        "enc_src": draw_enc_src(jax.random.fold_in(key_list[11], 71), 0),
        "enc_count": draw_enc_count(jax.random.fold_in(key_list[11], 71), 0),
        "dec_src": draw_dec_src(jax.random.fold_in(key_list[11], 71), 0),
        "w_in": noise(key_list[5], (CH, H), CH ** -0.5, 0.625),
        "enc_w": noise(key_list[6], (4, H, H), H ** -0.5, 0.1875),
        "proc_w": noise(key_list[7], (4, H, H), H ** -0.5, 0.1875),
        "dec_w": noise(key_list[8], (4, H, H), H ** -0.5, 0.1875),
        "w_out": noise(key_list[9], (H, CH), H ** -0.5, 0.1875),
        "logit_scale": draw_logit_scale(jax.random.fold_in(key_list[11], 71), 0),
    }


def layer_norm(values):
    center = values - lax.optimization_barrier(jnp.mean(values, axis=-1, keepdims=True))
    spread = lax.optimization_barrier(jnp.mean(center * center, axis=-1, keepdims=True))
    return center * lax.rsqrt(spread + 1e-05)

def edge_attend(query, keys, values, scale, valid):
    rows, degree, width = keys.shape
    heads = scale.shape[0]
    size = width // heads
    product = query.astype(jnp.float32)[:, None, :] * keys.astype(jnp.float32)
    scores = product.reshape(rows, degree, heads, size).sum(axis=-1) * (scale / math.sqrt(size))
    scores = jnp.where(valid[:, :, None], scores, -1e+30)
    highest = lax.optimization_barrier(jnp.max(scores, axis=1, keepdims=True))
    expo = jnp.where(valid[:, :, None], jnp.exp(scores - highest), 0.0)
    weights = expo / lax.optimization_barrier(jnp.sum(expo, axis=1, keepdims=True))
    spread_weights = jnp.repeat(weights, size, axis=2)
    return lax.optimization_barrier(jnp.sum(spread_weights * values.astype(jnp.float32), axis=1))

def window_attend(query, keys_wide, values_wide, scale, first, total):
    rows, width = query.shape
    heads = scale.shape[0]
    size = width // heads
    groups = heads // 4
    length = min(512, rows)
    span = length + WIN
    reach = WIN // 2
    factor = scale / math.sqrt(size)

    def one_block(number):
        begin = number * length
        queries = lax.dynamic_slice_in_dim(query, begin, length, 0).reshape(length, groups, 4, size)
        near_keys = lax.dynamic_slice_in_dim(keys_wide, begin, span, 0).reshape(span, groups, 4, size)
        near_values = lax.dynamic_slice_in_dim(values_wide, begin, span, 0).reshape(span, groups, 4, size)
        query_place = first + begin + jnp.arange(length, dtype=jnp.int32)
        key_place = first + begin - reach + jnp.arange(span, dtype=jnp.int32)
        inside = (jnp.abs(key_place[None, :] - query_place[:, None]) <= reach) & (key_place[None, :] >= 0) & (key_place[None, :] < total)

        def one_group(group):
            group_queries = lax.dynamic_index_in_dim(queries, group, 1, keepdims=False).astype(jnp.float32)
            group_keys = lax.dynamic_index_in_dim(near_keys, group, 1, keepdims=False).astype(jnp.float32)
            group_values = lax.dynamic_index_in_dim(near_values, group, 1, keepdims=False).astype(jnp.float32)
            group_factor = lax.dynamic_slice_in_dim(factor, group * 4, 4, 0)
            scores = jnp.einsum('qhd,khd->hqk', group_queries, group_keys) * group_factor[:, None, None]
            scores = jnp.where(inside[None], scores, -1e+30)
            highest = lax.optimization_barrier(jnp.max(scores, axis=-1, keepdims=True))
            expo = jnp.where(inside[None], jnp.exp(scores - highest), 0.0)
            weights = (expo / lax.optimization_barrier(jnp.sum(expo, axis=-1, keepdims=True))).astype(jnp.bfloat16)
            return jnp.einsum('hqk,khd->qhd', weights.astype(jnp.float32), group_values)
        mixed = lax.map(one_group, jnp.arange(groups, dtype=jnp.int32))
        return jnp.transpose(mixed, (1, 0, 2, 3)).reshape(length, width)
    result = lax.map(one_block, jnp.arange(rows // length, dtype=jnp.int32))
    return result.reshape(rows, width)

def project(rows, weight):
    return jnp.dot(rows, weight, preferred_element_type=jnp.float32)

def reference(grid_state, latent_init, enc_src, enc_count, dec_src, w_in, enc_w, proc_w, dec_w, w_out, logit_scale):
    embed = project(grid_state, w_in).astype(jnp.bfloat16)
    grid_keys = project(embed, enc_w[1]).astype(jnp.bfloat16)
    grid_values = project(embed, enc_w[2]).astype(jnp.bfloat16)
    enc_query = project(latent_init, enc_w[0]).astype(jnp.bfloat16)
    slots = jnp.arange(K_ENC, dtype=jnp.int32)

    def encode(pieces):
        query, offset, count, number = pieces
        source = (offset + (number * GRID_DEV - BG)).astype(jnp.int32)
        valid = slots[None, :] < count[:, None]
        return edge_attend(query, jnp.take(grid_keys, source, axis=0), jnp.take(grid_values, source, axis=0), logit_scale[0], valid).astype(jnp.bfloat16)
    parts_latent = LAT // LAT_DEV
    numbers = jnp.arange(parts_latent, dtype=jnp.int32)
    encoded = lax.map(encode, (enc_query.reshape(parts_latent, LAT_DEV, H), enc_src.reshape(parts_latent, LAT_DEV, K_ENC), enc_count.reshape(parts_latent, LAT_DEV), numbers)).reshape(LAT, H)
    latent = (latent_init.astype(jnp.float32) + project(encoded, enc_w[3])).astype(jnp.bfloat16)
    normed = layer_norm(latent.astype(jnp.float32)).astype(jnp.bfloat16)
    window_query = project(normed, proc_w[0]).astype(jnp.bfloat16)
    window_keys = project(normed, proc_w[1]).astype(jnp.bfloat16)
    window_values = project(normed, proc_w[2]).astype(jnp.bfloat16)
    reach = WIN // 2
    keys_wide = jnp.pad(window_keys, ((reach, reach), (0, 0)))
    values_wide = jnp.pad(window_values, ((reach, reach), (0, 0)))
    windowed = window_attend(window_query, keys_wide, values_wide, logit_scale[1], 0, LAT).astype(jnp.bfloat16)
    latent_out = (latent.astype(jnp.float32) + project(windowed, proc_w[3])).astype(jnp.bfloat16)
    mesh_keys = project(latent_out, dec_w[1]).astype(jnp.bfloat16)
    mesh_values = project(latent_out, dec_w[2]).astype(jnp.bfloat16)
    dec_query = project(embed, dec_w[0]).astype(jnp.bfloat16)
    every = jnp.ones((GRID_DEV, K_DEC), dtype=bool)

    def decode(pieces):
        query, source = pieces
        return edge_attend(query, jnp.take(mesh_keys, source, axis=0), jnp.take(mesh_values, source, axis=0), logit_scale[2], every).astype(jnp.bfloat16)
    parts_grid = GRID // GRID_DEV
    decoded = lax.map(decode, (dec_query.reshape(parts_grid, GRID_DEV, H), dec_src.reshape(parts_grid, GRID_DEV, K_DEC))).reshape(GRID, H)
    update = (embed.astype(jnp.float32) + project(decoded, dec_w[3])).astype(jnp.bfloat16)
    return project(update, w_out).astype(jnp.bfloat16)
```

```python
import math

import jax
import jax.numpy as jnp
from jax import lax
from jax.experimental import pallas as pl
from jax.experimental.pallas import tpu as pltpu
from jax.sharding import PartitionSpec as P

WIN = 512
BG = 1024
BL = 128
HEADS = 16
SIZE = 64
PAIRS = HEADS // 2
CPAD = 128
LOG2E = math.log2(math.e)
NEG = -1e30
BF = jnp.bfloat16
F32 = jnp.float32

VM = pl.BlockSpec(memory_space=pltpu.VMEM)
SM = pl.BlockSpec(memory_space=pltpu.SMEM)
ANY = pl.BlockSpec(memory_space=pl.ANY)


def dot(a, b):
    return jnp.dot(a, b, preferred_element_type=F32)


def dot_t(a, b):
    return lax.dot_general(a, b, (((1,), (1,)), ((), ())), preferred_element_type=F32)


def low_half(shape):
    return lax.broadcasted_iota(jnp.int32, shape, len(shape) - 1) < SIZE


def params(mib):
    return pltpu.CompilerParams(vmem_limit_bytes=mib * 2**20)


def fetch(source, rows, buffers, sems):
    copies = [
        pltpu.make_async_copy(source.at[row], buf, sems.at[at])
        for row, buf, at in zip(rows, buffers, range(len(rows)))
    ]
    for copy in copies:
        copy.start()
    return copies


def fold_kernel(win, enc_w, lat, scale, qt, av, w0, w1, w2, sems):
    got = fetch(enc_w, (1, 0, 2), (w1, w0, w2), sems)
    got[0].wait()
    ak = dot(win[...], w1[...]).astype(BF)
    got[1].wait()
    q = (dot(lat[...], w0[...]) * scale[0:1, :]).astype(BF)
    low = low_half((1, 128))
    for pair in range(PAIRS):
        at = slice(pair * 128, pair * 128 + 128)
        keys = ak[:, at]
        both = q[:, at]
        zero = jnp.zeros_like(both)
        qt[2 * pair] = dot_t(jnp.where(low, both, zero), keys).astype(BF)
        qt[2 * pair + 1] = dot_t(jnp.where(low, zero, both), keys).astype(BF)
    got[2].wait()
    av[...] = dot(win[...], w2[...]).astype(BF)


def encode_kernel(
    idx, left, own, right, qt, bias, av, lat, enc_w, latent, normed, grid, ge, z, w3, sems
):
    got = fetch(enc_w, (3,), (w3,), sems)
    rows = lat.shape[0]
    at = 0
    for piece in (left, own, right):
        for begin in range(0, piece.shape[1], 512):
            grid[at : at + 512, :] = piece[:, begin : begin + 512].astype(F32).T
            at += 512
    row = lax.broadcasted_iota(jnp.int32, (256, 256), 0)
    col = lax.broadcasted_iota(jnp.int32, (256, 256), 1)
    diag = jnp.where(row % 16 == col % 16, 0.0, NEG)

    def group(number, carry):
        base = number * 16
        for slot in range(16):
            for node in range(16):
                edge = slot * 16 + node
                ge[pl.ds(edge, 1), :] = grid[pl.ds(idx[base + (slot * rows + node)], 1), :]
        points = ge[...].astype(BF)
        base = pl.multiple_of(base, 16)
        queries = qt[:, pl.ds(base, 16), :].reshape(256, CPAD)
        score = dot_t(queries, points) + (diag + bias[pl.ds(number, 1), :])
        expo = jnp.exp2(score - jnp.max(score, axis=1, keepdims=True)).astype(BF)
        mixed = dot(expo, points)
        mixed = mixed / mixed[:, 100:101]
        z[:, pl.ds(base, 16), :] = mixed.reshape(16, 16, CPAD).astype(BF)
        return carry

    lax.fori_loop(0, rows // 16, group, 0)
    low = low_half((1, 128))
    parts = []
    for pair in range(PAIRS):
        values = av[:, pair * 128 : pair * 128 + 128]
        zero = jnp.zeros_like(values)
        parts.append(
            dot(z[2 * pair], jnp.where(low, values, zero))
            + dot(z[2 * pair + 1], jnp.where(low, zero, values))
        )
    encoded = jnp.concatenate(parts, axis=1).astype(BF)
    got[0].wait()
    rounded = (lat[...].astype(F32) + dot(encoded, w3[...])).astype(BF)
    latent[...] = rounded
    wide = rounded.astype(F32)
    center = wide - jnp.mean(wide, axis=1, keepdims=True)
    spread = jnp.mean(center * center, axis=1, keepdims=True)
    normed[...] = (center * lax.rsqrt(spread + 1e-05)).astype(BF)


def project_kernel(
    normed, win, wout, scale, proc_w, dec_w, q, k, v, aq, bo, co, b0, b1, b2, b3, b4, sems
):
    got = fetch(proc_w, (0, 1, 2), (b0, b1, b2), sems)
    more = fetch(dec_w, (0, 3), (b3, b4), sems.at[pl.ds(3, 2)])
    rows = normed[...]
    got[0].wait()
    q[...] = (dot(rows, b0[...]) * scale[1:2, :]).astype(BF)
    got[1].wait()
    k[...] = dot(rows, b1[...]).astype(BF)
    got[2].wait()
    v[...] = dot(rows, b2[...]).astype(BF)
    co[...] = dot_t(win[...], wout[...]).astype(BF)
    more[0].wait()
    aq[...] = (dot(win[...], b3[...]) * scale[2:3, :]).astype(BF)
    more[1].wait()
    bo[...] = dot_t(b4[...], wout[...]).astype(BF)


def window_kernel(
    ends, q, k, v, nl, nr, latent, proc_w, out, keys, values, bias, mixed, wk, wv, wo, sems
):
    got = fetch(proc_w, (1, 2, 3), (wk, wv, wo), sems)
    rows = q.shape[0]
    half = rows // 2
    span = half + WIN
    keys[rows : 2 * rows, :] = k[...]
    values[rows : 2 * rows, :] = v[...]
    row = lax.broadcasted_iota(jnp.int32, (half, span), 0)
    col = lax.broadcasted_iota(jnp.int32, (half, span), 1)
    for side in range(2):
        place = col + side * half
        inside = (col >= row) & (col - row <= WIN) & (place >= ends[0]) & (place < ends[1])
        bias[side] = jnp.where(inside, 0.0, NEG)
    got[0].wait()
    keys[:rows, :] = dot(nl[...], wk[...]).astype(BF)
    keys[2 * rows :, :] = dot(nr[...], wk[...]).astype(BF)
    got[1].wait()
    values[:rows, :] = dot(nl[...], wv[...]).astype(BF)
    values[2 * rows :, :] = dot(nr[...], wv[...]).astype(BF)
    low = low_half((1, 128))

    def one_pair(pair, carry):
        lanes = pl.ds(pl.multiple_of(pair * 128, 128), 128)
        for side in range(2):
            these = slice(side * half, side * half + half)
            near = slice(side * half, side * half + span)
            both = q[these, lanes]
            near_keys = keys[near, lanes]
            near_values = values[near, lanes]
            parts = []
            for keep in (low, ~low):
                score = dot_t(jnp.where(keep, both, jnp.zeros_like(both)), near_keys) + bias[side]
                expo = jnp.exp2(score - jnp.max(score, axis=1, keepdims=True)).astype(BF)
                total = dot(expo, jnp.where(keep, near_values, jnp.ones_like(near_values)))
                parts.append(total / pltpu.roll(total, SIZE, 1))
            mixed[these, lanes] = jnp.where(low, parts[0], parts[1]).astype(BF)
        return carry

    lax.fori_loop(0, PAIRS, one_pair, 0)
    got[2].wait()
    out[...] = (latent[...].astype(F32) + dot(mixed[...], wo[...])).astype(BF)


CHUNK = 128


def decode_kernel(
    idx, left, own, right, grid, aq, bo, co, dec_w, out, kf, vf, qb, prod, wts, dec, wk, wv, sems
):
    got = fetch(dec_w, (1, 2), (wk, wv), sems)
    points = grid.shape[1]
    for copy, weight, tiles in ((got[0], wk, kf), (got[1], wv, vf)):
        copy.wait()
        begin = 0
        for piece in (left, own, right):
            count = piece.shape[0]
            for block in range(8):
                tiles[pl.ds(begin * 8 + block, count, stride=8), :] = dot(
                    piece[...], weight[:, block * 128 : block * 128 + 128]
                )
            begin += count
    same = (lax.broadcasted_iota(jnp.int32, (128, 128), 0) < SIZE) == (
        lax.broadcasted_iota(jnp.int32, (128, 128), 1) < SIZE
    )
    ones = jnp.where(same, 1.0, 0.0).astype(BF)
    unroll = 8

    def one_chunk(number, carry):
        first = pl.multiple_of(number * CHUNK, CHUNK)
        state = grid[:, pl.ds(first, CHUNK)].astype(F32).T.astype(BF)
        for block in range(8):
            qb[pl.ds(block, CHUNK, stride=8), :] = dot(state, aq[:, block * 128 : block * 128 + 128])

        def products(step, carry):
            for at in range(0, unroll, 2):
                begin = pl.multiple_of((step * unroll + at) * 8, 16)
                query = qb[pl.ds(begin, 16), :]
                for edge in range(3):
                    where = edge * points + first + step * unroll + at
                    one = kf[pl.ds(pl.multiple_of(idx[where], 8), 8), :]
                    two = kf[pl.ds(pl.multiple_of(idx[where + 1], 8), 8), :]
                    prod[edge, pl.ds(begin, 16), :] = (
                        query * jnp.concatenate([one, two], axis=0)
                    ).astype(BF)
            return carry

        lax.fori_loop(0, CHUNK // unroll, products, 0)
        scores = [dot(prod[edge], ones) for edge in range(3)]
        highest = jnp.maximum(jnp.maximum(scores[0], scores[1]), scores[2])
        expo = [jnp.exp2(score - highest) for score in scores]
        inverse = 1.0 / (expo[0] + expo[1] + expo[2])
        for edge in range(3):
            wts[edge] = expo[edge] * inverse

        def mixtures(step, carry):
            for at in range(unroll):
                begin = pl.multiple_of((step * unroll + at) * 8, 8)
                where = first + step * unroll + at
                total = None
                for edge in range(3):
                    source = pl.multiple_of(idx[edge * points + where], 8)
                    term = wts[edge, pl.ds(begin, 8), :] * vf[pl.ds(source, 8), :]
                    total = term if total is None else total + term
                dec[pl.ds(begin, 8), :] = total
            return carry

        lax.fori_loop(0, CHUNK // unroll, mixtures, 0)
        result = dot(state, co[...])
        for block in range(8):
            result += dot(
                dec[pl.ds(block, CHUNK, stride=8), :].astype(BF),
                bo[block * 128 : block * 128 + 128, :],
            )
        out[:, pl.ds(first, CHUNK)] = result.T[: out.shape[0], :].astype(BF)
        return carry

    lax.fori_loop(0, points // CHUNK, one_chunk, 0)


def shape(dims, kind=BF):
    return jax.ShapeDtypeStruct(dims, kind)


def neighbours(head, tail):
    axes = ("wide", "narrow")
    count = lax.axis_size(axes)
    after = lax.ppermute(tail, axes, [(i, i + 1) for i in range(count - 1)])
    before = lax.ppermute(head, axes, [(i + 1, i) for i in range(count - 1)])
    return after, before


def on_device(
    grid_state,
    latent_init,
    enc_src,
    enc_count,
    dec_src,
    w_in,
    enc_w,
    proc_w,
    dec_w,
    w_out,
    logit_scale,
):
    points, channels = grid_state.shape
    rows, width = latent_init.shape
    slots = enc_src.shape[1]
    place = lax.axis_index(("wide", "narrow"))
    total = rows * lax.axis_size(("wide", "narrow"))
    weight = pltpu.VMEM((width, width), BF)
    dma = pltpu.SemaphoreType.DMA

    grid = jnp.concatenate(
        [
            grid_state.T,
            jnp.ones((1, points), BF),
            jnp.zeros((CPAD - channels - 1, points), BF),
        ],
        axis=0,
    )
    grid_left, grid_right = neighbours(grid[:, :BG], grid[:, points - BG :])
    win = jnp.pad(w_in, ((0, CPAD - channels), (0, 0)))
    wout = jnp.pad(w_out.T, ((0, CPAD - channels), (0, 0)))
    scale = jnp.repeat(logit_scale * (LOG2E / math.sqrt(SIZE)), SIZE, axis=1)
    enc_idx = jnp.clip(enc_src.T, 0, points + 2 * BG - 1).reshape(-1)
    live = jnp.arange(slots, dtype=jnp.int32)[:, None] < enc_count[None, :]
    bias = jnp.where(live, 0.0, NEG).astype(F32)
    bias = bias.reshape(slots, rows // 16, 16).transpose(1, 0, 2).reshape(rows // 16, slots * 16)
    dec_idx = jnp.clip(dec_src.T - (place * rows - BL), 0, rows + 2 * BL - 1).reshape(-1) * 8
    ends = jnp.stack([WIN // 2 - place * rows, total + WIN // 2 - place * rows])

    qt, av = pl.pallas_call(
        fold_kernel,
        out_shape=(shape((HEADS, rows, CPAD)), shape((CPAD, width))),
        in_specs=[VM, ANY, VM, VM],
        out_specs=(VM, VM),
        scratch_shapes=[weight] * 3 + [dma((3,))],
        compiler_params=params(24),
        cost_estimate=pl.CostEstimate(flops=2 * 10**9, bytes_accessed=8 * 2**20, transcendentals=0),
        name="fold",
    )(win, enc_w, latent_init, scale)
    latent, normed = pl.pallas_call(
        encode_kernel,
        out_shape=(shape((rows, width)), shape((rows, width))),
        in_specs=[SM] + [VM] * 7 + [ANY],
        out_specs=(VM, VM),
        scratch_shapes=[
            pltpu.VMEM((points + 2 * BG, CPAD), F32),
            pltpu.VMEM((slots * 16, CPAD), F32),
            pltpu.VMEM((HEADS, rows, CPAD), BF),
            weight,
            dma((1,)),
        ],
        compiler_params=params(24),
        name="encode",
    )(enc_idx, grid_left, grid, grid_right, qt, bias, av, latent_init, enc_w)
    near_left, near_right = neighbours(normed, normed)
    q, k, v, aq, bo, co = pl.pallas_call(
        project_kernel,
        out_shape=(shape((rows, width)),) * 3
        + (shape((CPAD, width)), shape((width, CPAD)), shape((CPAD, CPAD))),
        in_specs=[VM] * 4 + [ANY] * 2,
        out_specs=(VM,) * 6,
        scratch_shapes=[weight] * 5 + [dma((5,))],
        compiler_params=params(24),
        cost_estimate=pl.CostEstimate(flops=3 * 10**9, bytes_accessed=12 * 2**20, transcendentals=0),
        name="project",
    )(normed, win, wout, scale, proc_w, dec_w)
    latent_out = pl.pallas_call(
        window_kernel,
        out_shape=shape((rows, width)),
        in_specs=[SM] + [VM] * 6 + [ANY],
        out_specs=VM,
        scratch_shapes=[
            pltpu.VMEM((rows + WIN, width), BF),
            pltpu.VMEM((rows + WIN, width), BF),
            pltpu.VMEM((2, rows // 2, rows // 2 + WIN), F32),
            pltpu.VMEM((rows, width), BF),
        ]
        + [weight] * 3
        + [dma((3,))],
        compiler_params=params(32),
        name="window",
    )(ends, q, k, v, near_left, near_right, latent, proc_w)
    mesh_left, mesh_right = neighbours(latent_out[:BL], latent_out[rows - BL :])
    nodes = rows + 2 * BL
    out = pl.pallas_call(
        decode_kernel,
        out_shape=shape((channels, points)),
        in_specs=[SM] + [VM] * 7 + [ANY],
        out_specs=VM,
        scratch_shapes=[
            pltpu.VMEM((nodes * 8, 128), F32),
            pltpu.VMEM((nodes * 8, 128), F32),
            pltpu.VMEM((CHUNK * 8, 128), F32),
            pltpu.VMEM((3, CHUNK * 8, 128), BF),
            pltpu.VMEM((3, CHUNK * 8, 128), F32),
            pltpu.VMEM((CHUNK * 8, 128), F32),
        ]
        + [weight] * 2
        + [dma((2,))],
        compiler_params=params(32),
        name="decode",
    )(dec_idx, mesh_left, latent_out, mesh_right, grid, aq, bo, co, dec_w)
    return out.T


def solution(mesh):
    both = ("wide", "narrow")
    placed = (
        P(both, None),
        P(both, None),
        P(both, None),
        P(both),
        P(both, None),
        P(),
        P(),
        P(),
        P(),
        P(),
        P(),
    )
    return jax.shard_map(
        on_device,
        mesh=mesh,
        in_specs=placed,
        out_specs=P(both, None),
        check_vma=False,
    )
```

```python
import math

import jax
import jax.numpy as jnp
from jax import lax
from jax.experimental import pallas as pl
from jax.experimental.pallas import tpu as pltpu
from jax.sharding import PartitionSpec as P

WIN = 512
BG = 1024
BL = 128
HEADS = 16
SIZE = 64
PAIRS = HEADS // 2
CPAD = 128
LOG2E = math.log2(math.e)
NEG = -1e30
BF = jnp.bfloat16
F32 = jnp.float32

VM = pl.BlockSpec(memory_space=pltpu.VMEM)
SM = pl.BlockSpec(memory_space=pltpu.SMEM)
HBM = pl.BlockSpec(memory_space=pltpu.HBM)


def dot(a, b):
    return jnp.dot(a, b, preferred_element_type=F32)


def dot_t(a, b):
    return lax.dot_general(a, b, (((1,), (1,)), ((), ())), preferred_element_type=F32)


def low_half(shape):
    return lax.broadcasted_iota(jnp.int32, shape, len(shape) - 1) < SIZE


def params(mib):
    return pltpu.CompilerParams(vmem_limit_bytes=mib * 2**20)


def fetch(source, rows, buffers, sems):
    copies = [
        pltpu.make_async_copy(source.at[row], buf, sems.at[at])
        for row, buf, at in zip(rows, buffers, range(len(rows)))
    ]
    for copy in copies:
        copy.start()
    return copies


def fold_kernel(win, enc_w, lat, scale, qt, av, w0, w1, w2, sems):
    got = fetch(enc_w, (1, 0, 2), (w1, w0, w2), sems)
    got[0].wait()
    ak = dot(win[...], w1[...]).astype(BF)
    got[1].wait()
    q = (dot(lat[...], w0[...]) * scale[0:1, :]).astype(BF)
    low = low_half((1, 128))
    for pair in range(PAIRS):
        at = slice(pair * 128, pair * 128 + 128)
        keys = ak[:, at]
        both = q[:, at]
        zero = jnp.zeros_like(both)
        qt[2 * pair] = dot_t(jnp.where(low, both, zero), keys).astype(BF)
        qt[2 * pair + 1] = dot_t(jnp.where(low, zero, both), keys).astype(BF)
    got[2].wait()
    av[...] = dot(win[...], w2[...]).astype(BF)


def encode_kernel(
    idx, left, own, right, qt, bias, av, lat, enc_w, proc_w, dec_w,
    latent, normed, pw0, pw1, pw2, pw3, dw0, dw1, dw2, dw3,
    grid, ge0, ge1, z, w3, sems,
):
    got = fetch(enc_w, (3,), (w3,), sems.at[pl.ds(0, 1)])
    later = fetch(proc_w, (0, 1, 2, 3), (pw0, pw1, pw2, pw3), sems.at[pl.ds(1, 4)])
    later += fetch(dec_w, (0, 3, 1, 2), (dw0, dw3, dw1, dw2), sems.at[pl.ds(5, 4)])
    rows = lat.shape[0]
    groups = rows // 16
    at = 0
    for piece in (left, own, right):
        for begin in range(0, piece.shape[1], 512):
            grid[at : at + 512, :] = piece[:, begin : begin + 512].astype(F32).T
            at += 512
    row = lax.broadcasted_iota(jnp.int32, (256, 256), 0)
    col = lax.broadcasted_iota(jnp.int32, (256, 256), 1)
    diag = jnp.where(row % 16 == col % 16, 0.0, NEG)

    def collect(number, ge):
        base = number * 16
        for slot in range(16):
            for node in range(16):
                edge = slot * 16 + node
                ge[pl.ds(edge, 1), :] = grid[pl.ds(idx[base + (slot * rows + node)], 1), :]

    def attend(number, ge):
        points = ge[...].astype(BF)
        base = pl.multiple_of(number * 16, 16)
        queries = qt[:, pl.ds(base, 16), :].reshape(256, CPAD)
        score = dot_t(queries, points) + (diag + bias[pl.ds(number, 1), :])
        expo = jnp.exp2(score - jnp.max(score, axis=1, keepdims=True)).astype(BF)
        mixed = dot(expo, points)
        mixed = mixed / mixed[:, 100:101]
        z[:, pl.ds(base, 16), :] = mixed.reshape(16, 16, CPAD).astype(BF)

    collect(0, ge0)

    def two_groups(step, carry):
        number = step * 2
        attend(number, ge0)
        collect(number + 1, ge1)
        attend(number + 1, ge1)
        collect(jnp.minimum(number + 2, groups - 1), ge0)
        return carry

    lax.fori_loop(0, groups // 2, two_groups, 0)
    low = low_half((1, 128))
    parts = []
    for pair in range(PAIRS):
        values = av[:, pair * 128 : pair * 128 + 128]
        zero = jnp.zeros_like(values)
        parts.append(
            dot(z[2 * pair], jnp.where(low, values, zero))
            + dot(z[2 * pair + 1], jnp.where(low, zero, values))
        )
    encoded = jnp.concatenate(parts, axis=1).astype(BF)
    got[0].wait()
    rounded = (lat[...].astype(F32) + dot(encoded, w3[...])).astype(BF)
    latent[...] = rounded
    wide = rounded.astype(F32)
    center = wide - jnp.mean(wide, axis=1, keepdims=True)
    spread = jnp.mean(center * center, axis=1, keepdims=True)
    normed[...] = (center * lax.rsqrt(spread + 1e-05)).astype(BF)
    for copy in later:
        copy.wait()


def project_kernel(normed, win, wout, scale, wq, wk, wv, dq, do, q, k, v, aq, bo, co):
    rows = normed[...]
    q[...] = (dot(rows, wq[...]) * scale[1:2, :]).astype(BF)
    k[...] = dot(rows, wk[...]).astype(BF)
    v[...] = dot(rows, wv[...]).astype(BF)
    co[...] = dot_t(wout[...], win[...]).astype(BF)
    aq[...] = (dot(win[...], dq[...]) * scale[2:3, :]).astype(BF)
    bo[...] = dot_t(do[...], wout[...]).astype(BF)


def window_kernel(
    ends, q, k, v, nl, nr, latent, wk, wv, wo, out, keys, values, bias, mixed
):
    rows = q.shape[0]
    half = rows // 2
    span = half + WIN
    keys[rows : 2 * rows, :] = k[...]
    values[rows : 2 * rows, :] = v[...]
    row = lax.broadcasted_iota(jnp.int32, (half, span), 0)
    col = lax.broadcasted_iota(jnp.int32, (half, span), 1)
    for side in range(2):
        place = col + side * half
        inside = (col >= row) & (col - row <= WIN) & (place >= ends[0]) & (place < ends[1])
        bias[side] = jnp.where(inside, 0.0, NEG)
    keys[:rows, :] = dot(nl[...], wk[...]).astype(BF)
    keys[2 * rows :, :] = dot(nr[...], wk[...]).astype(BF)
    values[:rows, :] = dot(nl[...], wv[...]).astype(BF)
    values[2 * rows :, :] = dot(nr[...], wv[...]).astype(BF)
    low = low_half((1, 128))

    def one_pair(pair, carry):
        lanes = pl.ds(pl.multiple_of(pair * 128, 128), 128)
        for side in range(2):
            these = slice(side * half, side * half + half)
            near = slice(side * half, side * half + span)
            both = q[these, lanes]
            zero = jnp.zeros_like(both)
            stacked = jnp.concatenate(
                [jnp.where(low, both, zero), jnp.where(low, zero, both)], axis=0
            )
            near_values = values[near, lanes]
            score = dot_t(stacked, keys[near, lanes]).reshape(2, half, span) + bias[side][None]
            score = score.reshape(2 * half, span)
            expo = jnp.exp2(score - jnp.max(score, axis=1, keepdims=True)).astype(BF)
            total = dot(
                expo, jnp.concatenate([near_values, jnp.ones_like(near_values)], axis=1)
            )
            part = total[:, :128] / total[:, 128:]
            mixed[these, lanes] = jnp.where(low, part[:half], part[half:]).astype(BF)
        return carry

    lax.fori_loop(0, PAIRS, one_pair, 0)
    out[...] = (latent[...].astype(F32) + dot(mixed[...], wo[...])).astype(BF)


CHUNK = 128


def to_tiles(rows, weight, tiles, begin):
    count = rows.shape[0]
    for block in range(8):
        tiles[pl.ds(begin * 8 + block, count, stride=8), :] = dot(
            rows, weight[:, block * 128 : block * 128 + 128]
        )


def prepare_kernel(own, state, aq, wk, wv, q, k, v):
    to_tiles(own[...], wk, k, 0)
    to_tiles(own[...], wv, v, 0)
    points = state.shape[1]
    for first in range(0, points, 512):
        to_tiles(state[:, first : first + 512].astype(F32).T.astype(BF), aq, q, first)


def decode_kernel(
    idx, left, right, ko, vo, q, grid, bo, co, wk, wv, out, kf, vf, prod, wts, dec
):
    points = grid.shape[1]
    side = left.shape[0]
    for weight, tiles, own in ((wk, kf, ko), (wv, vf, vo)):
        to_tiles(left[...], weight, tiles, 0)
        tiles[side * 8 : side * 8 + own.shape[0], :] = own[...]
        to_tiles(right[...], weight, tiles, side + own.shape[0] // 8)
    head_row = lax.broadcasted_iota(jnp.int32, (256, 256), 0) // SIZE
    head_col = lax.broadcasted_iota(jnp.int32, (256, 256), 1) // SIZE
    ones = jnp.where(head_row == head_col, 1.0, 0.0).astype(BF)
    sub = 128

    def one_chunk(number, carry):
        first = pl.multiple_of(number * CHUNK, CHUNK)

        def tile_of(tiles, edge, at):
            return tiles[pl.ds(pl.multiple_of(idx[edge * points + first + at], 8), 8), :]

        for quad in range(0, CHUNK, 4):
            mine = [
                q[pl.ds(pl.multiple_of((first + quad + at) * 8, 8), 8), :] for at in range(4)
            ]
            for edge in range(3):
                terms = [mine[at] * tile_of(kf, edge, quad + at) for at in range(4)]
                place = slice(quad * 4, quad * 4 + 16)
                prod[edge, place, 0:128] = jnp.concatenate([terms[0], terms[2]], axis=0).astype(BF)
                prod[edge, place, 128:256] = jnp.concatenate([terms[1], terms[3]], axis=0).astype(BF)
        for begin in range(0, CHUNK * 4, sub):
            score = dot(prod[:, begin : begin + sub, :].reshape(3 * sub, 256), ones)
            score = [score[edge * sub : edge * sub + sub] for edge in range(3)]
            highest = jnp.maximum(jnp.maximum(score[0], score[1]), score[2])
            expo = [jnp.exp2(part - highest) for part in score]
            inverse = 1.0 / (expo[0] + expo[1] + expo[2])
            for edge in range(3):
                wts[edge, begin : begin + sub, :] = expo[edge] * inverse
        for at in range(CHUNK):
            top = at // 4 * 16 + (at % 4) // 2 * 8
            lane = at % 2 * 128
            total = None
            for edge in range(3):
                term = wts[edge, top : top + 8, lane : lane + 128] * tile_of(vf, edge, at)
                total = term if total is None else total + term
            dec[pl.ds(pl.multiple_of((first + at) * 8, 8), 8), :] = total
        return carry

    lax.fori_loop(0, points // CHUNK, one_chunk, 0)
    block = 256
    for first in range(0, points, block):
        wide = jnp.concatenate(
            [dec[pl.ds(first * 8 + part, block, stride=8), :] for part in range(8)], axis=1
        ).astype(BF)
        result = dot(wide, bo[...]).T + dot(co[...], grid[:, first : first + block])
        out[:, first : first + block] = result[: out.shape[0], :].astype(BF)


def shape(dims, kind=BF):
    return jax.ShapeDtypeStruct(dims, kind)


def neighbours(head, tail):
    axes = ("wide", "narrow")
    count = lax.axis_size(axes)
    after = lax.ppermute(tail, axes, [(i, i + 1) for i in range(count - 1)])
    before = lax.ppermute(head, axes, [(i + 1, i) for i in range(count - 1)])
    return after, before


def on_device(
    grid_state,
    latent_init,
    enc_src,
    enc_count,
    dec_src,
    w_in,
    enc_w,
    proc_w,
    dec_w,
    w_out,
    logit_scale,
):
    points, channels = grid_state.shape
    rows, width = latent_init.shape
    slots = enc_src.shape[1]
    place = lax.axis_index(("wide", "narrow"))
    total = rows * lax.axis_size(("wide", "narrow"))
    weight = pltpu.VMEM((width, width), BF)
    dma = pltpu.SemaphoreType.DMA

    grid = jnp.concatenate(
        [
            grid_state.T,
            jnp.ones((1, points), BF),
            jnp.zeros((CPAD - channels - 1, points), BF),
        ],
        axis=0,
    )
    grid_left, grid_right = neighbours(grid[:, :BG], grid[:, points - BG :])
    win = jnp.pad(w_in, ((0, CPAD - channels), (0, 0)))
    wout = jnp.pad(w_out.T, ((0, CPAD - channels), (0, 0)))
    scale = jnp.repeat(logit_scale * (LOG2E / math.sqrt(SIZE)), SIZE, axis=1)
    enc_idx = jnp.clip(enc_src.T, 0, points + 2 * BG - 1).reshape(-1)
    live = jnp.arange(slots, dtype=jnp.int32)[:, None] < enc_count[None, :]
    bias = jnp.where(live, 0.0, NEG).astype(F32)
    bias = bias.reshape(slots, rows // 16, 16).transpose(1, 0, 2).reshape(rows // 16, slots * 16)
    dec_idx = jnp.clip(dec_src.T - (place * rows - BL), 0, rows + 2 * BL - 1).reshape(-1) * 8
    ends = jnp.stack([WIN // 2 - place * rows, total + WIN // 2 - place * rows])

    qt, av = pl.pallas_call(
        fold_kernel,
        out_shape=(shape((HEADS, rows, CPAD)), shape((CPAD, width))),
        in_specs=[VM, HBM, VM, VM],
        out_specs=(VM, VM),
        scratch_shapes=[weight] * 3 + [dma((3,))],
        compiler_params=params(56),
        cost_estimate=pl.CostEstimate(flops=2 * 10**9, bytes_accessed=8 * 2**20, transcendentals=0),
        name="fold",
    )(win, enc_w, latent_init, scale)
    square = shape((width, width))
    latent, normed, pw0, pw1, pw2, pw3, dw0, dw1, dw2, dw3 = pl.pallas_call(
        encode_kernel,
        out_shape=(shape((rows, width)),) * 2 + (square,) * 8,
        in_specs=[SM] + [VM] * 7 + [HBM] * 3,
        out_specs=(VM,) * 10,
        scratch_shapes=[
            pltpu.VMEM((points + 2 * BG, CPAD), F32),
            pltpu.VMEM((slots * 16, CPAD), F32),
            pltpu.VMEM((slots * 16, CPAD), F32),
            pltpu.VMEM((HEADS, rows, CPAD), BF),
            weight,
            dma((9,)),
        ],
        compiler_params=params(28),
        name="encode",
    )(enc_idx, grid_left, grid, grid_right, qt, bias, av, latent_init, enc_w, proc_w, dec_w)
    near_left, near_right = neighbours(normed, normed)
    q, k, v, aq, bo, co = pl.pallas_call(
        project_kernel,
        out_shape=(shape((rows, width)),) * 3
        + (shape((CPAD, width)), shape((width, CPAD)), shape((CPAD, CPAD))),
        in_specs=[VM] * 9,
        out_specs=(VM,) * 6,
        compiler_params=params(24),
        cost_estimate=pl.CostEstimate(flops=3 * 10**9, bytes_accessed=12 * 2**20, transcendentals=0),
        name="project",
    )(normed, win, wout, scale, pw0, pw1, pw2, dw0, dw3)
    latent_out = pl.pallas_call(
        window_kernel,
        out_shape=shape((rows, width)),
        in_specs=[SM] + [VM] * 9,
        out_specs=VM,
        scratch_shapes=[
            pltpu.VMEM((rows + WIN, width), BF),
            pltpu.VMEM((rows + WIN, width), BF),
            pltpu.VMEM((2, rows // 2, rows // 2 + WIN), F32),
            pltpu.VMEM((rows, width), BF),
        ],
        compiler_params=params(24),
        name="window",
    )(ends, q, k, v, near_left, near_right, latent, pw1, pw2, pw3)
    mesh_left, mesh_right = neighbours(latent_out[:BL], latent_out[rows - BL :])
    nodes = rows + 2 * BL
    dq, dk, dv = pl.pallas_call(
        prepare_kernel,
        out_shape=(
            shape((points * 8, 128), F32),
            shape((rows * 8, 128), F32),
            shape((rows * 8, 128), F32),
        ),
        in_specs=[VM] * 5,
        out_specs=(VM,) * 3,
        compiler_params=params(24),
        cost_estimate=pl.CostEstimate(flops=3 * 10**9, bytes_accessed=12 * 2**20, transcendentals=0),
        name="prepare",
    )(latent_out, grid, aq, dw1, dw2)
    out = pl.pallas_call(
        decode_kernel,
        out_shape=shape((channels, points)),
        in_specs=[SM] + [VM] * 10,
        out_specs=VM,
        scratch_shapes=[
            pltpu.VMEM((nodes * 8, 128), F32),
            pltpu.VMEM((nodes * 8, 128), F32),
            pltpu.VMEM((3, CHUNK * 4, 256), BF),
            pltpu.VMEM((3, CHUNK * 4, 256), F32),
            pltpu.VMEM((points * 8, 128), F32),
        ],
        compiler_params=params(32),
        name="decode",
    )(dec_idx, mesh_left, mesh_right, dk, dv, dq, grid, bo, co, dw1, dw2)
    return out.T


def solution(mesh):
    both = ("wide", "narrow")
    placed = (
        P(both, None),
        P(both, None),
        P(both, None),
        P(both),
        P(both, None),
        P(),
        P(),
        P(),
        P(),
        P(),
        P(),
    )
    return jax.shard_map(
        on_device,
        mesh=mesh,
        in_specs=placed,
        out_specs=P(both, None),
        check_vma=False,
    )
```

```python
import math

import jax
import jax.numpy as jnp
from jax import lax
from jax.experimental import pallas as pl
from jax.experimental.pallas import tpu as pltpu
from jax.sharding import PartitionSpec as P

WIN = 512
BG = 1024
BL = 128
HEADS = 16
SIZE = 64
PAIRS = HEADS // 2
CPAD = 128
LOG2E = math.log2(math.e)
NEG = -1e30
BF = jnp.bfloat16
F32 = jnp.float32

VM = pl.BlockSpec(memory_space=pltpu.VMEM)
SM = pl.BlockSpec(memory_space=pltpu.SMEM)
HBM = pl.BlockSpec(memory_space=pltpu.HBM)


def dot(a, b):
    return jnp.dot(a, b, preferred_element_type=F32)


def dot_t(a, b):
    return lax.dot_general(a, b, (((1,), (1,)), ((), ())), preferred_element_type=F32)


def low_half(shape):
    return lax.broadcasted_iota(jnp.int32, shape, len(shape) - 1) < SIZE


def params(mib):
    return pltpu.CompilerParams(vmem_limit_bytes=mib * 2**20)


def fetch(source, rows, buffers, sems):
    copies = [
        pltpu.make_async_copy(source.at[row], buf, sems.at[at])
        for row, buf, at in zip(rows, buffers, range(len(rows)))
    ]
    for copy in copies:
        copy.start()
    return copies


def fold_kernel(win, enc_w, lat, scale, *others):
    qt, av, w0, w1, w2, sems = others[-6:]
    got = fetch(enc_w, (1, 0, 2), (w1, w0, w2), sems)
    got[0].wait()
    ak = dot(win[...], w1[...]).astype(BF)
    got[1].wait()
    q = (dot(lat[...], w0[...]) * scale[0:1, :]).astype(BF)
    low = low_half((1, 128))
    for pair in range(PAIRS):
        at = slice(pair * 128, pair * 128 + 128)
        keys = ak[:, at]
        both = q[:, at]
        zero = jnp.zeros_like(both)
        qt[2 * pair] = dot_t(jnp.where(low, both, zero), keys).astype(BF)
        qt[2 * pair + 1] = dot_t(jnp.where(low, zero, both), keys).astype(BF)
    got[2].wait()
    av[...] = dot(win[...], w2[...]).astype(BF)


def encode_kernel(
    idx, left, own, right, qt, bias, av, lat, enc_w, proc_w, dec_w,
    latent, normed, pw0, pw1, pw2, pw3, dw0, dw1, dw2, dw3,
    grid, ge0, ge1, z, w3, sems,
):
    got = fetch(enc_w, (3,), (w3,), sems.at[pl.ds(0, 1)])
    later = fetch(proc_w, (0, 1, 2, 3), (pw0, pw1, pw2, pw3), sems.at[pl.ds(1, 4)])
    later += fetch(dec_w, (0, 3, 1, 2), (dw0, dw3, dw1, dw2), sems.at[pl.ds(5, 4)])
    rows = lat.shape[0]
    groups = rows // 16
    at = 0
    for piece in (left, own, right):
        for begin in range(0, piece.shape[1], 512):
            grid[at : at + 512, :] = piece[:, begin : begin + 512].astype(F32).T
            at += 512
    row = lax.broadcasted_iota(jnp.int32, (256, 256), 0)
    col = lax.broadcasted_iota(jnp.int32, (256, 256), 1)
    diag = jnp.where(row % 16 == col % 16, 0.0, NEG)

    def collect(number, ge):
        base = number * 16
        for slot in range(16):
            for node in range(16):
                edge = slot * 16 + node
                ge[pl.ds(edge, 1), :] = grid[pl.ds(idx[base + (slot * rows + node)], 1), :]

    def attend(number, ge):
        points = ge[...].astype(BF)
        base = pl.multiple_of(number * 16, 16)
        queries = qt[:, pl.ds(base, 16), :].reshape(256, CPAD)
        score = dot_t(queries, points) + (diag + bias[pl.ds(number, 1), :])
        expo = jnp.exp2(score - jnp.max(score, axis=1, keepdims=True)).astype(BF)
        mixed = dot(expo, points)
        mixed = mixed / mixed[:, 100:101]
        z[:, pl.ds(base, 16), :] = mixed.reshape(16, 16, CPAD).astype(BF)

    collect(0, ge0)

    def two_groups(step, carry):
        number = step * 2
        attend(number, ge0)
        collect(number + 1, ge1)
        attend(number + 1, ge1)
        collect(jnp.minimum(number + 2, groups - 1), ge0)
        return carry

    lax.fori_loop(0, groups // 2, two_groups, 0)
    low = low_half((1, 128))
    parts = []
    for pair in range(PAIRS):
        values = av[:, pair * 128 : pair * 128 + 128]
        zero = jnp.zeros_like(values)
        parts.append(
            dot(z[2 * pair], jnp.where(low, values, zero))
            + dot(z[2 * pair + 1], jnp.where(low, zero, values))
        )
    encoded = jnp.concatenate(parts, axis=1).astype(BF)
    got[0].wait()
    rounded = (lat[...].astype(F32) + dot(encoded, w3[...])).astype(BF)
    latent[...] = rounded
    wide = rounded.astype(F32)
    center = wide - jnp.mean(wide, axis=1, keepdims=True)
    spread = jnp.mean(center * center, axis=1, keepdims=True)
    normed[...] = (center * lax.rsqrt(spread + 1e-05)).astype(BF)
    for copy in later:
        copy.wait()


def project_kernel(normed, win, wout, scale, wq, wk, wv, dq, do, q, k, v, aq, bo, co):
    rows = normed[...]
    q[...] = (dot(rows, wq[...]) * scale[1:2, :]).astype(BF)
    k[...] = dot(rows, wk[...]).astype(BF)
    v[...] = dot(rows, wv[...]).astype(BF)
    co[...] = dot_t(wout[...], win[...]).astype(BF)
    aq[...] = (dot(win[...], dq[...]) * scale[2:3, :]).astype(BF)
    bo[...] = dot_t(do[...], wout[...]).astype(BF)


def window_kernel(
    ends, q, k, v, nl, nr, latent, wk, wv, wo, out, head, tail, keys, values, bias, mixed
):
    rows = q.shape[0]
    half = rows // 2
    span = half + WIN
    keys[rows : 2 * rows, :] = k[...]
    values[rows : 2 * rows, :] = v[...]
    row = lax.broadcasted_iota(jnp.int32, (half, span), 0)
    col = lax.broadcasted_iota(jnp.int32, (half, span), 1)
    for side in range(2):
        place = col + side * half
        inside = (col >= row) & (col - row <= WIN) & (place >= ends[0]) & (place < ends[1])
        bias[side] = jnp.where(inside, 0.0, NEG)
    halo = jnp.concatenate([nl[...], nr[...]], axis=0)
    for weight, wide in ((wk, keys), (wv, values)):
        both = dot(halo, weight[...]).astype(BF)
        wide[:rows, :] = both[:rows]
        wide[2 * rows :, :] = both[rows:]
    low = low_half((1, 128))

    def one_pair(pair, carry):
        lanes = pl.ds(pl.multiple_of(pair * 128, 128), 128)
        for side in range(2):
            these = slice(side * half, side * half + half)
            near = slice(side * half, side * half + span)
            both = q[these, lanes]
            zero = jnp.zeros_like(both)
            stacked = jnp.concatenate(
                [jnp.where(low, both, zero), jnp.where(low, zero, both)], axis=0
            )
            near_values = values[near, lanes]
            score = dot_t(stacked, keys[near, lanes]).reshape(2, half, span) + bias[side][None]
            score = score.reshape(2 * half, span)
            expo = jnp.exp2(score - jnp.max(score, axis=1, keepdims=True)).astype(BF)
            total = dot(
                expo, jnp.concatenate([near_values, jnp.ones_like(near_values)], axis=1)
            )
            part = total[:, :128] / total[:, 128:]
            mixed[these, lanes] = jnp.where(low, part[:half], part[half:]).astype(BF)
        return carry

    lax.fori_loop(0, PAIRS, one_pair, 0, unroll=True)
    out[...] = (latent[...].astype(F32) + dot(mixed[...], wo[...])).astype(BF)
    head[...] = out[:BL, :]
    tail[...] = out[rows - BL :, :]


CHUNK = 128


def to_tiles(rows, weight, tiles, begin):
    count = rows.shape[0]
    for block in range(8):
        tiles[pl.ds(begin * 8 + block, count, stride=8), :] = dot(
            rows, weight[:, block * 128 : block * 128 + 128]
        )


def prepare_kernel(own, state, aq, wk, wv, q, k, v):
    to_tiles(own[...], wk, k, 0)
    to_tiles(own[...], wv, v, 0)
    points = state.shape[1]
    for first in range(0, points, 512):
        to_tiles(state[:, first : first + 512].astype(F32).T.astype(BF), aq, q, first)


def decode_kernel(
    idx, left, right, ko, vo, q, grid, bo, co, wk, wv, out, kf, vf, prod, wts, dec
):
    points = grid.shape[1]
    side = left.shape[0]
    halo = jnp.concatenate([left[...], right[...]], axis=0)
    for weight, tiles, own in ((wk, kf, ko), (wv, vf, vo)):
        tiles[side * 8 : side * 8 + own.shape[0], :] = own[...]
        for block in range(8):
            both = dot(halo, weight[:, block * 128 : block * 128 + 128])
            tiles[pl.ds(block, side, stride=8), :] = both[:side]
            tiles[pl.ds(side * 8 + own.shape[0] + block, side, stride=8), :] = both[side:]
    head_row = lax.broadcasted_iota(jnp.int32, (256, 256), 0) // SIZE
    head_col = lax.broadcasted_iota(jnp.int32, (256, 256), 1) // SIZE
    ones = jnp.where(head_row == head_col, 1.0, 0.0).astype(BF)
    sub = 128

    def one_chunk(number, carry):
        first = pl.multiple_of(number * CHUNK, CHUNK)

        def tile_of(tiles, edge, at):
            return tiles[pl.ds(pl.multiple_of(idx[edge * points + first + at], 8), 8), :]

        for quad in range(0, CHUNK, 4):
            mine = [
                q[pl.ds(pl.multiple_of((first + quad + at) * 8, 8), 8), :] for at in range(4)
            ]
            for edge in range(3):
                terms = [mine[at] * tile_of(kf, edge, quad + at) for at in range(4)]
                place = slice(quad * 4, quad * 4 + 16)
                prod[edge, place, 0:128] = jnp.concatenate([terms[0], terms[2]], axis=0).astype(BF)
                prod[edge, place, 128:256] = jnp.concatenate([terms[1], terms[3]], axis=0).astype(BF)
        for begin in range(0, CHUNK * 4, sub):
            score = dot(prod[:, begin : begin + sub, :].reshape(3 * sub, 256), ones)
            score = [score[edge * sub : edge * sub + sub] for edge in range(3)]
            highest = jnp.maximum(jnp.maximum(score[0], score[1]), score[2])
            expo = [jnp.exp2(part - highest) for part in score]
            inverse = 1.0 / (expo[0] + expo[1] + expo[2])
            for edge in range(3):
                wts[edge, begin : begin + sub, :] = expo[edge] * inverse
        for at in range(CHUNK):
            top = at // 4 * 16 + (at % 4) // 2 * 8
            lane = at % 2 * 128
            total = None
            for edge in range(3):
                term = wts[edge, top : top + 8, lane : lane + 128] * tile_of(vf, edge, at)
                total = term if total is None else total + term
            dec[pl.ds(pl.multiple_of((first + at) * 8, 8), 8), :] = total
        return carry

    lax.fori_loop(0, points // CHUNK, one_chunk, 0)
    block = 256
    for first in range(0, points, block):
        wide = jnp.concatenate(
            [dec[pl.ds(first * 8 + part, block, stride=8), :] for part in range(8)], axis=1
        ).astype(BF)
        result = dot(wide, bo[...]).T + dot(co[...], grid[:, first : first + block])
        out[:, first : first + block] = result[: out.shape[0], :].astype(BF)


def shape(dims, kind=BF):
    return jax.ShapeDtypeStruct(dims, kind)


def neighbours(head, tail):
    axes = ("wide", "narrow")
    count = lax.axis_size(axes)
    after = lax.ppermute(tail, axes, [(i, i + 1) for i in range(count - 1)])
    before = lax.ppermute(head, axes, [(i + 1, i) for i in range(count - 1)])
    return after, before


def on_device(
    grid_state,
    latent_init,
    enc_src,
    enc_count,
    dec_src,
    w_in,
    enc_w,
    proc_w,
    dec_w,
    w_out,
    logit_scale,
):
    points, channels = grid_state.shape
    rows, width = latent_init.shape
    slots = enc_src.shape[1]
    place = lax.axis_index(("wide", "narrow"))
    total = rows * lax.axis_size(("wide", "narrow"))
    weight = pltpu.VMEM((width, width), BF)
    dma = pltpu.SemaphoreType.DMA

    grid = jnp.concatenate(
        [
            grid_state.T,
            jnp.ones((1, points), BF),
            jnp.zeros((CPAD - channels - 1, points), BF),
        ],
        axis=0,
    )
    grid_left, grid_right = neighbours(grid[:, :BG], grid[:, points - BG :])
    win = jnp.pad(w_in, ((0, CPAD - channels), (0, 0)))
    wout = jnp.pad(w_out.T, ((0, CPAD - channels), (0, 0)))
    scale = jnp.repeat(logit_scale * (LOG2E / math.sqrt(SIZE)), SIZE, axis=1)
    enc_idx = jnp.clip(enc_src.T, 0, points + 2 * BG - 1).reshape(-1)
    live = jnp.arange(slots, dtype=jnp.int32)[:, None] < enc_count[None, :]
    bias = jnp.where(live, 0.0, NEG).astype(F32)
    bias = bias.reshape(slots, rows // 16, 16).transpose(1, 0, 2).reshape(rows // 16, slots * 16)
    dec_idx = jnp.clip(dec_src.T - (place * rows - BL), 0, rows + 2 * BL - 1).reshape(-1) * 8
    ends = jnp.stack([WIN // 2 - place * rows, total + WIN // 2 - place * rows])

    qt, av = pl.pallas_call(
        fold_kernel,
        out_shape=(shape((HEADS, rows, CPAD)), shape((CPAD, width))),
        in_specs=[VM, HBM, VM, VM] + [pl.BlockSpec(memory_space=pl.ANY)] * 5,
        out_specs=(VM, VM),
        scratch_shapes=[weight] * 3 + [dma((3,))],
        compiler_params=params(53),
        cost_estimate=pl.CostEstimate(flops=2 * 10**9, bytes_accessed=8 * 2**20, transcendentals=0),
        name="fold",
    )(win, enc_w, latent_init, scale, wout, enc_idx, bias, dec_idx, ends)
    square = shape((width, width))
    latent, normed, pw0, pw1, pw2, pw3, dw0, dw1, dw2, dw3 = pl.pallas_call(
        encode_kernel,
        out_shape=(shape((rows, width)),) * 2 + (square,) * 8,
        in_specs=[SM] + [VM] * 7 + [HBM] * 3,
        out_specs=(VM,) * 10,
        scratch_shapes=[
            pltpu.VMEM((points + 2 * BG, CPAD), F32),
            pltpu.VMEM((slots * 16, CPAD), F32),
            pltpu.VMEM((slots * 16, CPAD), F32),
            pltpu.VMEM((HEADS, rows, CPAD), BF),
            weight,
            dma((9,)),
        ],
        compiler_params=params(28),
        name="encode",
    )(enc_idx, grid_left, grid, grid_right, qt, bias, av, latent_init, enc_w, proc_w, dec_w)
    near_left, near_right = neighbours(normed, normed)
    q, k, v, aq, bo, co = pl.pallas_call(
        project_kernel,
        out_shape=(shape((rows, width)),) * 3
        + (shape((CPAD, width)), shape((width, CPAD)), shape((CPAD, CPAD))),
        in_specs=[VM] * 9,
        out_specs=(VM,) * 6,
        compiler_params=params(24),
        cost_estimate=pl.CostEstimate(flops=3 * 10**9, bytes_accessed=12 * 2**20, transcendentals=0),
        name="project",
    )(normed, win, wout, scale, pw0, pw1, pw2, dw0, dw3)
    latent_out, mesh_head, mesh_tail = pl.pallas_call(
        window_kernel,
        out_shape=(shape((rows, width)), shape((BL, width)), shape((BL, width))),
        in_specs=[SM] + [VM] * 9,
        out_specs=(VM,) * 3,
        scratch_shapes=[
            pltpu.VMEM((rows + WIN, width), BF),
            pltpu.VMEM((rows + WIN, width), BF),
            pltpu.VMEM((2, rows // 2, rows // 2 + WIN), F32),
            pltpu.VMEM((rows, width), BF),
        ],
        compiler_params=params(24),
        name="window",
    )(ends, q, k, v, near_left, near_right, latent, pw1, pw2, pw3)
    mesh_left, mesh_right = neighbours(mesh_head, mesh_tail)
    nodes = rows + 2 * BL
    dq, dk, dv = pl.pallas_call(
        prepare_kernel,
        out_shape=(
            shape((points * 8, 128), F32),
            shape((rows * 8, 128), F32),
            shape((rows * 8, 128), F32),
        ),
        in_specs=[VM] * 5,
        out_specs=(VM,) * 3,
        compiler_params=params(24),
        cost_estimate=pl.CostEstimate(flops=3 * 10**9, bytes_accessed=12 * 2**20, transcendentals=0),
        name="prepare",
    )(latent_out, grid, aq, dw1, dw2)
    out = pl.pallas_call(
        decode_kernel,
        out_shape=shape((channels, points)),
        in_specs=[SM] + [VM] * 10,
        out_specs=VM,
        scratch_shapes=[
            pltpu.VMEM((nodes * 8, 128), F32),
            pltpu.VMEM((nodes * 8, 128), F32),
            pltpu.VMEM((3, CHUNK * 4, 256), BF),
            pltpu.VMEM((3, CHUNK * 4, 256), F32),
            pltpu.VMEM((points * 8, 128), F32),
        ],
        compiler_params=params(32),
        name="decode",
    )(dec_idx, mesh_left, mesh_right, dk, dv, dq, grid, bo, co, dw1, dw2)
    return out.T


def solution(mesh):
    both = ("wide", "narrow")
    placed = (
        P(both, None),
        P(both, None),
        P(both, None),
        P(both),
        P(both, None),
        P(),
        P(),
        P(),
        P(),
        P(),
        P(),
    )
    return jax.shard_map(
        on_device,
        mesh=mesh,
        in_specs=placed,
        out_specs=P(both, None),
        check_vma=False,
    )
```

```python
import math

import jax
import jax.numpy as jnp
from jax import lax
from jax.experimental import pallas as pl
from jax.experimental.pallas import tpu as pltpu
from jax.sharding import PartitionSpec as P

WIN = 512
BG = 1024
BL = 128
HEADS = 16
SIZE = 64
PAIRS = HEADS // 2
CPAD = 128
LOG2E = math.log2(math.e)
NEG = -1e30
BF = jnp.bfloat16
F32 = jnp.float32

VM = pl.BlockSpec(memory_space=pltpu.VMEM)
SM = pl.BlockSpec(memory_space=pltpu.SMEM)
HBM = pl.BlockSpec(memory_space=pltpu.HBM)


def dot(a, b):
    return jnp.dot(a, b, preferred_element_type=F32)


def dot_t(a, b):
    return lax.dot_general(a, b, (((1,), (1,)), ((), ())), preferred_element_type=F32)


def low_half(shape):
    return lax.broadcasted_iota(jnp.int32, shape, len(shape) - 1) < SIZE


def sides(core, near, far):
    return jnp.where(core == 0, far, near), jnp.where(core == 0, near, far)


def params(mib):
    return pltpu.CompilerParams(vmem_limit_bytes=mib * 2**20)


def fetch(source, rows, buffers, sems):
    copies = [
        pltpu.make_async_copy(source.at[row], buf, sems.at[at])
        for row, buf, at in zip(rows, buffers, range(len(rows)))
    ]
    for copy in copies:
        copy.start()
    return copies


def fold_kernel(win, enc_w, lat, scale, *others):
    qt, av, w0, w1, w2, sems = others[-6:]
    got = fetch(enc_w, (1, 0, 2), (w1, w0, w2), sems)
    got[0].wait()
    ak = dot(win[...], w1[...]).astype(BF)
    got[1].wait()
    q = (dot(lat[...], w0[...]) * scale[0:1, :]).astype(BF)
    low = low_half((1, 128))
    for pair in range(PAIRS):
        at = slice(pair * 128, pair * 128 + 128)
        keys = ak[:, at]
        both = q[:, at]
        zero = jnp.zeros_like(both)
        qt[2 * pair] = dot_t(jnp.where(low, both, zero), keys).astype(BF)
        qt[2 * pair + 1] = dot_t(jnp.where(low, zero, both), keys).astype(BF)
    got[2].wait()
    av[...] = dot(win[...], w2[...]).astype(BF)


def encode_kernel(
    ends, idx, near, own, far, qt, bias, av, lat, enc_w, proc_w, dec_w,
    latent, normed, pw0, pw1, pw2, pw3, dw0, dw1, dw2, dw3,
    grid, ge0, ge1, z, w3, sems,
):
    got = fetch(enc_w, (3,), (w3,), sems.at[pl.ds(0, 1)])
    later = fetch(proc_w, (0, 1, 2, 3), (pw0, pw1, pw2, pw3), sems.at[pl.ds(1, 4)])
    later += fetch(dec_w, (0, 3, 1, 2), (dw0, dw3, dw1, dw2), sems.at[pl.ds(5, 4)])
    rows = lat.shape[0]
    groups = rows // 16
    at = 0
    left, right = sides(ends[2], near[...], far[...])
    for piece in (left, own[...], right):
        for begin in range(0, piece.shape[1], 512):
            grid[at : at + 512, :] = piece[:, begin : begin + 512].astype(F32).T
            at += 512
    row = lax.broadcasted_iota(jnp.int32, (256, 256), 0)
    col = lax.broadcasted_iota(jnp.int32, (256, 256), 1)
    diag = jnp.where(row % 16 == col % 16, 0.0, NEG)

    def collect(number, ge):
        base = number * 16
        for slot in range(16):
            for node in range(16):
                edge = slot * 16 + node
                ge[pl.ds(edge, 1), :] = grid[pl.ds(idx[base + (slot * rows + node)], 1), :]

    def attend(number, ge):
        points = ge[...].astype(BF)
        base = pl.multiple_of(number * 16, 16)
        queries = qt[:, pl.ds(base, 16), :].reshape(256, CPAD)
        score = dot_t(queries, points) + (diag + bias[pl.ds(number, 1), :])
        expo = jnp.exp2(score - jnp.max(score, axis=1, keepdims=True)).astype(BF)
        mixed = dot(expo, points)
        mixed = mixed / mixed[:, 100:101]
        z[:, pl.ds(base, 16), :] = mixed.reshape(16, 16, CPAD).astype(BF)

    collect(0, ge0)

    def two_groups(step, carry):
        number = step * 2
        attend(number, ge0)
        collect(number + 1, ge1)
        attend(number + 1, ge1)
        collect(jnp.minimum(number + 2, groups - 1), ge0)
        return carry

    lax.fori_loop(0, groups // 2, two_groups, 0)
    low = low_half((1, 128))
    parts = []
    for pair in range(PAIRS):
        values = av[:, pair * 128 : pair * 128 + 128]
        zero = jnp.zeros_like(values)
        parts.append(
            dot(z[2 * pair], jnp.where(low, values, zero))
            + dot(z[2 * pair + 1], jnp.where(low, zero, values))
        )
    encoded = jnp.concatenate(parts, axis=1).astype(BF)
    got[0].wait()
    rounded = (lat[...].astype(F32) + dot(encoded, w3[...])).astype(BF)
    latent[...] = rounded
    wide = rounded.astype(F32)
    center = wide - jnp.mean(wide, axis=1, keepdims=True)
    spread = jnp.mean(center * center, axis=1, keepdims=True)
    normed[...] = (center * lax.rsqrt(spread + 1e-05)).astype(BF)
    for copy in later:
        copy.wait()


def project_kernel(normed, win, wout, scale, wq, wk, wv, dq, do, q, k, v, aq, bo, co):
    rows = normed[...]
    q[...] = (dot(rows, wq[...]) * scale[1:2, :]).astype(BF)
    k[...] = dot(rows, wk[...]).astype(BF)
    v[...] = dot(rows, wv[...]).astype(BF)
    co[...] = dot_t(wout[...], win[...]).astype(BF)
    aq[...] = (dot(win[...], dq[...]) * scale[2:3, :]).astype(BF)
    bo[...] = dot_t(do[...], wout[...]).astype(BF)


def window_kernel(
    ends, q, k, v, near, far, latent, wk, wv, wo, out, inner, outer, keys, values, bias, mixed
):
    rows = q.shape[0]
    half = rows // 2
    span = half + WIN
    keys[rows : 2 * rows, :] = k[...]
    values[rows : 2 * rows, :] = v[...]
    row = lax.broadcasted_iota(jnp.int32, (half, span), 0)
    col = lax.broadcasted_iota(jnp.int32, (half, span), 1)
    for side in range(2):
        place = col + side * half
        inside = (col >= row) & (col - row <= WIN) & (place >= ends[0]) & (place < ends[1])
        bias[side] = jnp.where(inside, 0.0, NEG)
    halo = jnp.concatenate(sides(ends[2], near[...], far[...]), axis=0)
    for weight, wide in ((wk, keys), (wv, values)):
        both = dot(halo, weight[...]).astype(BF)
        wide[:rows, :] = both[:rows]
        wide[2 * rows :, :] = both[rows:]
    low = low_half((1, 128))

    def one_pair(pair, carry):
        lanes = pl.ds(pl.multiple_of(pair * 128, 128), 128)
        for side in range(2):
            these = slice(side * half, side * half + half)
            band = slice(side * half, side * half + span)
            both = q[these, lanes]
            zero = jnp.zeros_like(both)
            stacked = jnp.concatenate(
                [jnp.where(low, both, zero), jnp.where(low, zero, both)], axis=0
            )
            near_values = values[band, lanes]
            score = dot_t(stacked, keys[band, lanes]).reshape(2, half, span) + bias[side][None]
            score = score.reshape(2 * half, span)
            expo = jnp.exp2(score - jnp.max(score, axis=1, keepdims=True)).astype(BF)
            total = dot(
                expo, jnp.concatenate([near_values, jnp.ones_like(near_values)], axis=1)
            )
            part = total[:, :128] / total[:, 128:]
            mixed[these, lanes] = jnp.where(low, part[:half], part[half:]).astype(BF)
        return carry

    lax.fori_loop(0, PAIRS, one_pair, 0, unroll=True)
    out[...] = (latent[...].astype(F32) + dot(mixed[...], wo[...])).astype(BF)
    inner[...], outer[...] = sides(ends[2], out[:BL, :], out[rows - BL :, :])


CHUNK = 128


def to_tiles(rows, weight, tiles, begin):
    count = rows.shape[0]
    for block in range(8):
        tiles[pl.ds(begin * 8 + block, count, stride=8), :] = dot(
            rows, weight[:, block * 128 : block * 128 + 128]
        )


def prepare_kernel(own, state, aq, wk, wv, q, k, v):
    to_tiles(own[...], wk, k, 0)
    to_tiles(own[...], wv, v, 0)
    points = state.shape[1]
    for first in range(0, points, 512):
        to_tiles(state[:, first : first + 512].astype(F32).T.astype(BF), aq, q, first)


def decode_kernel(
    ends, idx, near, far, ko, vo, q, grid, bo, co, wk, wv, out, kf, vf, prod, wts, dec
):
    points = grid.shape[1]
    side = near.shape[0]
    halo = jnp.concatenate(sides(ends[2], near[...], far[...]), axis=0)
    for weight, tiles, own in ((wk, kf, ko), (wv, vf, vo)):
        tiles[side * 8 : side * 8 + own.shape[0], :] = own[...]
        for block in range(8):
            both = dot(halo, weight[:, block * 128 : block * 128 + 128])
            tiles[pl.ds(block, side, stride=8), :] = both[:side]
            tiles[pl.ds(side * 8 + own.shape[0] + block, side, stride=8), :] = both[side:]
    head_row = lax.broadcasted_iota(jnp.int32, (256, 256), 0) // SIZE
    head_col = lax.broadcasted_iota(jnp.int32, (256, 256), 1) // SIZE
    ones = jnp.where(head_row == head_col, 1.0, 0.0).astype(BF)
    sub = 128

    def one_chunk(number, carry):
        first = pl.multiple_of(number * CHUNK, CHUNK)

        def tile_of(tiles, edge, at):
            return tiles[pl.ds(pl.multiple_of(idx[edge * points + first + at], 8), 8), :]

        for quad in range(0, CHUNK, 4):
            mine = [
                q[pl.ds(pl.multiple_of((first + quad + at) * 8, 8), 8), :] for at in range(4)
            ]
            for edge in range(3):
                terms = [mine[at] * tile_of(kf, edge, quad + at) for at in range(4)]
                place = slice(quad * 4, quad * 4 + 16)
                prod[edge, place, 0:128] = jnp.concatenate([terms[0], terms[2]], axis=0).astype(BF)
                prod[edge, place, 128:256] = jnp.concatenate([terms[1], terms[3]], axis=0).astype(BF)
        for begin in range(0, CHUNK * 4, sub):
            score = dot(prod[:, begin : begin + sub, :].reshape(3 * sub, 256), ones)
            score = [score[edge * sub : edge * sub + sub] for edge in range(3)]
            highest = jnp.maximum(jnp.maximum(score[0], score[1]), score[2])
            expo = [jnp.exp2(part - highest) for part in score]
            inverse = 1.0 / (expo[0] + expo[1] + expo[2])
            for edge in range(3):
                wts[edge, begin : begin + sub, :] = expo[edge] * inverse
        for at in range(CHUNK):
            top = at // 4 * 16 + (at % 4) // 2 * 8
            lane = at % 2 * 128
            total = None
            for edge in range(3):
                term = wts[edge, top : top + 8, lane : lane + 128] * tile_of(vf, edge, at)
                total = term if total is None else total + term
            dec[pl.ds(pl.multiple_of((first + at) * 8, 8), 8), :] = total
        return carry

    lax.fori_loop(0, points // CHUNK, one_chunk, 0)
    block = 256
    for first in range(0, points, block):
        wide = jnp.concatenate(
            [dec[pl.ds(first * 8 + part, block, stride=8), :] for part in range(8)], axis=1
        ).astype(BF)
        result = dot(wide, bo[...]).T + dot(co[...], grid[:, first : first + block])
        out[:, first : first + block] = result[: out.shape[0], :].astype(BF)


def shape(dims, kind=BF):
    return jax.ShapeDtypeStruct(dims, kind)


def swap(inner, outer):
    axes = ("wide", "narrow")
    count = lax.axis_size(axes)
    pairs = []
    for i in range(1, count - 1, 2):
        pairs += [(i, i + 1), (i + 1, i)]
    far = lax.ppermute(outer, axes, pairs)
    near = lax.ppermute(inner, "narrow", [(0, 1), (1, 0)])
    return near, far


def on_device(
    grid_state,
    latent_init,
    enc_src,
    enc_count,
    dec_src,
    w_in,
    enc_w,
    proc_w,
    dec_w,
    w_out,
    logit_scale,
):
    points, channels = grid_state.shape
    rows, width = latent_init.shape
    slots = enc_src.shape[1]
    place = lax.axis_index(("wide", "narrow"))
    total = rows * lax.axis_size(("wide", "narrow"))
    weight = pltpu.VMEM((width, width), BF)
    dma = pltpu.SemaphoreType.DMA

    grid = jnp.concatenate(
        [
            grid_state.T,
            jnp.ones((1, points), BF),
            jnp.zeros((CPAD - channels - 1, points), BF),
        ],
        axis=0,
    )
    core = lax.axis_index("narrow")
    grid_near, grid_far = swap(
        lax.dynamic_slice_in_dim(grid, (1 - core) * (points - BG), BG, 1),
        lax.dynamic_slice_in_dim(grid, core * (points - BG), BG, 1),
    )
    win = jnp.pad(w_in, ((0, CPAD - channels), (0, 0)))
    wout = jnp.pad(w_out.T, ((0, CPAD - channels), (0, 0)))
    scale = jnp.repeat(logit_scale * (LOG2E / math.sqrt(SIZE)), SIZE, axis=1)
    enc_idx = jnp.clip(enc_src.T, 0, points + 2 * BG - 1).reshape(-1)
    live = jnp.arange(slots, dtype=jnp.int32)[:, None] < enc_count[None, :]
    bias = jnp.where(live, 0.0, NEG).astype(F32)
    bias = bias.reshape(slots, rows // 16, 16).transpose(1, 0, 2).reshape(rows // 16, slots * 16)
    dec_idx = jnp.clip(dec_src.T - (place * rows - BL), 0, rows + 2 * BL - 1).reshape(-1) * 8
    ends = jnp.stack([WIN // 2 - place * rows, total + WIN // 2 - place * rows, core])

    qt, av = pl.pallas_call(
        fold_kernel,
        out_shape=(shape((HEADS, rows, CPAD)), shape((CPAD, width))),
        in_specs=[VM, HBM, VM, VM] + [pl.BlockSpec(memory_space=pl.ANY)] * 5,
        out_specs=(VM, VM),
        scratch_shapes=[weight] * 3 + [dma((3,))],
        compiler_params=params(53),
        cost_estimate=pl.CostEstimate(flops=2 * 10**9, bytes_accessed=8 * 2**20, transcendentals=0),
        name="fold",
    )(win, enc_w, latent_init, scale, wout, enc_idx, bias, dec_idx, ends)
    square = shape((width, width))
    latent, normed, pw0, pw1, pw2, pw3, dw0, dw1, dw2, dw3 = pl.pallas_call(
        encode_kernel,
        out_shape=(shape((rows, width)),) * 2 + (square,) * 8,
        in_specs=[SM] * 2 + [VM] * 7 + [HBM] * 3,
        out_specs=(VM,) * 10,
        scratch_shapes=[
            pltpu.VMEM((points + 2 * BG, CPAD), F32),
            pltpu.VMEM((slots * 16, CPAD), F32),
            pltpu.VMEM((slots * 16, CPAD), F32),
            pltpu.VMEM((HEADS, rows, CPAD), BF),
            weight,
            dma((9,)),
        ],
        compiler_params=params(28),
        name="encode",
    )(ends, enc_idx, grid_near, grid, grid_far, qt, bias, av, latent_init, enc_w, proc_w, dec_w)
    normed_near, normed_far = swap(normed, normed)
    q, k, v, aq, bo, co = pl.pallas_call(
        project_kernel,
        out_shape=(shape((rows, width)),) * 3
        + (shape((CPAD, width)), shape((width, CPAD)), shape((CPAD, CPAD))),
        in_specs=[VM] * 9,
        out_specs=(VM,) * 6,
        compiler_params=params(24),
        cost_estimate=pl.CostEstimate(flops=3 * 10**9, bytes_accessed=12 * 2**20, transcendentals=0),
        name="project",
    )(normed, win, wout, scale, pw0, pw1, pw2, dw0, dw3)
    latent_out, mesh_inner, mesh_outer = pl.pallas_call(
        window_kernel,
        out_shape=(shape((rows, width)), shape((BL, width)), shape((BL, width))),
        in_specs=[SM] + [VM] * 9,
        out_specs=(VM,) * 3,
        scratch_shapes=[
            pltpu.VMEM((rows + WIN, width), BF),
            pltpu.VMEM((rows + WIN, width), BF),
            pltpu.VMEM((2, rows // 2, rows // 2 + WIN), F32),
            pltpu.VMEM((rows, width), BF),
        ],
        compiler_params=params(24),
        name="window",
    )(ends, q, k, v, normed_near, normed_far, latent, pw1, pw2, pw3)
    mesh_near, mesh_far = swap(mesh_inner, mesh_outer)
    nodes = rows + 2 * BL
    dq, dk, dv = pl.pallas_call(
        prepare_kernel,
        out_shape=(
            shape((points * 8, 128), F32),
            shape((rows * 8, 128), F32),
            shape((rows * 8, 128), F32),
        ),
        in_specs=[VM] * 5,
        out_specs=(VM,) * 3,
        compiler_params=params(24),
        cost_estimate=pl.CostEstimate(flops=3 * 10**9, bytes_accessed=12 * 2**20, transcendentals=0),
        name="prepare",
    )(latent_out, grid, aq, dw1, dw2)
    out = pl.pallas_call(
        decode_kernel,
        out_shape=shape((channels, points)),
        in_specs=[SM] * 2 + [VM] * 10,
        out_specs=VM,
        scratch_shapes=[
            pltpu.VMEM((nodes * 8, 128), F32),
            pltpu.VMEM((nodes * 8, 128), F32),
            pltpu.VMEM((3, CHUNK * 4, 256), BF),
            pltpu.VMEM((3, CHUNK * 4, 256), F32),
            pltpu.VMEM((points * 8, 128), F32),
        ],
        compiler_params=params(32),
        name="decode",
    )(ends, dec_idx, mesh_near, mesh_far, dk, dv, dq, grid, bo, co, dw1, dw2)
    return out.T


def solution(mesh):
    both = ("wide", "narrow")
    placed = (
        P(both, None),
        P(both, None),
        P(both, None),
        P(both),
        P(both, None),
        P(),
        P(),
        P(),
        P(),
        P(),
        P(),
    )
    return jax.shard_map(
        on_device,
        mesh=mesh,
        in_specs=placed,
        out_specs=P(both, None),
        check_vma=False,
    )
```

```python
import math

import jax
import jax.numpy as jnp
from jax import lax
from jax.experimental import pallas as pl
from jax.experimental.pallas import tpu as pltpu
from jax.sharding import PartitionSpec as P

WIN = 512
BG = 1024
BL = 128
HEADS = 16
SIZE = 64
PAIRS = HEADS // 2
CPAD = 128
CSENT = 112
LOG2E = math.log2(math.e)
NEG = -1e30
BF = jnp.bfloat16
F32 = jnp.float32

VM = pl.BlockSpec(memory_space=pltpu.VMEM)
SM = pl.BlockSpec(memory_space=pltpu.SMEM)
HBM = pl.BlockSpec(memory_space=pltpu.HBM)


def dot(a, b):
    return jnp.dot(a, b, preferred_element_type=F32)


def dot_t(a, b):
    return lax.dot_general(a, b, (((1,), (1,)), ((), ())), preferred_element_type=F32)


def low_half(shape):
    return lax.broadcasted_iota(jnp.int32, shape, len(shape) - 1) < SIZE


def sides(core, near, far):
    return jnp.where(core == 0, far, near), jnp.where(core == 0, near, far)


def params(mib):
    return pltpu.CompilerParams(vmem_limit_bytes=mib * 2**20)


def fetch(source, rows, buffers, sems):
    copies = [
        pltpu.make_async_copy(source.at[row], buf, sems.at[at])
        for row, buf, at in zip(rows, buffers, range(len(rows)))
    ]
    for copy in copies:
        copy.start()
    return copies


def fold_kernel(win, enc_w, lat, scale, *others):
    qt, w0, w1, sems = others[-4:]
    got = fetch(enc_w, (1, 0), (w1, w0), sems)
    got[0].wait()
    ak = dot(win[...], w1[...]).astype(BF)
    got[1].wait()
    q = (dot(lat[...], w0[...]) * scale[0:1, :]).astype(BF)
    low = low_half((1, 128))
    for pair in range(PAIRS):
        at = slice(pair * 128, pair * 128 + 128)
        keys = ak[:, at]
        both = q[:, at]
        zero = jnp.zeros_like(both)
        qt[2 * pair] = dot_t(jnp.where(low, both, zero), keys).astype(BF)
        qt[2 * pair + 1] = dot_t(jnp.where(low, zero, both), keys).astype(BF)


def encode_kernel(
    ends, idx, near, own, far, qt, bias, win, lat, enc_w, proc_w, dec_w,
    latent, normed, pw0, pw1, pw2, pw3, dw0, dw1, dw2, dw3,
    grid, ge0, ge1, ge2, ge3, z, w2, w3, sems,
):
    got = fetch(enc_w, (2, 3), (w2, w3), sems.at[pl.ds(8, 2)])
    later = fetch(proc_w, (0, 1, 2, 3), (pw0, pw1, pw2, pw3), sems.at[pl.ds(0, 4)])
    later += fetch(dec_w, (0, 3, 1, 2), (dw0, dw3, dw1, dw2), sems.at[pl.ds(4, 4)])
    rows = lat.shape[0]
    groups = rows // 16
    at = 0
    left, right = sides(ends[2], near[...], far[...])
    empty = jnp.zeros((CPAD - CSENT, 512), BF)
    for piece in (left, own[:CSENT, :], right):
        for begin in range(0, piece.shape[1], 512):
            part = jnp.concatenate([piece[:, begin : begin + 512], empty], axis=0)
            grid[at : at + 512, :] = part.astype(F32).T
            at += 512
    row = lax.broadcasted_iota(jnp.int32, (256, 256), 0)
    col = lax.broadcasted_iota(jnp.int32, (256, 256), 1)
    diag = jnp.where(row % 16 == col % 16, 0.0, NEG)

    def collect(number, ge):
        base = number * 16
        for slot in range(16):
            for node in range(16):
                edge = slot * 16 + node
                ge[pl.ds(edge, 1), :] = grid[pl.ds(idx[base + (slot * rows + node)], 1), :]

    def attend(numbers, buffers):
        points = [ge[...].astype(BF) for ge in buffers]
        score = [
            dot_t(qt[:, number * 16 : number * 16 + 16, :].reshape(256, CPAD), rows_of)
            + (diag + bias[number : number + 1, :])
            for number, rows_of in zip(numbers, points)
        ]
        expo = [
            jnp.exp2(part - jnp.max(part, axis=1, keepdims=True)).astype(BF) for part in score
        ]
        for number, part, rows_of in zip(numbers, expo, points):
            mixed = dot(part, rows_of)
            mixed = mixed * (1.0 / mixed[:, 100:101])
            z[:, number * 16 : number * 16 + 16, :] = mixed.reshape(16, 16, CPAD).astype(BF)

    buffers = ((ge0, ge1), (ge2, ge3))
    for number in range(0, groups + 2, 2):
        if number < groups:
            for at in range(2):
                collect(number + at, buffers[number // 2 % 2][at])
        if number:
            attend((number - 2, number - 1), buffers[(number // 2 + 1) % 2])
    got[0].wait()
    av = dot(win[...], w2[...]).astype(BF)
    low = low_half((1, 128))
    parts = []
    for pair in range(PAIRS):
        values = av[:, pair * 128 : pair * 128 + 128]
        zero = jnp.zeros_like(values)
        parts.append(
            dot(z[2 * pair], jnp.where(low, values, zero))
            + dot(z[2 * pair + 1], jnp.where(low, zero, values))
        )
    encoded = jnp.concatenate(parts, axis=1).astype(BF)
    got[1].wait()
    rounded = (lat[...].astype(F32) + dot(encoded, w3[...])).astype(BF)
    latent[...] = rounded
    wide = rounded.astype(F32)
    center = wide - jnp.mean(wide, axis=1, keepdims=True)
    spread = jnp.mean(center * center, axis=1, keepdims=True)
    normed[...] = (center * lax.rsqrt(spread + 1e-05)).astype(BF)
    for copy in later:
        copy.wait()


def project_kernel(normed, win, wout, scale, wq, wk, wv, dq, do, q, k, v, aq, bo, co):
    rows = normed[...]
    q[...] = (dot(rows, wq[...]) * scale[1:2, :]).astype(BF)
    k[...] = dot(rows, wk[...]).astype(BF)
    v[...] = dot(rows, wv[...]).astype(BF)
    co[...] = dot_t(wout[...], win[...]).astype(BF)
    aq[...] = (dot(win[...], dq[...]) * scale[2:3, :]).astype(BF)
    bo[...] = dot_t(do[...], wout[...]).astype(BF)


def window_kernel(
    ends, q, k, v, near, far, latent, wk, wv, wo, out, inner, outer, keys, values, bias, mixed
):
    rows = q.shape[0]
    half = rows // 2
    span = half + WIN
    keys[rows : 2 * rows, :] = k[...]
    values[rows : 2 * rows, :] = v[...]
    row = lax.broadcasted_iota(jnp.int32, (half, span), 0)
    col = lax.broadcasted_iota(jnp.int32, (half, span), 1)
    for side in range(2):
        place = col + side * half
        inside = (col >= row) & (col - row <= WIN) & (place >= ends[0]) & (place < ends[1])
        bias[side] = jnp.where(inside, 0.0, NEG)
    halo = jnp.concatenate(sides(ends[2], near[...], far[...]), axis=0)
    for weight, wide in ((wk, keys), (wv, values)):
        both = dot(halo, weight[...]).astype(BF)
        wide[:rows, :] = both[:rows]
        wide[2 * rows :, :] = both[rows:]
    low = low_half((1, 128))

    for pair in range(PAIRS):
        lanes = slice(pair * 128, pair * 128 + 128)
        bands = [slice(side * half, side * half + span) for side in range(2)]
        score = []
        for side in range(2):
            both = q[side * half : side * half + half, lanes]
            zero = jnp.zeros_like(both)
            stacked = jnp.concatenate(
                [jnp.where(low, both, zero), jnp.where(low, zero, both)], axis=0
            )
            part = dot_t(stacked, keys[bands[side], lanes])
            score.append(
                (part.reshape(2, half, span) + bias[side][None]).reshape(2 * half, span)
            )
        expo = [
            jnp.exp2(part - jnp.max(part, axis=1, keepdims=True)).astype(BF) for part in score
        ]
        for side in range(2):
            near_values = values[bands[side], lanes]
            total = dot(
                expo[side], jnp.concatenate([near_values, jnp.ones_like(near_values)], axis=1)
            )
            part = total[:, :128] * (1.0 / total[:, 128:])
            mixed[side * half : side * half + half, lanes] = jnp.where(
                low, part[:half], part[half:]
            ).astype(BF)
    out[...] = (latent[...].astype(F32) + dot(mixed[...], wo[...])).astype(BF)
    inner[...], outer[...] = sides(ends[2], out[:BL, :], out[rows - BL :, :])


CHUNK = 128


def to_tiles(rows, weight, tiles, begin):
    count = rows.shape[0]
    for block in range(8):
        tiles[begin : begin + count, block, :] = dot(
            rows, weight[:, block * 128 : block * 128 + 128]
        )


def prepare_kernel(own, state, aq, wk, wv, q, k, v):
    to_tiles(own[...], wk, k, 0)
    to_tiles(own[...], wv, v, 0)
    points = state.shape[1]
    for first in range(0, points, 512):
        to_tiles(state[:, first : first + 512].astype(F32).T.astype(BF), aq, q, first)


def decode_kernel(
    ends, idx, near, far, ko, vo, q, grid, bo, co, wk, wv, out, kf, vf, prod, wts, dec
):
    points = grid.shape[1]
    side = near.shape[0]
    halo = jnp.concatenate(sides(ends[2], near[...], far[...]), axis=0)
    for weight, tiles, own in ((wk, kf, ko), (wv, vf, vo)):
        tiles[side : side + own.shape[0]] = own[...]
        for block in range(8):
            both = dot(halo, weight[:, block * 128 : block * 128 + 128])
            tiles[:side, block, :] = both[:side]
            tiles[side + own.shape[0] :, block, :] = both[side:]
    head_row = lax.broadcasted_iota(jnp.int32, (256, 256), 0) // SIZE
    head_col = lax.broadcasted_iota(jnp.int32, (256, 256), 1) // SIZE
    ones = jnp.where(head_row == head_col, 1.0, 0.0).astype(BF)
    sub = 128

    def one_chunk(number, carry):
        first = pl.multiple_of(number * CHUNK, CHUNK)

        def tile_of(tiles, edge, at):
            return tiles[idx[edge * points + first + at]]

        for quad in range(0, CHUNK, 4):
            mine = [
                q[first + quad + at] for at in range(4)
            ]
            for edge in range(3):
                terms = [mine[at] * tile_of(kf, edge, quad + at) for at in range(4)]
                place = slice(quad * 4, quad * 4 + 16)
                prod[edge, place, 0:128] = jnp.concatenate([terms[0], terms[2]], axis=0).astype(BF)
                prod[edge, place, 128:256] = jnp.concatenate([terms[1], terms[3]], axis=0).astype(BF)
        for begin in range(0, CHUNK * 4, sub):
            score = dot(prod[:, begin : begin + sub, :].reshape(3 * sub, 256), ones)
            score = [score[edge * sub : edge * sub + sub] for edge in range(3)]
            highest = jnp.maximum(jnp.maximum(score[0], score[1]), score[2])
            expo = [jnp.exp2(part - highest) for part in score]
            inverse = 1.0 / (expo[0] + expo[1] + expo[2])
            for edge in range(3):
                wts[edge, begin : begin + sub, :] = expo[edge] * inverse
        for at in range(CHUNK):
            top = at // 4 * 16 + (at % 4) // 2 * 8
            lane = at % 2 * 128
            total = None
            for edge in range(3):
                term = wts[edge, top : top + 8, lane : lane + 128] * tile_of(vf, edge, at)
                total = term if total is None else total + term
            dec[first + at] = total
        return carry

    lax.fori_loop(0, points // CHUNK, one_chunk, 0)
    block = 256
    for first in range(0, points, block):
        wide = jnp.concatenate(
            [dec[first : first + block, part, :] for part in range(8)], axis=1
        ).astype(BF)
        result = dot(wide, bo[...]).T + dot(co[...], grid[:, first : first + block])
        out[:, first : first + block] = result[: out.shape[0], :].astype(BF)


def shape(dims, kind=BF):
    return jax.ShapeDtypeStruct(dims, kind)


def swap(inner, outer):
    axes = ("wide", "narrow")
    count = lax.axis_size(axes)
    pairs = []
    for i in range(1, count - 1, 2):
        pairs += [(i, i + 1), (i + 1, i)]
    far = lax.ppermute(outer, axes, pairs)
    near = lax.ppermute(inner, "narrow", [(0, 1), (1, 0)])
    return near, far


def on_device(
    grid_state,
    latent_init,
    enc_src,
    enc_count,
    dec_src,
    w_in,
    enc_w,
    proc_w,
    dec_w,
    w_out,
    logit_scale,
):
    points, channels = grid_state.shape
    rows, width = latent_init.shape
    slots = enc_src.shape[1]
    place = lax.axis_index(("wide", "narrow"))
    total = rows * lax.axis_size(("wide", "narrow"))
    weight = pltpu.VMEM((width, width), BF)
    dma = pltpu.SemaphoreType.DMA

    grid = jnp.concatenate(
        [
            grid_state.T,
            jnp.ones((1, points), BF),
            jnp.zeros((CPAD - channels - 1, points), BF),
        ],
        axis=0,
    )
    core = lax.axis_index("narrow")
    grid_near, grid_far = swap(
        lax.dynamic_slice_in_dim(grid[:CSENT], (1 - core) * (points - BG), BG, 1),
        lax.dynamic_slice_in_dim(grid[:CSENT], core * (points - BG), BG, 1),
    )
    win = jnp.pad(w_in, ((0, CPAD - channels), (0, 0)))
    wout = jnp.pad(w_out.T, ((0, CPAD - channels), (0, 0)))
    scale = jnp.repeat(logit_scale * (LOG2E / math.sqrt(SIZE)), SIZE, axis=1)
    enc_idx = jnp.clip(enc_src.T, 0, points + 2 * BG - 1).reshape(-1)
    live = jnp.arange(slots, dtype=jnp.int32)[:, None] < enc_count[None, :]
    bias = jnp.where(live, 0.0, NEG).astype(F32)
    bias = bias.reshape(slots, rows // 16, 16).transpose(1, 0, 2).reshape(rows // 16, slots * 16)
    dec_idx = jnp.clip(dec_src.T - (place * rows - BL), 0, rows + 2 * BL - 1).reshape(-1)
    ends = jnp.stack([WIN // 2 - place * rows, total + WIN // 2 - place * rows, core])

    qt = pl.pallas_call(
        fold_kernel,
        out_shape=shape((HEADS, rows, CPAD)),
        in_specs=[VM, HBM, VM, VM] + [pl.BlockSpec(memory_space=pl.ANY)] * 5,
        out_specs=VM,
        scratch_shapes=[weight] * 2 + [dma((2,))],
        compiler_params=params(53),
        cost_estimate=pl.CostEstimate(flops=2 * 10**9, bytes_accessed=8 * 2**20, transcendentals=0),
        name="fold",
    )(win, enc_w, latent_init, scale, wout, enc_idx, bias, dec_idx, ends)
    square = shape((width, width))
    latent, normed, pw0, pw1, pw2, pw3, dw0, dw1, dw2, dw3 = pl.pallas_call(
        encode_kernel,
        out_shape=(shape((rows, width)),) * 2 + (square,) * 8,
        in_specs=[SM] * 2 + [VM] * 7 + [HBM] * 3,
        out_specs=(VM,) * 10,
        scratch_shapes=[
            pltpu.VMEM((points + 2 * BG, CPAD), F32),
            pltpu.VMEM((slots * 16, CPAD), F32),
            pltpu.VMEM((slots * 16, CPAD), F32),
            pltpu.VMEM((slots * 16, CPAD), F32),
            pltpu.VMEM((slots * 16, CPAD), F32),
            pltpu.VMEM((HEADS, rows, CPAD), BF),
            weight,
            weight,
            dma((10,)),
        ],
        compiler_params=params(28),
        name="encode",
    )(ends, enc_idx, grid_near, grid, grid_far, qt, bias, win, latent_init, enc_w, proc_w, dec_w)
    normed_near, normed_far = swap(normed, normed)
    q, k, v, aq, bo, co = pl.pallas_call(
        project_kernel,
        out_shape=(shape((rows, width)),) * 3
        + (shape((CPAD, width)), shape((width, CPAD)), shape((CPAD, CPAD))),
        in_specs=[VM] * 9,
        out_specs=(VM,) * 6,
        compiler_params=params(24),
        cost_estimate=pl.CostEstimate(flops=3 * 10**9, bytes_accessed=12 * 2**20, transcendentals=0),
        name="project",
    )(normed, win, wout, scale, pw0, pw1, pw2, dw0, dw3)
    latent_out, mesh_inner, mesh_outer = pl.pallas_call(
        window_kernel,
        out_shape=(shape((rows, width)), shape((BL, width)), shape((BL, width))),
        in_specs=[SM] + [VM] * 9,
        out_specs=(VM,) * 3,
        scratch_shapes=[
            pltpu.VMEM((rows + WIN, width), BF),
            pltpu.VMEM((rows + WIN, width), BF),
            pltpu.VMEM((2, rows // 2, rows // 2 + WIN), F32),
            pltpu.VMEM((rows, width), BF),
        ],
        compiler_params=params(24),
        name="window",
    )(ends, q, k, v, normed_near, normed_far, latent, pw1, pw2, pw3)
    mesh_near, mesh_far = swap(mesh_inner, mesh_outer)
    nodes = rows + 2 * BL
    dq, dk, dv = pl.pallas_call(
        prepare_kernel,
        out_shape=(
            shape((points, 8, 128), F32),
            shape((rows, 8, 128), F32),
            shape((rows, 8, 128), F32),
        ),
        in_specs=[VM] * 5,
        out_specs=(VM,) * 3,
        compiler_params=params(24),
        cost_estimate=pl.CostEstimate(flops=3 * 10**9, bytes_accessed=12 * 2**20, transcendentals=0),
        name="prepare",
    )(latent_out, grid, aq, dw1, dw2)
    out = pl.pallas_call(
        decode_kernel,
        out_shape=shape((channels, points)),
        in_specs=[SM] * 2 + [VM] * 10,
        out_specs=VM,
        scratch_shapes=[
            pltpu.VMEM((nodes, 8, 128), F32),
            pltpu.VMEM((nodes, 8, 128), F32),
            pltpu.VMEM((3, CHUNK * 4, 256), BF),
            pltpu.VMEM((3, CHUNK * 4, 256), F32),
            pltpu.VMEM((points, 8, 128), F32),
        ],
        compiler_params=params(32),
        name="decode",
    )(ends, dec_idx, mesh_near, mesh_far, dk, dv, dq, grid, bo, co, dw1, dw2)
    return out.T


def solution(mesh):
    both = ("wide", "narrow")
    placed = (
        P(both, None),
        P(both, None),
        P(both, None),
        P(both),
        P(both, None),
        P(),
        P(),
        P(),
        P(),
        P(),
        P(),
    )
    return jax.shard_map(
        on_device,
        mesh=mesh,
        in_specs=placed,
        out_specs=P(both, None),
        check_vma=False,
    )
```

```python
import math

import jax
import jax.numpy as jnp
from jax import lax
from jax.experimental import pallas as pl
from jax.experimental.pallas import tpu as pltpu
from jax.sharding import PartitionSpec as P

WIN = 512
BG = 1024
BL = 128
HEADS = 16
SIZE = 64
PAIRS = HEADS // 2
CPAD = 128
LOG2E = math.log2(math.e)
NEG = -1e30
BF = jnp.bfloat16
F32 = jnp.float32

VM = pl.BlockSpec(memory_space=pltpu.VMEM)
SM = pl.BlockSpec(memory_space=pltpu.SMEM)
HBM = pl.BlockSpec(memory_space=pltpu.HBM)


def dot(a, b):
    return jnp.dot(a, b, preferred_element_type=F32)


def dot_t(a, b):
    return lax.dot_general(a, b, (((1,), (1,)), ((), ())), preferred_element_type=F32)


def low_half(shape):
    return lax.broadcasted_iota(jnp.int32, shape, len(shape) - 1) < SIZE


def sides(core, near, far):
    return jnp.where(core == 0, far, near), jnp.where(core == 0, near, far)


def params(mib):
    return pltpu.CompilerParams(vmem_limit_bytes=mib * 2**20)


def fetch(source, rows, buffers, sems):
    copies = [
        pltpu.make_async_copy(source.at[row], buf, sems.at[at])
        for row, buf, at in zip(rows, buffers, range(len(rows)))
    ]
    for copy in copies:
        copy.start()
    return copies


def fold_kernel(win, enc_w, lat, scale, *others):
    qt, av, w0, w1, w2, sems = others[-6:]
    got = fetch(enc_w, (1, 0, 2), (w1, w0, w2), sems)
    got[0].wait()
    ak = dot(win[...], w1[...]).astype(BF)
    got[1].wait()
    q = (dot(lat[...], w0[...]) * scale[0:1, :]).astype(BF)
    low = low_half((1, 128))
    for pair in range(PAIRS):
        at = slice(pair * 128, pair * 128 + 128)
        keys = ak[:, at]
        both = q[:, at]
        zero = jnp.zeros_like(both)
        qt[2 * pair] = dot_t(jnp.where(low, both, zero), keys).astype(BF)
        qt[2 * pair + 1] = dot_t(jnp.where(low, zero, both), keys).astype(BF)
    got[2].wait()
    av[...] = dot(win[...], w2[...]).astype(BF)


def encode_kernel(
    ends, idx, near, own, far, qt, bias, av, lat, enc_w, proc_w, dec_w,
    latent, normed, pw0, pw1, pw2, pw3, dw0, dw1, dw2, dw3,
    grid, ge0, ge1, z, w3, sems,
):
    got = fetch(enc_w, (3,), (w3,), sems.at[pl.ds(0, 1)])
    later = fetch(proc_w, (0, 1, 2, 3), (pw0, pw1, pw2, pw3), sems.at[pl.ds(1, 4)])
    later += fetch(dec_w, (0, 3, 1, 2), (dw0, dw3, dw1, dw2), sems.at[pl.ds(5, 4)])
    rows = lat.shape[0]
    groups = rows // 16
    at = 0
    left, right = sides(ends[2], near[...], far[...])
    for piece in (left, own[...], right):
        for begin in range(0, piece.shape[1], 512):
            grid[at : at + 512, :] = piece[:, begin : begin + 512].astype(F32).T
            at += 512
    row = lax.broadcasted_iota(jnp.int32, (256, 256), 0)
    col = lax.broadcasted_iota(jnp.int32, (256, 256), 1)
    diag = jnp.where(row % 16 == col % 16, 0.0, NEG)

    def collect(number, ge):
        base = number * 16
        for slot in range(16):
            for node in range(16):
                edge = slot * 16 + node
                ge[pl.ds(edge, 1), :] = grid[pl.ds(idx[base + (slot * rows + node)], 1), :]

    def attend(number, ge):
        points = ge[...].astype(BF)
        these = slice(number * 16, number * 16 + 16)
        queries = qt[:, these, :].reshape(256, CPAD)
        score = dot_t(queries, points) + (diag + bias[number : number + 1, :])
        expo = jnp.exp2(score - jnp.max(score, axis=1, keepdims=True)).astype(BF)
        mixed = dot(expo, jnp.concatenate([points, jnp.ones_like(points)], axis=1))
        mixed = mixed[:, :CPAD] * (1.0 / mixed[:, CPAD:])
        z[:, these, :] = mixed.reshape(16, 16, CPAD).astype(BF)

    buffers = (ge0, ge1)
    collect(0, ge0)
    for number in range(groups):
        attend(number, buffers[number % 2])
        if number + 1 < groups:
            collect(number + 1, buffers[(number + 1) % 2])
    low = low_half((1, 128))
    parts = []
    for pair in range(PAIRS):
        values = av[:, pair * 128 : pair * 128 + 128]
        zero = jnp.zeros_like(values)
        parts.append(
            dot(z[2 * pair], jnp.where(low, values, zero))
            + dot(z[2 * pair + 1], jnp.where(low, zero, values))
        )
    encoded = jnp.concatenate(parts, axis=1).astype(BF)
    got[0].wait()
    rounded = (lat[...].astype(F32) + dot(encoded, w3[...])).astype(BF)
    latent[...] = rounded
    wide = rounded.astype(F32)
    center = wide - jnp.mean(wide, axis=1, keepdims=True)
    spread = jnp.mean(center * center, axis=1, keepdims=True)
    normed[...] = (center * lax.rsqrt(spread + 1e-05)).astype(BF)
    for copy in later:
        copy.wait()


def project_kernel(normed, win, wout, scale, wq, wk, wv, dq, do, q, k, v, aq, bo, co):
    rows = normed[...]
    q[...] = (dot(rows, wq[...]) * scale[1:2, :]).astype(BF)
    k[...] = dot(rows, wk[...]).astype(BF)
    v[...] = dot(rows, wv[...]).astype(BF)
    co[...] = dot_t(wout[...], win[...]).astype(BF)
    aq[...] = (dot(win[...], dq[...]) * scale[2:3, :]).astype(BF)
    bo[...] = dot_t(do[...], wout[...]).astype(BF)


def window_kernel(
    ends, q, k, v, near, far, latent, wk, wv, wo, out, inner, outer, keys, values, bias, mixed
):
    rows = q.shape[0]
    half = rows // 2
    span = half + WIN
    keys[rows : 2 * rows, :] = k[...]
    values[rows : 2 * rows, :] = v[...]
    row = lax.broadcasted_iota(jnp.int32, (half, span), 0)
    col = lax.broadcasted_iota(jnp.int32, (half, span), 1)
    for side in range(2):
        place = col + side * half
        inside = (col >= row) & (col - row <= WIN) & (place >= ends[0]) & (place < ends[1])
        bias[side] = jnp.where(inside, 0.0, NEG)
    halo = jnp.concatenate(sides(ends[2], near[...], far[...]), axis=0)
    for weight, wide in ((wk, keys), (wv, values)):
        both = dot(halo, weight[...]).astype(BF)
        wide[:rows, :] = both[:rows]
        wide[2 * rows :, :] = both[rows:]
    low = low_half((1, 128))

    for pair in range(PAIRS):
        lanes = slice(pair * 128, pair * 128 + 128)
        bands = [slice(side * half, side * half + span) for side in range(2)]
        score = []
        for side in range(2):
            both = q[side * half : side * half + half, lanes]
            zero = jnp.zeros_like(both)
            stacked = jnp.concatenate(
                [jnp.where(low, both, zero), jnp.where(low, zero, both)], axis=0
            )
            part = dot_t(stacked, keys[bands[side], lanes])
            score.append(
                (part.reshape(2, half, span) + bias[side][None]).reshape(2 * half, span)
            )
        expo = [
            jnp.exp2(part - jnp.max(part, axis=1, keepdims=True)).astype(BF) for part in score
        ]
        for side in range(2):
            near_values = values[bands[side], lanes]
            total = dot(
                expo[side], jnp.concatenate([near_values, jnp.ones_like(near_values)], axis=1)
            )
            part = total[:, :128] * (1.0 / total[:, 128:])
            mixed[side * half : side * half + half, lanes] = jnp.where(
                low, part[:half], part[half:]
            ).astype(BF)
    out[...] = (latent[...].astype(F32) + dot(mixed[...], wo[...])).astype(BF)
    inner[...], outer[...] = sides(ends[2], out[:BL, :], out[rows - BL :, :])


CHUNK = 128


def to_tiles(rows, weight, tiles, begin):
    count = rows.shape[0]
    for two in range(4):
        wide = dot(rows, weight[:, two * 256 : two * 256 + 256])
        for block in (2 * two, 2 * two + 1):
            tiles[pl.ds(begin * 8 + block, count, stride=8), :] = wide[
                :, block % 2 * 128 : block % 2 * 128 + 128
            ]


def prepare_kernel(own, state, aq, wk, wv, q, k, v):
    to_tiles(own[...], wk, k, 0)
    to_tiles(own[...], wv, v, 0)
    points = state.shape[1]
    for first in range(0, points, 512):
        to_tiles(state[:, first : first + 512].astype(F32).T.astype(BF), aq, q, first)


def decode_kernel(
    ends, idx, near, far, ko, vo, q, grid, bo, co, wk, wv, out, kf, vf, prod, wts, dec
):
    points = grid.shape[1]
    side = near.shape[0]
    halo = jnp.concatenate(sides(ends[2], near[...], far[...]), axis=0)
    for weight, tiles, own in ((wk, kf, ko), (wv, vf, vo)):
        tiles[side * 8 : side * 8 + own.shape[0], :] = own[...]
        for two in range(4):
            wide = dot(halo, weight[:, two * 256 : two * 256 + 256])
            for block in (2 * two, 2 * two + 1):
                both = wide[:, block % 2 * 128 : block % 2 * 128 + 128]
                tiles[pl.ds(block, side, stride=8), :] = both[:side]
                tiles[pl.ds(side * 8 + own.shape[0] + block, side, stride=8), :] = both[side:]
    head_row = lax.broadcasted_iota(jnp.int32, (256, 256), 0) // SIZE
    head_col = lax.broadcasted_iota(jnp.int32, (256, 256), 1) // SIZE
    ones = jnp.where(head_row == head_col, 1.0, 0.0).astype(BF)
    sub = 128

    def one_chunk(number, carry):
        first = pl.multiple_of(number * CHUNK, CHUNK)

        def tile_of(tiles, edge, at):
            return tiles[pl.ds(pl.multiple_of(idx[edge * points + first + at], 8), 8), :]

        for quad in range(0, CHUNK, 4):
            mine = [
                q[pl.ds(pl.multiple_of((first + quad + at) * 8, 8), 8), :] for at in range(4)
            ]
            for edge in range(3):
                terms = [mine[at] * tile_of(kf, edge, quad + at) for at in range(4)]
                place = slice(quad * 4, quad * 4 + 16)
                prod[edge, place, 0:128] = jnp.concatenate([terms[0], terms[2]], axis=0).astype(BF)
                prod[edge, place, 128:256] = jnp.concatenate([terms[1], terms[3]], axis=0).astype(BF)
        for begin in range(0, CHUNK * 4, sub):
            score = dot(prod[:, begin : begin + sub, :].reshape(3 * sub, 256), ones)
            score = [score[edge * sub : edge * sub + sub] for edge in range(3)]
            highest = jnp.maximum(jnp.maximum(score[0], score[1]), score[2])
            expo = [jnp.exp2(part - highest) for part in score]
            inverse = 1.0 / (expo[0] + expo[1] + expo[2])
            for edge in range(3):
                wts[edge, begin : begin + sub, :] = expo[edge] * inverse
        for at in range(CHUNK):
            top = at // 4 * 16 + (at % 4) // 2 * 8
            lane = at % 2 * 128
            total = None
            for edge in range(3):
                term = wts[edge, top : top + 8, lane : lane + 128] * tile_of(vf, edge, at)
                total = term if total is None else total + term
            dec[pl.ds(pl.multiple_of((first + at) * 8, 8), 8), :] = total
        return carry

    lax.fori_loop(0, points // CHUNK, one_chunk, 0)
    block = 256
    for first in range(0, points, block):
        wide = jnp.concatenate(
            [dec[pl.ds(first * 8 + part, block, stride=8), :] for part in range(8)], axis=1
        ).astype(BF)
        result = dot(wide, bo[...]).T + dot(co[...], grid[:, first : first + block])
        out[:, first : first + block] = result[: out.shape[0], :].astype(BF)


def shape(dims, kind=BF):
    return jax.ShapeDtypeStruct(dims, kind)


def swap(inner, outer):
    axes = ("wide", "narrow")
    count = lax.axis_size(axes)
    pairs = []
    for i in range(1, count - 1, 2):
        pairs += [(i, i + 1), (i + 1, i)]
    far = lax.ppermute(outer, axes, pairs)
    near = lax.ppermute(inner, "narrow", [(0, 1), (1, 0)])
    return near, far


def on_device(
    grid_state,
    latent_init,
    enc_src,
    enc_count,
    dec_src,
    w_in,
    enc_w,
    proc_w,
    dec_w,
    w_out,
    logit_scale,
):
    points, channels = grid_state.shape
    rows, width = latent_init.shape
    slots = enc_src.shape[1]
    place = lax.axis_index(("wide", "narrow"))
    total = rows * lax.axis_size(("wide", "narrow"))
    weight = pltpu.VMEM((width, width), BF)
    dma = pltpu.SemaphoreType.DMA

    grid = jnp.concatenate(
        [
            grid_state.T,
            jnp.ones((1, points), BF),
            jnp.zeros((CPAD - channels - 1, points), BF),
        ],
        axis=0,
    )
    core = lax.axis_index("narrow")
    grid_near, grid_far = swap(
        lax.dynamic_slice_in_dim(grid, (1 - core) * (points - BG), BG, 1),
        lax.dynamic_slice_in_dim(grid, core * (points - BG), BG, 1),
    )
    win = jnp.pad(w_in, ((0, CPAD - channels), (0, 0)))
    wout = jnp.pad(w_out.T, ((0, CPAD - channels), (0, 0)))
    scale = jnp.repeat(logit_scale * (LOG2E / math.sqrt(SIZE)), SIZE, axis=1)
    enc_idx = jnp.clip(enc_src.T, 0, points + 2 * BG - 1).reshape(-1)
    live = jnp.arange(slots, dtype=jnp.int32)[:, None] < enc_count[None, :]
    bias = jnp.where(live, 0.0, NEG).astype(F32)
    bias = bias.reshape(slots, rows // 16, 16).transpose(1, 0, 2).reshape(rows // 16, slots * 16)
    dec_idx = jnp.clip(dec_src.T - (place * rows - BL), 0, rows + 2 * BL - 1).reshape(-1) * 8
    ends = jnp.stack([WIN // 2 - place * rows, total + WIN // 2 - place * rows, core])

    qt, av = pl.pallas_call(
        fold_kernel,
        out_shape=(shape((HEADS, rows, CPAD)), shape((CPAD, width))),
        in_specs=[VM, HBM, VM, VM] + [pl.BlockSpec(memory_space=pl.ANY)] * 5,
        out_specs=(VM, VM),
        scratch_shapes=[weight] * 3 + [dma((3,))],
        compiler_params=params(53),
        cost_estimate=pl.CostEstimate(flops=2 * 10**9, bytes_accessed=8 * 2**20, transcendentals=0),
        name="fold",
    )(win, enc_w, latent_init, scale, wout, enc_idx, bias, dec_idx, ends)
    square = shape((width, width))
    latent, normed, pw0, pw1, pw2, pw3, dw0, dw1, dw2, dw3 = pl.pallas_call(
        encode_kernel,
        out_shape=(shape((rows, width)),) * 2 + (square,) * 8,
        in_specs=[SM] * 2 + [VM] * 7 + [HBM] * 3,
        out_specs=(VM,) * 10,
        scratch_shapes=[
            pltpu.VMEM((points + 2 * BG, CPAD), F32),
            pltpu.VMEM((slots * 16, CPAD), F32),
            pltpu.VMEM((slots * 16, CPAD), F32),
            pltpu.VMEM((HEADS, rows, CPAD), BF),
            weight,
            dma((9,)),
        ],
        compiler_params=params(28),
        name="encode",
    )(ends, enc_idx, grid_near, grid, grid_far, qt, bias, av, latent_init, enc_w, proc_w, dec_w)
    normed_near, normed_far = swap(normed, normed)
    q, k, v, aq, bo, co = pl.pallas_call(
        project_kernel,
        out_shape=(shape((rows, width)),) * 3
        + (shape((CPAD, width)), shape((width, CPAD)), shape((CPAD, CPAD))),
        in_specs=[VM] * 9,
        out_specs=(VM,) * 6,
        compiler_params=params(24),
        cost_estimate=pl.CostEstimate(flops=3 * 10**9, bytes_accessed=12 * 2**20, transcendentals=0),
        name="project",
    )(normed, win, wout, scale, pw0, pw1, pw2, dw0, dw3)
    latent_out, mesh_inner, mesh_outer = pl.pallas_call(
        window_kernel,
        out_shape=(shape((rows, width)), shape((BL, width)), shape((BL, width))),
        in_specs=[SM] + [VM] * 9,
        out_specs=(VM,) * 3,
        scratch_shapes=[
            pltpu.VMEM((rows + WIN, width), BF),
            pltpu.VMEM((rows + WIN, width), BF),
            pltpu.VMEM((2, rows // 2, rows // 2 + WIN), F32),
            pltpu.VMEM((rows, width), BF),
        ],
        compiler_params=params(24),
        name="window",
    )(ends, q, k, v, normed_near, normed_far, latent, pw1, pw2, pw3)
    mesh_near, mesh_far = swap(mesh_inner, mesh_outer)
    nodes = rows + 2 * BL
    dq, dk, dv = pl.pallas_call(
        prepare_kernel,
        out_shape=(
            shape((points * 8, 128), F32),
            shape((rows * 8, 128), F32),
            shape((rows * 8, 128), F32),
        ),
        in_specs=[VM] * 5,
        out_specs=(VM,) * 3,
        compiler_params=params(24),
        cost_estimate=pl.CostEstimate(flops=3 * 10**9, bytes_accessed=12 * 2**20, transcendentals=0),
        name="prepare",
    )(latent_out, grid, aq, dw1, dw2)
    out = pl.pallas_call(
        decode_kernel,
        out_shape=shape((channels, points)),
        in_specs=[SM] * 2 + [VM] * 10,
        out_specs=VM,
        scratch_shapes=[
            pltpu.VMEM((nodes * 8, 128), F32),
            pltpu.VMEM((nodes * 8, 128), F32),
            pltpu.VMEM((3, CHUNK * 4, 256), BF),
            pltpu.VMEM((3, CHUNK * 4, 256), F32),
            pltpu.VMEM((points * 8, 128), F32),
        ],
        compiler_params=params(32),
        name="decode",
    )(ends, dec_idx, mesh_near, mesh_far, dk, dv, dq, grid, bo, co, dw1, dw2)
    return out.T


def solution(mesh):
    both = ("wide", "narrow")
    placed = (
        P(both, None),
        P(both, None),
        P(both, None),
        P(both),
        P(both, None),
        P(),
        P(),
        P(),
        P(),
        P(),
        P(),
    )
    return jax.shard_map(
        on_device,
        mesh=mesh,
        in_specs=placed,
        out_specs=P(both, None),
        check_vma=False,
    )
```

```python
import math

import jax
import jax.numpy as jnp
from jax import lax
from jax.experimental import pallas as pl
from jax.experimental.pallas import tpu as pltpu
from jax.sharding import PartitionSpec as P

WIN = 512
BG = 1024
BL = 128
HEADS = 16
SIZE = 64
PAIRS = HEADS // 2
CPAD = 128
LOG2E = math.log2(math.e)
NEG = -1e30
BF = jnp.bfloat16
F32 = jnp.float32

VM = pl.BlockSpec(memory_space=pltpu.VMEM)
SM = pl.BlockSpec(memory_space=pltpu.SMEM)
HBM = pl.BlockSpec(memory_space=pltpu.HBM)


def dot(a, b):
    return jnp.dot(a, b, preferred_element_type=F32)


def dot_t(a, b):
    return lax.dot_general(a, b, (((1,), (1,)), ((), ())), preferred_element_type=F32)


def low_half(shape):
    return lax.broadcasted_iota(jnp.int32, shape, len(shape) - 1) < SIZE


def sides(core, near, far):
    return jnp.where(core == 0, far, near), jnp.where(core == 0, near, far)


def params(mib):
    return pltpu.CompilerParams(vmem_limit_bytes=mib * 2**20)


def fetch(source, rows, buffers, sems):
    copies = [
        pltpu.make_async_copy(source.at[row], buf, sems.at[at])
        for row, buf, at in zip(rows, buffers, range(len(rows)))
    ]
    for copy in copies:
        copy.start()
    return copies


def fold_kernel(win, enc_w, lat, scale, *others):
    qt, av, w0, w1, w2, sems = others[-6:]
    got = fetch(enc_w, (1, 0, 2), (w1, w0, w2), sems)
    got[0].wait()
    ak = dot(win[...], w1[...]).astype(BF)
    got[1].wait()
    q = (dot(lat[...], w0[...]) * scale[0:1, :]).astype(BF)
    low = low_half((1, 128))
    for pair in range(PAIRS):
        at = slice(pair * 128, pair * 128 + 128)
        keys = ak[:, at]
        both = q[:, at]
        zero = jnp.zeros_like(both)
        qt[2 * pair] = dot_t(jnp.where(low, both, zero), keys).astype(BF)
        qt[2 * pair + 1] = dot_t(jnp.where(low, zero, both), keys).astype(BF)
    got[2].wait()
    av[...] = dot(win[...], w2[...]).astype(BF)


def encode_kernel(
    ends, idx, near, own, far, qt, bias, av, lat, enc_w, proc_w,
    latent, normed, pw0, pw1, pw2,
    grid, ge0, ge1, z, w3, sems,
):
    got = fetch(enc_w, (3,), (w3,), sems.at[pl.ds(0, 1)])
    later = fetch(proc_w, (0, 1, 2), (pw0, pw1, pw2), sems.at[pl.ds(1, 3)])
    rows = lat.shape[0]
    groups = rows // 16
    at = 0
    left, right = sides(ends[2], near[...], far[...])
    for piece in (left, own[...], right):
        for begin in range(0, piece.shape[1], 512):
            grid[at : at + 512, :] = piece[:, begin : begin + 512].astype(F32).T
            at += 512
    row = lax.broadcasted_iota(jnp.int32, (256, 256), 0)
    col = lax.broadcasted_iota(jnp.int32, (256, 256), 1)
    diag = jnp.where(row % 16 == col % 16, 0.0, NEG)

    def collect(number, ge):
        base = number * 16
        for slot in range(16):
            for node in range(16):
                edge = slot * 16 + node
                ge[pl.ds(edge, 1), :] = grid[pl.ds(idx[base + (slot * rows + node)], 1), :]

    def attend(number, ge):
        points = ge[...].astype(BF)
        these = slice(number * 16, number * 16 + 16)
        queries = qt[:, these, :].reshape(256, CPAD)
        score = dot_t(queries, points) + (diag + bias[number : number + 1, :])
        expo = jnp.exp2(score - jnp.max(score, axis=1, keepdims=True)).astype(BF)
        mixed = dot(expo, jnp.concatenate([points, jnp.ones_like(points)], axis=1))
        mixed = mixed[:, :CPAD] * (1.0 / mixed[:, CPAD:])
        z[:, these, :] = mixed.reshape(16, 16, CPAD).astype(BF)

    buffers = (ge0, ge1)
    collect(0, ge0)
    for number in range(groups):
        attend(number, buffers[number % 2])
        if number + 1 < groups:
            collect(number + 1, buffers[(number + 1) % 2])
    low = low_half((1, 128))
    parts = []
    for pair in range(PAIRS):
        values = av[:, pair * 128 : pair * 128 + 128]
        zero = jnp.zeros_like(values)
        parts.append(
            dot(z[2 * pair], jnp.where(low, values, zero))
            + dot(z[2 * pair + 1], jnp.where(low, zero, values))
        )
    encoded = jnp.concatenate(parts, axis=1).astype(BF)
    got[0].wait()
    rounded = (lat[...].astype(F32) + dot(encoded, w3[...])).astype(BF)
    latent[...] = rounded
    wide = rounded.astype(F32)
    center = wide - jnp.mean(wide, axis=1, keepdims=True)
    spread = jnp.mean(center * center, axis=1, keepdims=True)
    normed[...] = (center * lax.rsqrt(spread + 1e-05)).astype(BF)
    for copy in later:
        copy.wait()


def project_kernel(
    normed, win, wout, scale, wq, wk, wv, proc_w, dec_w,
    q, k, v, aq, bo, co, pw3, dw1, dw2, dw0, dw3, sems,
):
    got = fetch(dec_w, (0, 3), (dw0, dw3), sems.at[pl.ds(0, 2)])
    later = fetch(proc_w, (3,), (pw3,), sems.at[pl.ds(2, 1)])
    later += fetch(dec_w, (1, 2), (dw1, dw2), sems.at[pl.ds(3, 2)])
    rows = normed[...]
    q[...] = (dot(rows, wq[...]) * scale[1:2, :]).astype(BF)
    k[...] = dot(rows, wk[...]).astype(BF)
    v[...] = dot(rows, wv[...]).astype(BF)
    co[...] = dot_t(wout[...], win[...]).astype(BF)
    got[0].wait()
    aq[...] = (dot(win[...], dw0[...]) * scale[2:3, :]).astype(BF)
    got[1].wait()
    bo[...] = dot_t(dw3[...], wout[...]).astype(BF)
    for copy in later:
        copy.wait()


def window_half(side, ends, q, keys, values, latent, wo, bias, mixed, out):
    half, span = bias.shape
    row = lax.broadcasted_iota(jnp.int32, (half, span), 0)
    col = lax.broadcasted_iota(jnp.int32, (half, span), 1)
    begin = pl.multiple_of(side * half, half)
    place = col + begin
    inside = (col >= row) & (col - row <= WIN) & (place >= ends[0]) & (place < ends[1])
    bias[...] = jnp.where(inside, 0.0, NEG)
    these = pl.ds(begin, half)
    band = pl.ds(begin, span)
    low = low_half((1, 128))
    for first in range(0, PAIRS, 2):
        lanes = [slice(pair * 128, pair * 128 + 128) for pair in (first, first + 1)]
        score = []
        for at in lanes:
            both = q[these, at]
            zero = jnp.zeros_like(both)
            stacked = jnp.concatenate(
                [jnp.where(low, both, zero), jnp.where(low, zero, both)], axis=0
            )
            part = dot_t(stacked, keys[band, at])
            score.append(
                (part.reshape(2, half, span) + bias[...][None]).reshape(2 * half, span)
            )
        expo = [
            jnp.exp2(part - jnp.max(part, axis=1, keepdims=True)).astype(BF) for part in score
        ]
        for at, weights in zip(lanes, expo):
            near_values = values[band, at]
            total = dot(
                weights, jnp.concatenate([near_values, jnp.ones_like(near_values)], axis=1)
            )
            part = total[:, :128] * (1.0 / total[:, 128:])
            mixed[:, at] = jnp.where(low, part[:half], part[half:]).astype(BF)
    out[...] = (latent[these, :].astype(F32) + dot(mixed[...], wo[...])).astype(BF)


def window_outer_kernel(
    ends, q, k, v, near, far, latent, wk, wv, wo, outer, keys, values, bias, mixed
):
    rows = q.shape[0]
    keys[rows : 2 * rows, :] = k[...]
    values[rows : 2 * rows, :] = v[...]
    halo = jnp.concatenate(sides(ends[2], near[...], far[...]), axis=0)
    for weight, wide in ((wk, keys), (wv, values)):
        both = dot(halo, weight[...]).astype(BF)
        wide[:rows, :] = both[:rows]
        wide[2 * rows :, :] = both[rows:]
    window_half(ends[2], ends, q, keys, values, latent, wo, bias, mixed, outer)


def window_inner_kernel(ends, q, keys, values, latent, wo, inner, bias, mixed):
    window_half(1 - ends[2], ends, q, keys, values, latent, wo, bias, mixed, inner)


CHUNK = 128


def to_tiles(rows, weight, tiles, begin):
    count = rows.shape[0]
    for two in range(4):
        wide = dot(rows, weight[:, two * 256 : two * 256 + 256])
        for block in (2 * two, 2 * two + 1):
            tiles[pl.ds(begin * 8 + block, count, stride=8), :] = wide[
                :, block % 2 * 128 : block % 2 * 128 + 128
            ]


def prepare_kernel(ends, inner, outer, state, aq, wk, wv, q, k, v):
    own = jnp.concatenate(sides(ends[2], inner[...], outer[...]), axis=0)
    to_tiles(own, wk, k, 0)
    to_tiles(own, wv, v, 0)
    points = state.shape[1]
    for first in range(0, points, 512):
        to_tiles(state[:, first : first + 512].astype(F32).T.astype(BF), aq, q, first)


def decode_kernel(
    ends, idx, far, near, ko, vo, q, grid, bo, co, wk, wv, out, kf, vf, prod, wts, dec
):
    points = grid.shape[1]
    side = near.shape[0]
    halo = jnp.concatenate(sides(ends[2], near[...], far[...]), axis=0)
    for weight, tiles, own in ((wk, kf, ko), (wv, vf, vo)):
        tiles[side * 8 : side * 8 + own.shape[0], :] = own[...]
        for two in range(4):
            wide = dot(halo, weight[:, two * 256 : two * 256 + 256])
            for block in (2 * two, 2 * two + 1):
                both = wide[:, block % 2 * 128 : block % 2 * 128 + 128]
                tiles[pl.ds(block, side, stride=8), :] = both[:side]
                tiles[pl.ds(side * 8 + own.shape[0] + block, side, stride=8), :] = both[side:]
    head_row = lax.broadcasted_iota(jnp.int32, (256, 256), 0) // SIZE
    head_col = lax.broadcasted_iota(jnp.int32, (256, 256), 1) // SIZE
    ones = jnp.where(head_row == head_col, 1.0, 0.0).astype(BF)
    sub = 128

    def one_chunk(number, carry):
        first = pl.multiple_of(number * CHUNK, CHUNK)

        def tile_of(tiles, edge, at):
            return tiles[pl.ds(pl.multiple_of(idx[edge * points + first + at], 8), 8), :]

        for quad in range(0, CHUNK, 4):
            mine = [
                q[pl.ds(pl.multiple_of((first + quad + at) * 8, 8), 8), :] for at in range(4)
            ]
            for edge in range(3):
                terms = [mine[at] * tile_of(kf, edge, quad + at) for at in range(4)]
                place = slice(quad * 4, quad * 4 + 16)
                prod[edge, place, 0:128] = jnp.concatenate([terms[0], terms[2]], axis=0).astype(BF)
                prod[edge, place, 128:256] = jnp.concatenate([terms[1], terms[3]], axis=0).astype(BF)
        for begin in range(0, CHUNK * 4, sub):
            score = dot(prod[:, begin : begin + sub, :].reshape(3 * sub, 256), ones)
            score = [score[edge * sub : edge * sub + sub] for edge in range(3)]
            highest = jnp.maximum(jnp.maximum(score[0], score[1]), score[2])
            expo = [jnp.exp2(part - highest) for part in score]
            inverse = 1.0 / (expo[0] + expo[1] + expo[2])
            for edge in range(3):
                wts[edge, begin : begin + sub, :] = expo[edge] * inverse
        for at in range(CHUNK):
            top = at // 4 * 16 + (at % 4) // 2 * 8
            lane = at % 2 * 128
            total = None
            for edge in range(3):
                term = wts[edge, top : top + 8, lane : lane + 128] * tile_of(vf, edge, at)
                total = term if total is None else total + term
            dec[pl.ds(pl.multiple_of((first + at) * 8, 8), 8), :] = total
        return carry

    lax.fori_loop(0, points // CHUNK, one_chunk, 0)
    block = 256
    for first in range(0, points, block):
        wide = jnp.concatenate(
            [dec[pl.ds(first * 8 + part, block, stride=8), :] for part in range(8)], axis=1
        ).astype(BF)
        result = dot(wide, bo[...]).T + dot(co[...], grid[:, first : first + block])
        out[:, first : first + block] = result[: out.shape[0], :].astype(BF)


def pass_kernel(given, same):
    pass


def shape(dims, kind=BF):
    return jax.ShapeDtypeStruct(dims, kind)


def swap_near(inner):
    return lax.ppermute(inner, "narrow", [(0, 1), (1, 0)])


def swap_far(outer):
    axes = ("wide", "narrow")
    pairs = []
    for i in range(1, lax.axis_size(axes) - 1, 2):
        pairs += [(i, i + 1), (i + 1, i)]
    return lax.ppermute(outer, axes, pairs)


def on_device(
    grid_state,
    latent_init,
    enc_src,
    enc_count,
    dec_src,
    w_in,
    enc_w,
    proc_w,
    dec_w,
    w_out,
    logit_scale,
):
    points, channels = grid_state.shape
    rows, width = latent_init.shape
    slots = enc_src.shape[1]
    place = lax.axis_index(("wide", "narrow"))
    total = rows * lax.axis_size(("wide", "narrow"))
    weight = pltpu.VMEM((width, width), BF)
    dma = pltpu.SemaphoreType.DMA

    grid = jnp.concatenate(
        [
            grid_state.T,
            jnp.ones((1, points), BF),
            jnp.zeros((CPAD - channels - 1, points), BF),
        ],
        axis=0,
    )
    core = lax.axis_index("narrow")
    grid_far = swap_far(lax.dynamic_slice_in_dim(grid, core * (points - BG), BG, 1))
    grid_near = swap_near(lax.dynamic_slice_in_dim(grid, (1 - core) * (points - BG), BG, 1))
    win = jnp.pad(w_in, ((0, CPAD - channels), (0, 0)))
    wout = jnp.pad(w_out.T, ((0, CPAD - channels), (0, 0)))
    scale = jnp.repeat(logit_scale * (LOG2E / math.sqrt(SIZE)), SIZE, axis=1)
    enc_idx = jnp.clip(enc_src.T, 0, points + 2 * BG - 1).reshape(-1)
    live = jnp.arange(slots, dtype=jnp.int32)[:, None] < enc_count[None, :]
    bias = jnp.where(live, 0.0, NEG).astype(F32)
    bias = bias.reshape(slots, rows // 16, 16).transpose(1, 0, 2).reshape(rows // 16, slots * 16)
    dec_idx = jnp.clip(dec_src.T - (place * rows - BL), 0, rows + 2 * BL - 1).reshape(-1) * 8
    ends = jnp.stack([WIN // 2 - place * rows, total + WIN // 2 - place * rows, core])

    qt, av = pl.pallas_call(
        fold_kernel,
        out_shape=(shape((HEADS, rows, CPAD)), shape((CPAD, width))),
        in_specs=[VM, HBM, VM, VM] + [pl.BlockSpec(memory_space=pl.ANY)] * 5,
        out_specs=(VM, VM),
        scratch_shapes=[weight] * 3 + [dma((3,))],
        compiler_params=params(53),
        cost_estimate=pl.CostEstimate(flops=2 * 10**9, bytes_accessed=8 * 2**20, transcendentals=0),
        name="fold",
    )(win, enc_w, latent_init, scale, wout, enc_idx, bias, dec_idx, ends)
    square = shape((width, width))
    latent, normed, pw0, pw1, pw2 = pl.pallas_call(
        encode_kernel,
        out_shape=(shape((rows, width)),) * 2 + (square,) * 3,
        in_specs=[SM] * 2 + [VM] * 7 + [HBM] * 2,
        out_specs=(VM,) * 5,
        scratch_shapes=[
            pltpu.VMEM((points + 2 * BG, CPAD), F32),
            pltpu.VMEM((slots * 16, CPAD), F32),
            pltpu.VMEM((slots * 16, CPAD), F32),
            pltpu.VMEM((HEADS, rows, CPAD), BF),
            weight,
            dma((4,)),
        ],
        compiler_params=params(48),
        name="encode",
    )(ends, enc_idx, grid_near, grid, grid_far, qt, bias, av, latent_init, enc_w, proc_w)
    normed_far = swap_far(normed)
    normed_near = swap_near(normed)
    q, k, v, aq, bo, co, pw3, dw1, dw2 = pl.pallas_call(
        project_kernel,
        out_shape=(shape((rows, width)),) * 3
        + (shape((CPAD, width)), shape((width, CPAD)), shape((CPAD, CPAD)))
        + (square,) * 3,
        in_specs=[VM] * 7 + [HBM] * 2,
        out_specs=(VM,) * 9,
        scratch_shapes=[weight] * 2 + [dma((5,))],
        compiler_params=params(40),
        cost_estimate=pl.CostEstimate(flops=3 * 10**9, bytes_accessed=12 * 2**20, transcendentals=0),
        name="project",
    )(normed, win, wout, scale, pw0, pw1, pw2, proc_w, dec_w)
    half_scratch = [
        pltpu.VMEM((rows // 2, rows // 2 + WIN), F32),
        pltpu.VMEM((rows // 2, width), BF),
    ]
    wide = shape((rows + WIN, width))
    mesh_outer, keys, values = pl.pallas_call(
        window_outer_kernel,
        out_shape=(shape((BL, width)), wide, wide),
        in_specs=[SM] + [VM] * 9,
        out_specs=(VM,) * 3,
        scratch_shapes=half_scratch,
        compiler_params=params(24),
        name="window_outer",
    )(ends, q, k, v, normed_near, normed_far, latent, pw1, pw2, pw3)
    mesh_far = swap_far(mesh_outer)
    mesh_inner = pl.pallas_call(
        window_inner_kernel,
        out_shape=shape((BL, width)),
        in_specs=[SM] + [VM] * 5,
        out_specs=VM,
        scratch_shapes=half_scratch,
        compiler_params=params(24),
        cost_estimate=pl.CostEstimate(flops=3 * 10**9, bytes_accessed=12 * 2**20, transcendentals=0),
        name="window_inner",
    )(ends, q, keys, values, latent, pw3)
    mesh_near = swap_near(mesh_inner)
    mesh_far = pl.pallas_call(
        pass_kernel,
        out_shape=shape((BL, width)),
        in_specs=[pl.BlockSpec(memory_space=pl.ANY)],
        out_specs=pl.BlockSpec(memory_space=pl.ANY),
        input_output_aliases={0: 0},
        compiler_params=params(16),
        name="pass",
    )(mesh_far)
    nodes = rows + 2 * BL
    dq, dk, dv = pl.pallas_call(
        prepare_kernel,
        out_shape=(
            shape((points * 8, 128), F32),
            shape((rows * 8, 128), F32),
            shape((rows * 8, 128), F32),
        ),
        in_specs=[SM] + [VM] * 6,
        out_specs=(VM,) * 3,
        compiler_params=params(24),
        cost_estimate=pl.CostEstimate(flops=10**6, bytes_accessed=2**16, transcendentals=0),
        name="prepare",
    )(ends, mesh_inner, mesh_outer, grid, aq, dw1, dw2)
    out = pl.pallas_call(
        decode_kernel,
        out_shape=shape((channels, points)),
        in_specs=[SM] * 2 + [VM] * 10,
        out_specs=VM,
        scratch_shapes=[
            pltpu.VMEM((nodes * 8, 128), F32),
            pltpu.VMEM((nodes * 8, 128), F32),
            pltpu.VMEM((3, CHUNK * 4, 256), BF),
            pltpu.VMEM((3, CHUNK * 4, 256), F32),
            pltpu.VMEM((points * 8, 128), F32),
        ],
        compiler_params=params(32),
        name="decode",
    )(ends, dec_idx, mesh_far, mesh_near, dk, dv, dq, grid, bo, co, dw1, dw2)
    return out.T


def solution(mesh):
    both = ("wide", "narrow")
    placed = (
        P(both, None),
        P(both, None),
        P(both, None),
        P(both),
        P(both, None),
        P(),
        P(),
        P(),
        P(),
        P(),
        P(),
    )
    return jax.shard_map(
        on_device,
        mesh=mesh,
        in_specs=placed,
        out_specs=P(both, None),
        check_vma=False,
    )
```

```python
import math

import jax
import jax.numpy as jnp
from jax import lax
from jax.experimental import pallas as pl
from jax.experimental.pallas import tpu as pltpu
from jax.sharding import PartitionSpec as P

WIN = 512
BG = 1024
BL = 128
HEADS = 16
SIZE = 64
PAIRS = HEADS // 2
CPAD = 128
LOG2E = math.log2(math.e)
NEG = -1e30
BF = jnp.bfloat16
F32 = jnp.float32

VM = pl.BlockSpec(memory_space=pltpu.VMEM)
SM = pl.BlockSpec(memory_space=pltpu.SMEM)
HBM = pl.BlockSpec(memory_space=pltpu.HBM)


def dot(a, b):
    return jnp.dot(a, b, preferred_element_type=F32)


def dot_t(a, b):
    return lax.dot_general(a, b, (((1,), (1,)), ((), ())), preferred_element_type=F32)


def low_half(shape):
    return lax.broadcasted_iota(jnp.int32, shape, len(shape) - 1) < SIZE


def sides(core, near, far):
    return jnp.where(core == 0, far, near), jnp.where(core == 0, near, far)


def params(mib):
    return pltpu.CompilerParams(vmem_limit_bytes=mib * 2**20)


def fetch(source, rows, buffers, sems):
    copies = [
        pltpu.make_async_copy(source.at[row], buf, sems.at[at])
        for row, buf, at in zip(rows, buffers, range(len(rows)))
    ]
    for copy in copies:
        copy.start()
    return copies


def fold_kernel(win, enc_w, lat, scale, *others):
    qt, av, w0, w1, w2, sems = others[-6:]
    got = fetch(enc_w, (1, 0, 2), (w1, w0, w2), sems)
    got[0].wait()
    ak = dot(win[...], w1[...]).astype(BF)
    got[1].wait()
    q = (dot(lat[...], w0[...]) * scale[0:1, :]).astype(BF)
    low = low_half((1, 128))
    for pair in range(PAIRS):
        at = slice(pair * 128, pair * 128 + 128)
        keys = ak[:, at]
        both = q[:, at]
        zero = jnp.zeros_like(both)
        qt[2 * pair] = dot_t(jnp.where(low, both, zero), keys).astype(BF)
        qt[2 * pair + 1] = dot_t(jnp.where(low, zero, both), keys).astype(BF)
    got[2].wait()
    av[...] = dot(win[...], w2[...]).astype(BF)


def encode_kernel(
    ends, idx, near, own, far, qt, bias, av, lat, enc_w, proc_w,
    latent, normed, pw0, pw1, pw2,
    grid, ge0, ge1, z, w3, sems,
):
    got = fetch(enc_w, (3,), (w3,), sems.at[pl.ds(0, 1)])
    later = fetch(proc_w, (0, 1, 2), (pw0, pw1, pw2), sems.at[pl.ds(1, 3)])
    rows = lat.shape[0]
    groups = rows // 16
    at = 0
    left, right = sides(ends[2], near[...], far[...])
    for piece in (left, own[...], right):
        for begin in range(0, piece.shape[1], 512):
            grid[at : at + 512, :] = piece[:, begin : begin + 512].astype(F32).T
            at += 512
    row = lax.broadcasted_iota(jnp.int32, (256, 256), 0)
    col = lax.broadcasted_iota(jnp.int32, (256, 256), 1)
    diag = jnp.where(row % 16 == col % 16, 0.0, NEG)

    def collect(number, ge):
        base = number * 16
        for slot in range(16):
            for node in range(16):
                edge = slot * 16 + node
                ge[pl.ds(edge, 1), :] = grid[pl.ds(idx[base + (slot * rows + node)], 1), :]

    def attend(number, ge):
        points = ge[...].astype(BF)
        these = slice(number * 16, number * 16 + 16)
        queries = qt[:, these, :].reshape(256, CPAD)
        score = dot_t(queries, points) + (diag + bias[number : number + 1, :])
        expo = jnp.exp2(score - jnp.max(score, axis=1, keepdims=True)).astype(BF)
        mixed = dot(expo, jnp.concatenate([points, jnp.ones_like(points)], axis=1))
        mixed = mixed[:, :CPAD] * (1.0 / mixed[:, CPAD:])
        z[:, these, :] = mixed.reshape(16, 16, CPAD).astype(BF)

    buffers = (ge0, ge1)
    collect(0, ge0)
    for number in range(groups):
        attend(number, buffers[number % 2])
        if number + 1 < groups:
            collect(number + 1, buffers[(number + 1) % 2])
    low = low_half((1, 128))
    parts = []
    for pair in range(PAIRS):
        values = av[:, pair * 128 : pair * 128 + 128]
        zero = jnp.zeros_like(values)
        parts.append(
            dot(z[2 * pair], jnp.where(low, values, zero))
            + dot(z[2 * pair + 1], jnp.where(low, zero, values))
        )
    encoded = jnp.concatenate(parts, axis=1).astype(BF)
    got[0].wait()
    rounded = (lat[...].astype(F32) + dot(encoded, w3[...])).astype(BF)
    latent[...] = rounded
    wide = rounded.astype(F32)
    center = wide - jnp.mean(wide, axis=1, keepdims=True)
    spread = jnp.mean(center * center, axis=1, keepdims=True)
    normed[...] = (center * lax.rsqrt(spread + 1e-05)).astype(BF)
    for copy in later:
        copy.wait()


def project_kernel(
    normed, win, wout, scale, wq, wk, wv, proc_w, dec_w,
    q, k, v, aq, bo, co, pw3, dw1, dw2, dw0, dw3, sems,
):
    got = fetch(dec_w, (0, 3), (dw0, dw3), sems.at[pl.ds(0, 2)])
    later = fetch(proc_w, (3,), (pw3,), sems.at[pl.ds(2, 1)])
    later += fetch(dec_w, (1, 2), (dw1, dw2), sems.at[pl.ds(3, 2)])
    rows = normed[...]
    q[...] = (dot(rows, wq[...]) * scale[1:2, :]).astype(BF)
    k[...] = dot(rows, wk[...]).astype(BF)
    v[...] = dot(rows, wv[...]).astype(BF)
    co[...] = dot_t(wout[...], win[...]).astype(BF)
    got[0].wait()
    aq[...] = (dot(win[...], dw0[...]) * scale[2:3, :]).astype(BF)
    got[1].wait()
    bo[...] = dot_t(dw3[...], wout[...]).astype(BF)
    for copy in later:
        copy.wait()


def window_half(side, ends, q, keys, values, latent, wo, bias, mixed, out):
    half, span = bias.shape
    row = lax.broadcasted_iota(jnp.int32, (half, span), 0)
    col = lax.broadcasted_iota(jnp.int32, (half, span), 1)
    begin = pl.multiple_of(side * half, half)
    place = col + begin
    inside = (col >= row) & (col - row <= WIN) & (place >= ends[0]) & (place < ends[1])
    bias[...] = jnp.where(inside, 0.0, NEG)
    these = pl.ds(begin, half)
    band = pl.ds(begin, span)
    low = low_half((1, 128))
    for first in range(0, PAIRS, 2):
        lanes = [slice(pair * 128, pair * 128 + 128) for pair in (first, first + 1)]
        score = []
        for at in lanes:
            both = q[these, at]
            zero = jnp.zeros_like(both)
            stacked = jnp.concatenate(
                [jnp.where(low, both, zero), jnp.where(low, zero, both)], axis=0
            )
            part = dot_t(stacked, keys[band, at])
            score.append(
                (part.reshape(2, half, span) + bias[...][None]).reshape(2 * half, span)
            )
        expo = [
            jnp.exp2(part - jnp.max(part, axis=1, keepdims=True)).astype(BF) for part in score
        ]
        for at, weights in zip(lanes, expo):
            near_values = values[band, at]
            total = dot(
                weights, jnp.concatenate([near_values, jnp.ones_like(near_values)], axis=1)
            )
            part = total[:, :128] * (1.0 / total[:, 128:])
            mixed[:, at] = jnp.where(low, part[:half], part[half:]).astype(BF)
    out[...] = (latent[these, :].astype(F32) + dot(mixed[...], wo[...])).astype(BF)


def window_outer_kernel(
    ends, q, k, v, near, far, latent, wk, wv, wo, outer, keys, values, bias, mixed
):
    rows = q.shape[0]
    keys[rows : 2 * rows, :] = k[...]
    values[rows : 2 * rows, :] = v[...]
    halo = jnp.concatenate(sides(ends[2], near[...], far[...]), axis=0)
    for weight, wide in ((wk, keys), (wv, values)):
        both = dot(halo, weight[...]).astype(BF)
        wide[:rows, :] = both[:rows]
        wide[2 * rows :, :] = both[rows:]
    window_half(ends[2], ends, q, keys, values, latent, wo, bias, mixed, outer)


def window_inner_kernel(ends, q, keys, values, latent, wo, inner, bias, mixed):
    window_half(1 - ends[2], ends, q, keys, values, latent, wo, bias, mixed, inner)


CHUNK = 128


def to_tiles(rows, weight, tiles, begin):
    count = rows.shape[0]
    for two in range(4):
        wide = dot(rows, weight[:, two * 256 : two * 256 + 256])
        for block in (2 * two, 2 * two + 1):
            tiles[pl.ds(begin * 8 + block, count, stride=8), :] = wide[
                :, block % 2 * 128 : block % 2 * 128 + 128
            ]


def prepare_kernel(ends, inner, outer, state, aq, wk, wv, q, k, v):
    own = jnp.concatenate(sides(ends[2], inner[...], outer[...]), axis=0)
    to_tiles(own, wk, k, 0)
    to_tiles(own, wv, v, 0)
    points = state.shape[1]
    for first in range(0, points, 512):
        to_tiles(state[:, first : first + 512].astype(F32).T.astype(BF), aq, q, first)


def decode_kernel(
    ends, idx, far, near, ko, vo, q, grid, bo, co, wk, wv, out, kf, vf, prod, wts, dec
):
    points = grid.shape[1]
    side = near.shape[0]
    halo = jnp.concatenate(sides(ends[2], near[...], far[...]), axis=0)
    for weight, tiles, own in ((wk, kf, ko), (wv, vf, vo)):
        tiles[side * 8 : side * 8 + own.shape[0], :] = own[...]
        for two in range(4):
            wide = dot(halo, weight[:, two * 256 : two * 256 + 256])
            for block in (2 * two, 2 * two + 1):
                both = wide[:, block % 2 * 128 : block % 2 * 128 + 128]
                tiles[pl.ds(block, side, stride=8), :] = both[:side]
                tiles[pl.ds(side * 8 + own.shape[0] + block, side, stride=8), :] = both[side:]
    head_row = lax.broadcasted_iota(jnp.int32, (256, 256), 0) // SIZE
    head_col = lax.broadcasted_iota(jnp.int32, (256, 256), 1) // SIZE
    ones = jnp.where(head_row == head_col, 1.0, 0.0).astype(BF)
    sub = 128

    def one_chunk(number, carry):
        first = pl.multiple_of(number * CHUNK, CHUNK)

        def tile_of(tiles, edge, at):
            return tiles[pl.ds(pl.multiple_of(idx[edge * points + first + at], 8), 8), :]

        for quad in range(0, CHUNK, 4):
            mine = [
                q[pl.ds(pl.multiple_of((first + quad + at) * 8, 8), 8), :] for at in range(4)
            ]
            for edge in range(3):
                terms = [mine[at] * tile_of(kf, edge, quad + at) for at in range(4)]
                place = slice(quad * 4, quad * 4 + 16)
                prod[edge, place, 0:128] = jnp.concatenate([terms[0], terms[2]], axis=0).astype(BF)
                prod[edge, place, 128:256] = jnp.concatenate([terms[1], terms[3]], axis=0).astype(BF)
        for begin in range(0, CHUNK * 4, sub):
            score = dot(prod[:, begin : begin + sub, :].reshape(3 * sub, 256), ones)
            score = [score[edge * sub : edge * sub + sub] for edge in range(3)]
            highest = jnp.maximum(jnp.maximum(score[0], score[1]), score[2])
            expo = [jnp.exp2(part - highest) for part in score]
            inverse = 1.0 / (expo[0] + expo[1] + expo[2])
            for edge in range(3):
                wts[edge, begin : begin + sub, :] = expo[edge] * inverse
        for at in range(CHUNK):
            top = at // 4 * 16 + (at % 4) // 2 * 8
            lane = at % 2 * 128
            total = None
            for edge in range(3):
                term = wts[edge, top : top + 8, lane : lane + 128] * tile_of(vf, edge, at)
                total = term if total is None else total + term
            dec[pl.ds(pl.multiple_of((first + at) * 8, 8), 8), :] = total
        return carry

    lax.fori_loop(0, points // CHUNK, one_chunk, 0)
    block = 256
    for first in range(0, points, block):
        wide = jnp.concatenate(
            [dec[pl.ds(first * 8 + part, block, stride=8), :] for part in range(8)], axis=1
        ).astype(BF)
        result = dot(wide, bo[...]).T + dot(co[...], grid[:, first : first + block])
        out[:, first : first + block] = result[: out.shape[0], :].astype(BF)


def pass_kernel(given, same):
    pass


def shape(dims, kind=BF):
    return jax.ShapeDtypeStruct(dims, kind)


def swap_near(inner):
    return lax.ppermute(inner, "narrow", [(0, 1), (1, 0)])


def swap_far(outer):
    axes = ("wide", "narrow")
    pairs = []
    for i in range(1, lax.axis_size(axes) - 1, 2):
        pairs += [(i, i + 1), (i + 1, i)]
    return lax.ppermute(outer, axes, pairs)


def on_device(
    grid_state,
    latent_init,
    enc_src,
    enc_count,
    dec_src,
    w_in,
    enc_w,
    proc_w,
    dec_w,
    w_out,
    logit_scale,
):
    points, channels = grid_state.shape
    rows, width = latent_init.shape
    slots = enc_src.shape[1]
    place = lax.axis_index(("wide", "narrow"))
    total = rows * lax.axis_size(("wide", "narrow"))
    weight = pltpu.VMEM((width, width), BF)
    dma = pltpu.SemaphoreType.DMA

    grid = jnp.concatenate(
        [
            grid_state.T,
            jnp.ones((1, points), BF),
            jnp.zeros((CPAD - channels - 1, points), BF),
        ],
        axis=0,
    )
    core = lax.axis_index("narrow")
    grid_far = swap_far(lax.dynamic_slice_in_dim(grid, core * (points - BG), BG, 1))
    grid_near = swap_near(lax.dynamic_slice_in_dim(grid, (1 - core) * (points - BG), BG, 1))
    win = jnp.pad(w_in, ((0, CPAD - channels), (0, 0)))
    wout = jnp.pad(w_out.T, ((0, CPAD - channels), (0, 0)))
    scale = jnp.repeat(logit_scale * (LOG2E / math.sqrt(SIZE)), SIZE, axis=1)
    enc_idx = jnp.clip(enc_src.T, 0, points + 2 * BG - 1).reshape(-1)
    live = jnp.arange(slots, dtype=jnp.int32)[:, None] < enc_count[None, :]
    bias = jnp.where(live, 0.0, NEG).astype(F32)
    bias = bias.reshape(slots, rows // 16, 16).transpose(1, 0, 2).reshape(rows // 16, slots * 16)
    dec_idx = jnp.clip(dec_src.T - (place * rows - BL), 0, rows + 2 * BL - 1).reshape(-1) * 8
    ends = jnp.stack([WIN // 2 - place * rows, total + WIN // 2 - place * rows, core])

    qt, av = pl.pallas_call(
        fold_kernel,
        out_shape=(shape((HEADS, rows, CPAD)), shape((CPAD, width))),
        in_specs=[VM, HBM, VM, VM] + [pl.BlockSpec(memory_space=pl.ANY)] * 5,
        out_specs=(VM, VM),
        scratch_shapes=[weight] * 3 + [dma((3,))],
        compiler_params=params(50),
        cost_estimate=pl.CostEstimate(flops=2 * 10**9, bytes_accessed=8 * 2**20, transcendentals=0),
        name="fold",
    )(win, enc_w, latent_init, scale, wout, enc_idx, bias, dec_idx, ends)
    square = shape((width, width))
    latent, normed, pw0, pw1, pw2 = pl.pallas_call(
        encode_kernel,
        out_shape=(shape((rows, width)),) * 2 + (square,) * 3,
        in_specs=[SM] * 2 + [VM] * 7 + [HBM] * 2,
        out_specs=(VM,) * 5,
        scratch_shapes=[
            pltpu.VMEM((points + 2 * BG, CPAD), F32),
            pltpu.VMEM((slots * 16, CPAD), F32),
            pltpu.VMEM((slots * 16, CPAD), F32),
            pltpu.VMEM((HEADS, rows, CPAD), BF),
            weight,
            dma((4,)),
        ],
        compiler_params=params(44),
        name="encode",
    )(ends, enc_idx, grid_near, grid, grid_far, qt, bias, av, latent_init, enc_w, proc_w)
    normed_far = swap_far(normed)
    normed_near = swap_near(normed)
    q, k, v, aq, bo, co, pw3, dw1, dw2 = pl.pallas_call(
        project_kernel,
        out_shape=(shape((rows, width)),) * 3
        + (shape((CPAD, width)), shape((width, CPAD)), shape((CPAD, CPAD)))
        + (square,) * 3,
        in_specs=[VM] * 7 + [HBM] * 2,
        out_specs=(VM,) * 9,
        scratch_shapes=[weight] * 2 + [dma((5,))],
        compiler_params=params(36),
        cost_estimate=pl.CostEstimate(flops=3 * 10**9, bytes_accessed=12 * 2**20, transcendentals=0),
        name="project",
    )(normed, win, wout, scale, pw0, pw1, pw2, proc_w, dec_w)
    half_scratch = [
        pltpu.VMEM((rows // 2, rows // 2 + WIN), F32),
        pltpu.VMEM((rows // 2, width), BF),
    ]
    wide = shape((rows + WIN, width))
    mesh_outer, keys, values = pl.pallas_call(
        window_outer_kernel,
        out_shape=(shape((BL, width)), wide, wide),
        in_specs=[SM] + [VM] * 9,
        out_specs=(VM,) * 3,
        scratch_shapes=half_scratch,
        compiler_params=params(24),
        name="window_outer",
    )(ends, q, k, v, normed_near, normed_far, latent, pw1, pw2, pw3)
    mesh_far = swap_far(mesh_outer)
    mesh_inner = pl.pallas_call(
        window_inner_kernel,
        out_shape=shape((BL, width)),
        in_specs=[SM] + [VM] * 5,
        out_specs=VM,
        scratch_shapes=half_scratch,
        compiler_params=params(24),
        cost_estimate=pl.CostEstimate(flops=3 * 10**9, bytes_accessed=12 * 2**20, transcendentals=0),
        name="window_inner",
    )(ends, q, keys, values, latent, pw3)
    mesh_near = swap_near(mesh_inner)
    mesh_far = pl.pallas_call(
        pass_kernel,
        out_shape=shape((BL, width)),
        in_specs=[pl.BlockSpec(memory_space=pl.ANY)],
        out_specs=pl.BlockSpec(memory_space=pl.ANY),
        input_output_aliases={0: 0},
        compiler_params=params(16),
        name="pass",
    )(mesh_far)
    nodes = rows + 2 * BL
    dq, dk, dv = pl.pallas_call(
        prepare_kernel,
        out_shape=(
            shape((points * 8, 128), F32),
            shape((rows * 8, 128), F32),
            shape((rows * 8, 128), F32),
        ),
        in_specs=[SM] + [VM] * 6,
        out_specs=(VM,) * 3,
        compiler_params=params(24),
        cost_estimate=pl.CostEstimate(flops=10**6, bytes_accessed=2**16, transcendentals=0),
        name="prepare",
    )(ends, mesh_inner, mesh_outer, grid, aq, dw1, dw2)
    out = pl.pallas_call(
        decode_kernel,
        out_shape=shape((channels, points)),
        in_specs=[SM] * 2 + [VM] * 10,
        out_specs=VM,
        scratch_shapes=[
            pltpu.VMEM((nodes * 8, 128), F32),
            pltpu.VMEM((nodes * 8, 128), F32),
            pltpu.VMEM((3, CHUNK * 4, 256), BF),
            pltpu.VMEM((3, CHUNK * 4, 256), F32),
            pltpu.VMEM((points * 8, 128), F32),
        ],
        compiler_params=params(32),
        name="decode",
    )(ends, dec_idx, mesh_far, mesh_near, dk, dv, dq, grid, bo, co, dw1, dw2)
    return out.T


def solution(mesh):
    both = ("wide", "narrow")
    placed = (
        P(both, None),
        P(both, None),
        P(both, None),
        P(both),
        P(both, None),
        P(),
        P(),
        P(),
        P(),
        P(),
        P(),
    )
    return jax.shard_map(
        on_device,
        mesh=mesh,
        in_specs=placed,
        out_specs=P(both, None),
        check_vma=False,
    )
```

```python
import math

import jax
import jax.numpy as jnp
from jax import lax
from jax.experimental import pallas as pl
from jax.experimental.pallas import tpu as pltpu
from jax.sharding import PartitionSpec as P

WIN = 512
BG = 1024
BL = 128
HEADS = 16
SIZE = 64
PAIRS = HEADS // 2
CPAD = 128
LOG2E = math.log2(math.e)
NEG = -1e30
BF = jnp.bfloat16
F32 = jnp.float32

VM = pl.BlockSpec(memory_space=pltpu.VMEM)
SM = pl.BlockSpec(memory_space=pltpu.SMEM)
HBM = pl.BlockSpec(memory_space=pltpu.HBM)


def dot(a, b):
    return jnp.dot(a, b, preferred_element_type=F32)


def dot_t(a, b):
    return lax.dot_general(a, b, (((1,), (1,)), ((), ())), preferred_element_type=F32)


def low_half(shape):
    return lax.broadcasted_iota(jnp.int32, shape, len(shape) - 1) < SIZE


def sides(core, near, far):
    return jnp.where(core == 0, far, near), jnp.where(core == 0, near, far)


def params(mib):
    return pltpu.CompilerParams(vmem_limit_bytes=mib * 2**20)


def fetch(source, rows, buffers, sems):
    copies = [
        pltpu.make_async_copy(source.at[row], buf, sems.at[at])
        for row, buf, at in zip(rows, buffers, range(len(rows)))
    ]
    for copy in copies:
        copy.start()
    return copies


def fold_kernel(win, enc_w, lat, scale, *others):
    qt, av, w0, w1, w2, sems = others[-6:]
    got = fetch(enc_w, (1, 0, 2), (w1, w0, w2), sems)
    got[0].wait()
    ak = dot(win[...], w1[...]).astype(BF)
    got[1].wait()
    q = (dot(lat[...], w0[...]) * scale[0:1, :]).astype(BF)
    low = low_half((1, 128))
    for pair in range(PAIRS):
        at = slice(pair * 128, pair * 128 + 128)
        keys = ak[:, at]
        both = q[:, at]
        zero = jnp.zeros_like(both)
        qt[2 * pair] = dot_t(jnp.where(low, both, zero), keys).astype(BF)
        qt[2 * pair + 1] = dot_t(jnp.where(low, zero, both), keys).astype(BF)
    got[2].wait()
    av[...] = dot(win[...], w2[...]).astype(BF)


def encode_kernel(
    ends, idx, near, own, far, qt, bias, av, lat, enc_w, proc_w,
    latent, normed, pw0, pw1, pw2,
    grid, ge0, ge1, z, w3, sems,
):
    got = fetch(enc_w, (3,), (w3,), sems.at[pl.ds(0, 1)])
    later = fetch(proc_w, (0, 1, 2), (pw0, pw1, pw2), sems.at[pl.ds(1, 3)])
    rows = lat.shape[0]
    groups = rows // 16
    at = 0
    left, right = sides(ends[2], near[...], far[...])
    for piece in (left, own[...], right):
        for begin in range(0, piece.shape[1], 512):
            grid[at : at + 512, :] = piece[:, begin : begin + 512].astype(F32).T
            at += 512
    row = lax.broadcasted_iota(jnp.int32, (256, 256), 0)
    col = lax.broadcasted_iota(jnp.int32, (256, 256), 1)
    diag = jnp.where(row % 16 == col % 16, 0.0, NEG)

    def collect(number, ge):
        base = number * 16
        for slot in range(16):
            for node in range(16):
                edge = slot * 16 + node
                ge[pl.ds(edge, 1), :] = grid[pl.ds(idx[base + (slot * rows + node)], 1), :]

    def attend(number, ge):
        points = ge[...].astype(BF)
        these = slice(number * 16, number * 16 + 16)
        queries = qt[:, these, :].reshape(256, CPAD)
        score = dot_t(queries, points) + (diag + bias[number : number + 1, :])
        expo = jnp.exp2(score - jnp.max(score, axis=1, keepdims=True)).astype(BF)
        mixed = dot(expo, jnp.concatenate([points, jnp.ones_like(points)], axis=1))
        mixed = mixed[:, :CPAD] * (1.0 / mixed[:, CPAD:])
        z[:, these, :] = mixed.reshape(16, 16, CPAD).astype(BF)

    buffers = (ge0, ge1)
    collect(0, ge0)
    for number in range(groups):
        attend(number, buffers[number % 2])
        if number + 1 < groups:
            collect(number + 1, buffers[(number + 1) % 2])
    low = low_half((1, 128))
    parts = []
    for pair in range(PAIRS):
        values = av[:, pair * 128 : pair * 128 + 128]
        zero = jnp.zeros_like(values)
        parts.append(
            dot(z[2 * pair], jnp.where(low, values, zero))
            + dot(z[2 * pair + 1], jnp.where(low, zero, values))
        )
    encoded = jnp.concatenate(parts, axis=1).astype(BF)
    got[0].wait()
    rounded = (lat[...].astype(F32) + dot(encoded, w3[...])).astype(BF)
    latent[...] = rounded
    wide = rounded.astype(F32)
    center = wide - jnp.mean(wide, axis=1, keepdims=True)
    spread = jnp.mean(center * center, axis=1, keepdims=True)
    normed[...] = (center * lax.rsqrt(spread + 1e-05)).astype(BF)
    for copy in later:
        copy.wait()


def attend_pair(both, keys, values, bias):
    low = low_half((1, 128))
    zero = jnp.zeros_like(both)
    rows = both.shape[0]
    stacked = jnp.concatenate([jnp.where(low, both, zero), jnp.where(low, zero, both)], axis=0)
    score = dot_t(stacked, keys)
    if bias is not None:
        score = (score.reshape(2, rows, -1) + bias[None]).reshape(2 * rows, -1)
    highest = jnp.max(score, axis=1, keepdims=True)
    expo = jnp.exp2(score - highest).astype(BF)
    total = dot(expo, jnp.concatenate([values, jnp.ones_like(values)], axis=1))
    highest = jnp.broadcast_to(highest, (2 * rows, 128))
    return (
        jnp.where(low, total[:rows, :128], total[rows:, :128]),
        jnp.where(low, total[:rows, 128:], total[rows:, 128:]),
        jnp.where(low, highest[:rows], highest[rows:]),
    )


def project_kernel(
    normed, win, wout, scale, wq, wk, wv, proc_w, dec_w,
    q, num, den, top, aq, bo, co, pw3, dw1, dw2, k, v, dw0, dw3, sems,
):
    got = fetch(dec_w, (0, 3), (dw0, dw3), sems.at[pl.ds(0, 2)])
    later = fetch(proc_w, (3,), (pw3,), sems.at[pl.ds(2, 1)])
    later += fetch(dec_w, (1, 2), (dw1, dw2), sems.at[pl.ds(3, 2)])
    rows = normed[...]
    q[...] = (dot(rows, wq[...]) * scale[1:2, :]).astype(BF)
    k[...] = dot(rows, wk[...]).astype(BF)
    v[...] = dot(rows, wv[...]).astype(BF)
    for pair in range(PAIRS):
        at = slice(pair * 128, pair * 128 + 128)
        num[:, at], den[:, at], top[:, at] = attend_pair(q[:, at], k[:, at], v[:, at], None)
    co[...] = dot_t(wout[...], win[...]).astype(BF)
    got[0].wait()
    aq[...] = (dot(win[...], dw0[...]) * scale[2:3, :]).astype(BF)
    got[1].wait()
    bo[...] = dot_t(dw3[...], wout[...]).astype(BF)
    for copy in later:
        copy.wait()


def window_half(side, ends, q, keys, values, num, den, top, latent, wo, bias, mixed, out):
    half, span = bias.shape
    row = lax.broadcasted_iota(jnp.int32, (half, span), 0)
    col = lax.broadcasted_iota(jnp.int32, (half, span), 1)
    begin = pl.multiple_of(side * half, half)
    place = col + begin
    place = jnp.where(place < WIN // 2, place, place + 2 * half)
    far = place - begin - row
    inside = (far >= 0) & (far <= WIN) & (place >= ends[0]) & (place < ends[1])
    bias[...] = jnp.where(inside, 0.0, NEG)
    these = pl.ds(begin, half)
    band = pl.ds(begin, span)
    for pair in range(PAIRS):
        at = slice(pair * 128, pair * 128 + 128)
        more, weight, highest = attend_pair(
            q[these, at], keys[band, at], values[band, at], bias[...]
        )
        own = top[these, at]
        joint = jnp.maximum(own, highest)
        own = jnp.exp2(own - joint)
        other = jnp.exp2(highest - joint)
        mixed[:, at] = (
            (num[these, at] * own + more * other) / (den[these, at] * own + weight * other)
        ).astype(BF)
    out[...] = (latent[these, :].astype(F32) + dot(mixed[...], wo[...])).astype(BF)


def window_outer_kernel(
    ends, q, num, den, top, near, far, latent, wk, wv, wo, outer, keys, values, bias, mixed
):
    halo = jnp.concatenate(sides(ends[2], near[...], far[...]), axis=0)
    keys[...] = dot(halo, wk[...]).astype(BF)
    values[...] = dot(halo, wv[...]).astype(BF)
    window_half(
        ends[2], ends, q, keys, values, num, den, top, latent, wo, bias, mixed, outer
    )


def window_inner_kernel(
    ends, q, num, den, top, keys, values, latent, wo, inner, bias, mixed
):
    window_half(
        1 - ends[2], ends, q, keys, values, num, den, top, latent, wo, bias, mixed, inner
    )


CHUNK = 128


def to_tiles(rows, weight, tiles, begin):
    count = rows.shape[0]
    for two in range(4):
        wide = dot(rows, weight[:, two * 256 : two * 256 + 256])
        for block in (2 * two, 2 * two + 1):
            tiles[pl.ds(begin * 8 + block, count, stride=8), :] = wide[
                :, block % 2 * 128 : block % 2 * 128 + 128
            ]


def prepare_kernel(ends, inner, outer, state, aq, wk, wv, q, k, v):
    own = jnp.concatenate(sides(ends[2], inner[...], outer[...]), axis=0)
    to_tiles(own, wk, k, 0)
    to_tiles(own, wv, v, 0)
    points = state.shape[1]
    for first in range(0, points, 512):
        to_tiles(state[:, first : first + 512].astype(F32).T.astype(BF), aq, q, first)


def decode_kernel(
    ends, idx, far, near, ko, vo, q, grid, bo, co, wk, wv, out, kf, vf, prod, wts, dec
):
    points = grid.shape[1]
    side = near.shape[0]
    halo = jnp.concatenate(sides(ends[2], near[...], far[...]), axis=0)
    for weight, tiles, own in ((wk, kf, ko), (wv, vf, vo)):
        tiles[side * 8 : side * 8 + own.shape[0], :] = own[...]
        for two in range(4):
            wide = dot(halo, weight[:, two * 256 : two * 256 + 256])
            for block in (2 * two, 2 * two + 1):
                both = wide[:, block % 2 * 128 : block % 2 * 128 + 128]
                tiles[pl.ds(block, side, stride=8), :] = both[:side]
                tiles[pl.ds(side * 8 + own.shape[0] + block, side, stride=8), :] = both[side:]
    head_row = lax.broadcasted_iota(jnp.int32, (256, 256), 0) // SIZE
    head_col = lax.broadcasted_iota(jnp.int32, (256, 256), 1) // SIZE
    ones = jnp.where(head_row == head_col, 1.0, 0.0).astype(BF)
    sub = 128

    def one_chunk(number, carry):
        first = pl.multiple_of(number * CHUNK, CHUNK)

        def tile_of(tiles, edge, at):
            return tiles[pl.ds(pl.multiple_of(idx[edge * points + first + at], 8), 8), :]

        for quad in range(0, CHUNK, 4):
            mine = [
                q[pl.ds(pl.multiple_of((first + quad + at) * 8, 8), 8), :] for at in range(4)
            ]
            for edge in range(3):
                terms = [mine[at] * tile_of(kf, edge, quad + at) for at in range(4)]
                place = slice(quad * 4, quad * 4 + 16)
                prod[edge, place, 0:128] = jnp.concatenate([terms[0], terms[2]], axis=0).astype(BF)
                prod[edge, place, 128:256] = jnp.concatenate([terms[1], terms[3]], axis=0).astype(BF)
        for begin in range(0, CHUNK * 4, sub):
            score = dot(prod[:, begin : begin + sub, :].reshape(3 * sub, 256), ones)
            score = [score[edge * sub : edge * sub + sub] for edge in range(3)]
            highest = jnp.maximum(jnp.maximum(score[0], score[1]), score[2])
            expo = [jnp.exp2(part - highest) for part in score]
            inverse = 1.0 / (expo[0] + expo[1] + expo[2])
            for edge in range(3):
                wts[edge, begin : begin + sub, :] = expo[edge] * inverse
        for at in range(CHUNK):
            top = at // 4 * 16 + (at % 4) // 2 * 8
            lane = at % 2 * 128
            total = None
            for edge in range(3):
                term = wts[edge, top : top + 8, lane : lane + 128] * tile_of(vf, edge, at)
                total = term if total is None else total + term
            dec[pl.ds(pl.multiple_of((first + at) * 8, 8), 8), :] = total
        return carry

    lax.fori_loop(0, points // CHUNK, one_chunk, 0)
    block = 256
    for first in range(0, points, block):
        wide = jnp.concatenate(
            [dec[pl.ds(first * 8 + part, block, stride=8), :] for part in range(8)], axis=1
        ).astype(BF)
        result = dot(wide, bo[...]).T + dot(co[...], grid[:, first : first + block])
        out[:, first : first + block] = result[: out.shape[0], :].astype(BF)


def pass_kernel(given, same):
    pass


def shape(dims, kind=BF):
    return jax.ShapeDtypeStruct(dims, kind)


def swap_near(inner):
    return lax.ppermute(inner, "narrow", [(0, 1), (1, 0)])


def swap_far(outer):
    axes = ("wide", "narrow")
    pairs = []
    for i in range(1, lax.axis_size(axes) - 1, 2):
        pairs += [(i, i + 1), (i + 1, i)]
    return lax.ppermute(outer, axes, pairs)


def on_device(
    grid_state,
    latent_init,
    enc_src,
    enc_count,
    dec_src,
    w_in,
    enc_w,
    proc_w,
    dec_w,
    w_out,
    logit_scale,
):
    points, channels = grid_state.shape
    rows, width = latent_init.shape
    slots = enc_src.shape[1]
    place = lax.axis_index(("wide", "narrow"))
    total = rows * lax.axis_size(("wide", "narrow"))
    weight = pltpu.VMEM((width, width), BF)
    dma = pltpu.SemaphoreType.DMA

    grid = jnp.concatenate(
        [
            grid_state.T,
            jnp.ones((1, points), BF),
            jnp.zeros((CPAD - channels - 1, points), BF),
        ],
        axis=0,
    )
    core = lax.axis_index("narrow")
    grid_far = swap_far(lax.dynamic_slice_in_dim(grid, core * (points - BG), BG, 1))
    grid_near = swap_near(lax.dynamic_slice_in_dim(grid, (1 - core) * (points - BG), BG, 1))
    win = jnp.pad(w_in, ((0, CPAD - channels), (0, 0)))
    wout = jnp.pad(w_out.T, ((0, CPAD - channels), (0, 0)))
    scale = jnp.repeat(logit_scale * (LOG2E / math.sqrt(SIZE)), SIZE, axis=1)
    enc_idx = jnp.clip(enc_src.T, 0, points + 2 * BG - 1).reshape(-1)
    live = jnp.arange(slots, dtype=jnp.int32)[:, None] < enc_count[None, :]
    bias = jnp.where(live, 0.0, NEG).astype(F32)
    bias = bias.reshape(slots, rows // 16, 16).transpose(1, 0, 2).reshape(rows // 16, slots * 16)
    dec_idx = jnp.clip(dec_src.T - (place * rows - BL), 0, rows + 2 * BL - 1).reshape(-1) * 8
    ends = jnp.stack([WIN // 2 - place * rows, total + WIN // 2 - place * rows, core])

    qt, av = pl.pallas_call(
        fold_kernel,
        out_shape=(shape((HEADS, rows, CPAD)), shape((CPAD, width))),
        in_specs=[VM, HBM, VM, VM] + [pl.BlockSpec(memory_space=pl.ANY)] * 5,
        out_specs=(VM, VM),
        scratch_shapes=[weight] * 3 + [dma((3,))],
        compiler_params=params(50),
        cost_estimate=pl.CostEstimate(flops=2 * 10**9, bytes_accessed=8 * 2**20, transcendentals=0),
        name="fold",
    )(win, enc_w, latent_init, scale, wout, enc_idx, bias, dec_idx, ends)
    square = shape((width, width))
    latent, normed, pw0, pw1, pw2 = pl.pallas_call(
        encode_kernel,
        out_shape=(shape((rows, width)),) * 2 + (square,) * 3,
        in_specs=[SM] * 2 + [VM] * 7 + [HBM] * 2,
        out_specs=(VM,) * 5,
        scratch_shapes=[
            pltpu.VMEM((points + 2 * BG, CPAD), F32),
            pltpu.VMEM((slots * 16, CPAD), F32),
            pltpu.VMEM((slots * 16, CPAD), F32),
            pltpu.VMEM((HEADS, rows, CPAD), BF),
            weight,
            dma((4,)),
        ],
        compiler_params=params(44),
        name="encode",
    )(ends, enc_idx, grid_near, grid, grid_far, qt, bias, av, latent_init, enc_w, proc_w)
    normed_far = swap_far(normed)
    normed_near = swap_near(normed)
    q, num, den, top, aq, bo, co, pw3, dw1, dw2 = pl.pallas_call(
        project_kernel,
        out_shape=(shape((rows, width)),)
        + (shape((rows, width), F32),) * 3
        + (shape((CPAD, width)), shape((width, CPAD)), shape((CPAD, CPAD)))
        + (square,) * 3,
        in_specs=[VM] * 7 + [HBM] * 2,
        out_specs=(VM,) * 10,
        scratch_shapes=[pltpu.VMEM((rows, width), BF)] * 2 + [weight] * 2 + [dma((5,))],
        compiler_params=params(36),
        cost_estimate=pl.CostEstimate(flops=3 * 10**9, bytes_accessed=12 * 2**20, transcendentals=0),
        name="project",
    )(normed, win, wout, scale, pw0, pw1, pw2, proc_w, dec_w)
    half_scratch = [
        pltpu.VMEM((rows // 2, WIN - rows // 2), F32),
        pltpu.VMEM((rows // 2, width), BF),
    ]
    wide = shape((WIN, width))
    mesh_outer, keys, values = pl.pallas_call(
        window_outer_kernel,
        out_shape=(shape((BL, width)), wide, wide),
        in_specs=[SM] + [VM] * 10,
        out_specs=(VM,) * 3,
        scratch_shapes=half_scratch,
        compiler_params=params(24),
        name="window_outer",
    )(ends, q, num, den, top, normed_near, normed_far, latent, pw1, pw2, pw3)
    mesh_far = swap_far(mesh_outer)
    mesh_inner = pl.pallas_call(
        window_inner_kernel,
        out_shape=shape((BL, width)),
        in_specs=[SM] + [VM] * 8,
        out_specs=VM,
        scratch_shapes=half_scratch,
        compiler_params=params(24),
        cost_estimate=pl.CostEstimate(flops=3 * 10**9, bytes_accessed=12 * 2**20, transcendentals=0),
        name="window_inner",
    )(ends, q, num, den, top, keys, values, latent, pw3)
    mesh_near = swap_near(mesh_inner)
    mesh_far = pl.pallas_call(
        pass_kernel,
        out_shape=shape((BL, width)),
        in_specs=[pl.BlockSpec(memory_space=pl.ANY)],
        out_specs=pl.BlockSpec(memory_space=pl.ANY),
        input_output_aliases={0: 0},
        compiler_params=params(16),
        name="pass",
    )(mesh_far)
    nodes = rows + 2 * BL
    dq, dk, dv = pl.pallas_call(
        prepare_kernel,
        out_shape=(
            shape((points * 8, 128), F32),
            shape((rows * 8, 128), F32),
            shape((rows * 8, 128), F32),
        ),
        in_specs=[SM] + [VM] * 6,
        out_specs=(VM,) * 3,
        compiler_params=params(24),
        cost_estimate=pl.CostEstimate(flops=10**6, bytes_accessed=2**16, transcendentals=0),
        name="prepare",
    )(ends, mesh_inner, mesh_outer, grid, aq, dw1, dw2)
    out = pl.pallas_call(
        decode_kernel,
        out_shape=shape((channels, points)),
        in_specs=[SM] * 2 + [VM] * 10,
        out_specs=VM,
        scratch_shapes=[
            pltpu.VMEM((nodes * 8, 128), F32),
            pltpu.VMEM((nodes * 8, 128), F32),
            pltpu.VMEM((3, CHUNK * 4, 256), BF),
            pltpu.VMEM((3, CHUNK * 4, 256), F32),
            pltpu.VMEM((points * 8, 128), F32),
        ],
        compiler_params=params(32),
        name="decode",
    )(ends, dec_idx, mesh_far, mesh_near, dk, dv, dq, grid, bo, co, dw1, dw2)
    return out.T


def solution(mesh):
    both = ("wide", "narrow")
    placed = (
        P(both, None),
        P(both, None),
        P(both, None),
        P(both),
        P(both, None),
        P(),
        P(),
        P(),
        P(),
        P(),
        P(),
    )
    return jax.shard_map(
        on_device,
        mesh=mesh,
        in_specs=placed,
        out_specs=P(both, None),
        check_vma=False,
    )
```

```python
import math

import jax
import jax.numpy as jnp
from jax import lax
from jax.experimental import pallas as pl
from jax.experimental.pallas import tpu as pltpu
from jax.sharding import PartitionSpec as P

WIN = 512
BG = 1024
BL = 128
HEADS = 16
SIZE = 64
PAIRS = HEADS // 2
CPAD = 128
LOG2E = math.log2(math.e)
NEG = -1e30
BF = jnp.bfloat16
F32 = jnp.float32

VM = pl.BlockSpec(memory_space=pltpu.VMEM)
SM = pl.BlockSpec(memory_space=pltpu.SMEM)
HBM = pl.BlockSpec(memory_space=pltpu.HBM)


def dot(a, b):
    return jnp.dot(a, b, preferred_element_type=F32)


def dot_t(a, b):
    return lax.dot_general(a, b, (((1,), (1,)), ((), ())), preferred_element_type=F32)


def low_half(shape):
    return lax.broadcasted_iota(jnp.int32, shape, len(shape) - 1) < SIZE


def sides(core, near, far):
    return jnp.where(core == 0, far, near), jnp.where(core == 0, near, far)


def params(mib):
    return pltpu.CompilerParams(vmem_limit_bytes=mib * 2**20)


def fetch(source, rows, buffers, sems):
    copies = [
        pltpu.make_async_copy(source.at[row], buf, sems.at[at])
        for row, buf, at in zip(rows, buffers, range(len(rows)))
    ]
    for copy in copies:
        copy.start()
    return copies


def fold_kernel(win, enc_w, lat, scale, *others):
    qt, av, w0, w1, w2, sems = others[-6:]
    got = fetch(enc_w, (1, 0, 2), (w1, w0, w2), sems)
    got[0].wait()
    ak = dot(win[...], w1[...]).astype(BF)
    got[1].wait()
    q = (dot(lat[...], w0[...]) * scale[0:1, :]).astype(BF)
    low = low_half((1, 128))
    for pair in range(PAIRS):
        at = slice(pair * 128, pair * 128 + 128)
        keys = ak[:, at]
        both = q[:, at]
        zero = jnp.zeros_like(both)
        qt[2 * pair] = dot_t(jnp.where(low, both, zero), keys).astype(BF)
        qt[2 * pair + 1] = dot_t(jnp.where(low, zero, both), keys).astype(BF)
    got[2].wait()
    av[...] = dot(win[...], w2[...]).astype(BF)


def encode_kernel(
    ends, idx, near, own, far, qt, bias, av, lat, enc_w, proc_w,
    latent, normed, pw0, pw1, pw2,
    grid, wide, ge0, ge1, z, w3, sems,
):
    got = fetch(enc_w, (3,), (w3,), sems.at[pl.ds(0, 1)])
    later = fetch(proc_w, (0, 1, 2), (pw0, pw1, pw2), sems.at[pl.ds(1, 3)])
    rows = lat.shape[0]
    groups = rows // 16
    reach = near.shape[1]
    wide[...] = jnp.zeros_like(wide)
    for begin in (0, own.shape[1] + reach):
        given = sides(ends[2], near[...], far[...])[begin > 0]
        wide[0 : given.shape[0], :] = given.astype(F32)
        for part in range(0, reach, 512):
            grid[begin + part : begin + part + 512, :] = wide[:, part : part + 512].T
    for part in range(0, own.shape[1], 512):
        grid[reach + part : reach + part + 512, :] = own[:, part : part + 512].astype(F32).T
    row = lax.broadcasted_iota(jnp.int32, (256, 256), 0)
    col = lax.broadcasted_iota(jnp.int32, (256, 256), 1)
    diag = jnp.where(row % 16 == col % 16, 0.0, NEG)

    def collect(number, ge):
        base = number * 16
        for slot in range(16):
            for node in range(16):
                edge = slot * 16 + node
                ge[pl.ds(edge, 1), :] = grid[pl.ds(idx[base + (slot * rows + node)], 1), :]

    def attend(number, ge):
        points = ge[...].astype(BF)
        these = slice(number * 16, number * 16 + 16)
        queries = qt[:, these, :].reshape(256, CPAD)
        score = dot_t(queries, points) + (diag + bias[number : number + 1, :])
        expo = jnp.exp2(score - jnp.max(score, axis=1, keepdims=True)).astype(BF)
        mixed = dot(expo, jnp.concatenate([points, jnp.ones_like(points)], axis=1))
        mixed = mixed[:, :CPAD] * (1.0 / mixed[:, CPAD:])
        z[:, these, :] = mixed.reshape(16, 16, CPAD).astype(BF)

    buffers = (ge0, ge1)
    collect(0, ge0)
    for number in range(groups):
        attend(number, buffers[number % 2])
        if number + 1 < groups:
            collect(number + 1, buffers[(number + 1) % 2])
    low = low_half((1, 128))
    parts = []
    for pair in range(PAIRS):
        values = av[:, pair * 128 : pair * 128 + 128]
        zero = jnp.zeros_like(values)
        parts.append(
            dot(z[2 * pair], jnp.where(low, values, zero))
            + dot(z[2 * pair + 1], jnp.where(low, zero, values))
        )
    encoded = jnp.concatenate(parts, axis=1).astype(BF)
    got[0].wait()
    rounded = (lat[...].astype(F32) + dot(encoded, w3[...])).astype(BF)
    latent[...] = rounded
    wide = rounded.astype(F32)
    center = wide - jnp.mean(wide, axis=1, keepdims=True)
    spread = jnp.mean(center * center, axis=1, keepdims=True)
    normed[...] = (center * lax.rsqrt(spread + 1e-05)).astype(BF)
    for copy in later:
        copy.wait()


def attend_pair(both, keys, values, bias):
    low = low_half((1, 128))
    zero = jnp.zeros_like(both)
    rows = both.shape[0]
    stacked = jnp.concatenate([jnp.where(low, both, zero), jnp.where(low, zero, both)], axis=0)
    score = dot_t(stacked, keys)
    if bias is not None:
        score = (score.reshape(2, rows, -1) + bias[None]).reshape(2 * rows, -1)
    highest = jnp.max(score, axis=1, keepdims=True)
    expo = jnp.exp2(score - highest).astype(BF)
    total = dot(expo, jnp.concatenate([values, jnp.ones_like(values)], axis=1))
    highest = jnp.broadcast_to(highest, (2 * rows, 128))
    return (
        jnp.where(low, total[:rows, :128], total[rows:, :128]),
        jnp.where(low, total[:rows, 128:], total[rows:, 128:]),
        jnp.where(low, highest[:rows], highest[rows:]),
    )


def project_kernel(
    normed, win, wout, scale, wq, wk, wv, proc_w, dec_w,
    q, num, den, top, aq, bo, co, pw3, dw1, dw2, k, v, dw0, dw3, sems,
):
    got = fetch(dec_w, (0, 3), (dw0, dw3), sems.at[pl.ds(0, 2)])
    later = fetch(proc_w, (3,), (pw3,), sems.at[pl.ds(2, 1)])
    later += fetch(dec_w, (1, 2), (dw1, dw2), sems.at[pl.ds(3, 2)])
    rows = normed[...]
    q[...] = (dot(rows, wq[...]) * scale[1:2, :]).astype(BF)
    k[...] = dot(rows, wk[...]).astype(BF)
    v[...] = dot(rows, wv[...]).astype(BF)
    for pair in range(PAIRS):
        at = slice(pair * 128, pair * 128 + 128)
        num[:, at], den[:, at], top[:, at] = attend_pair(q[:, at], k[:, at], v[:, at], None)
    co[...] = dot_t(wout[...], win[...]).astype(BF)
    got[0].wait()
    aq[...] = (dot(win[...], dw0[...]) * scale[2:3, :]).astype(BF)
    got[1].wait()
    bo[...] = dot_t(dw3[...], wout[...]).astype(BF)
    for copy in later:
        copy.wait()


def window_half(side, ends, q, keys, values, num, den, top, latent, wo, bias, mixed, out):
    half, span = bias.shape
    row = lax.broadcasted_iota(jnp.int32, (half, span), 0)
    col = lax.broadcasted_iota(jnp.int32, (half, span), 1)
    begin = pl.multiple_of(side * half, half)
    place = col + begin
    place = jnp.where(place < WIN // 2, place, place + 2 * half)
    far = place - begin - row
    inside = (far >= 0) & (far <= WIN) & (place >= ends[0]) & (place < ends[1])
    bias[...] = jnp.where(inside, 0.0, NEG)
    these = pl.ds(begin, half)
    band = pl.ds(begin, span)
    for pair in range(PAIRS):
        at = slice(pair * 128, pair * 128 + 128)
        more, weight, highest = attend_pair(
            q[these, at], keys[band, at], values[band, at], bias[...]
        )
        own = top[these, at]
        joint = jnp.maximum(own, highest)
        own = jnp.exp2(own - joint)
        other = jnp.exp2(highest - joint)
        mixed[:, at] = (
            (num[these, at] * own + more * other) / (den[these, at] * own + weight * other)
        ).astype(BF)
    out[...] = (latent[these, :].astype(F32) + dot(mixed[...], wo[...])).astype(BF)


def window_outer_kernel(
    ends, q, num, den, top, near, far, latent, wk, wv, wo, outer, keys, values, bias, mixed
):
    halo = jnp.concatenate(sides(ends[2], near[...], far[...]), axis=0)
    keys[...] = dot(halo, wk[...]).astype(BF)
    values[...] = dot(halo, wv[...]).astype(BF)
    window_half(
        ends[2], ends, q, keys, values, num, den, top, latent, wo, bias, mixed, outer
    )


def window_inner_kernel(
    ends, q, num, den, top, keys, values, latent, wo, inner, bias, mixed
):
    window_half(
        1 - ends[2], ends, q, keys, values, num, den, top, latent, wo, bias, mixed, inner
    )


CHUNK = 128


def to_tiles(rows, weight, tiles, begin):
    count = rows.shape[0]
    for two in range(4):
        wide = dot(rows, weight[:, two * 256 : two * 256 + 256])
        for block in (2 * two, 2 * two + 1):
            tiles[pl.ds(begin * 8 + block, count, stride=8), :] = wide[
                :, block % 2 * 128 : block % 2 * 128 + 128
            ]


def prepare_kernel(ends, inner, outer, state, aq, wk, wv, q, k, v):
    own = jnp.concatenate(sides(ends[2], inner[...], outer[...]), axis=0)
    to_tiles(own, wk, k, 0)
    to_tiles(own, wv, v, 0)
    points = state.shape[1]
    for first in range(0, points, 512):
        to_tiles(state[:, first : first + 512].astype(F32).T.astype(BF), aq, q, first)


def decode_kernel(
    ends, idx, far, near, ko, vo, q, grid, bo, co, wk, wv, out, kf, vf, prod, wts, dec
):
    points = grid.shape[1]
    side = near.shape[0]
    halo = jnp.concatenate(sides(ends[2], near[...], far[...]), axis=0)
    for weight, tiles, own in ((wk, kf, ko), (wv, vf, vo)):
        tiles[side * 8 : side * 8 + own.shape[0], :] = own[...]
        for two in range(4):
            wide = dot(halo, weight[:, two * 256 : two * 256 + 256])
            for block in (2 * two, 2 * two + 1):
                both = wide[:, block % 2 * 128 : block % 2 * 128 + 128]
                tiles[pl.ds(block, side, stride=8), :] = both[:side]
                tiles[pl.ds(side * 8 + own.shape[0] + block, side, stride=8), :] = both[side:]
    head_row = lax.broadcasted_iota(jnp.int32, (256, 256), 0) // SIZE
    head_col = lax.broadcasted_iota(jnp.int32, (256, 256), 1) // SIZE
    ones = jnp.where(head_row == head_col, 1.0, 0.0).astype(BF)
    sub = 128

    def one_chunk(number, carry):
        first = pl.multiple_of(number * CHUNK, CHUNK)

        def tile_of(tiles, edge, at):
            return tiles[pl.ds(pl.multiple_of(idx[edge * points + first + at], 8), 8), :]

        for quad in range(0, CHUNK, 4):
            mine = [
                q[pl.ds(pl.multiple_of((first + quad + at) * 8, 8), 8), :] for at in range(4)
            ]
            for edge in range(3):
                terms = [mine[at] * tile_of(kf, edge, quad + at) for at in range(4)]
                place = slice(quad * 4, quad * 4 + 16)
                prod[edge, place, 0:128] = jnp.concatenate([terms[0], terms[2]], axis=0).astype(BF)
                prod[edge, place, 128:256] = jnp.concatenate([terms[1], terms[3]], axis=0).astype(BF)
        for begin in range(0, CHUNK * 4, sub):
            score = dot(prod[:, begin : begin + sub, :].reshape(3 * sub, 256), ones)
            score = [score[edge * sub : edge * sub + sub] for edge in range(3)]
            highest = jnp.maximum(jnp.maximum(score[0], score[1]), score[2])
            expo = [jnp.exp2(part - highest) for part in score]
            inverse = 1.0 / (expo[0] + expo[1] + expo[2])
            for edge in range(3):
                wts[edge, begin : begin + sub, :] = expo[edge] * inverse
        for at in range(CHUNK):
            top = at // 4 * 16 + (at % 4) // 2 * 8
            lane = at % 2 * 128
            total = None
            for edge in range(3):
                term = wts[edge, top : top + 8, lane : lane + 128] * tile_of(vf, edge, at)
                total = term if total is None else total + term
            dec[pl.ds(pl.multiple_of((first + at) * 8, 8), 8), :] = total
        return carry

    lax.fori_loop(0, points // CHUNK, one_chunk, 0)
    block = 256
    for first in range(0, points, block):
        wide = jnp.concatenate(
            [dec[pl.ds(first * 8 + part, block, stride=8), :] for part in range(8)], axis=1
        ).astype(BF)
        result = dot(wide, bo[...]).T + dot(co[...], grid[:, first : first + block])
        out[:, first : first + block] = result[: out.shape[0], :].astype(BF)


def pass_kernel(given, same):
    pass


def shape(dims, kind=BF):
    return jax.ShapeDtypeStruct(dims, kind)


def swap_near(inner):
    return lax.ppermute(inner, "narrow", [(0, 1), (1, 0)])


def swap_far(outer):
    axes = ("wide", "narrow")
    pairs = []
    for i in range(1, lax.axis_size(axes) - 1, 2):
        pairs += [(i, i + 1), (i + 1, i)]
    return lax.ppermute(outer, axes, pairs)


def on_device(
    grid_state,
    latent_init,
    enc_src,
    enc_count,
    dec_src,
    w_in,
    enc_w,
    proc_w,
    dec_w,
    w_out,
    logit_scale,
):
    points, channels = grid_state.shape
    rows, width = latent_init.shape
    slots = enc_src.shape[1]
    place = lax.axis_index(("wide", "narrow"))
    total = rows * lax.axis_size(("wide", "narrow"))
    weight = pltpu.VMEM((width, width), BF)
    dma = pltpu.SemaphoreType.DMA

    grid = jnp.pad(grid_state.T, ((0, CPAD - channels), (0, 0)))
    core = lax.axis_index("narrow")
    channel_rows = grid_state.T
    grid_far = swap_far(lax.dynamic_slice_in_dim(channel_rows, core * (points - BG), BG, 1))
    grid_near = swap_near(
        lax.dynamic_slice_in_dim(channel_rows, (1 - core) * (points - BG), BG, 1)
    )
    win = jnp.pad(w_in, ((0, CPAD - channels), (0, 0)))
    wout = jnp.pad(w_out.T, ((0, CPAD - channels), (0, 0)))
    scale = jnp.repeat(logit_scale * (LOG2E / math.sqrt(SIZE)), SIZE, axis=1)
    enc_idx = jnp.clip(enc_src.T, 0, points + 2 * BG - 1).reshape(-1)
    live = jnp.arange(slots, dtype=jnp.int32)[:, None] < enc_count[None, :]
    bias = jnp.where(live, 0.0, NEG).astype(F32)
    bias = bias.reshape(slots, rows // 16, 16).transpose(1, 0, 2).reshape(rows // 16, slots * 16)
    dec_idx = jnp.clip(dec_src.T - (place * rows - BL), 0, rows + 2 * BL - 1).reshape(-1) * 8
    ends = jnp.stack([WIN // 2 - place * rows, total + WIN // 2 - place * rows, core])

    qt, av = pl.pallas_call(
        fold_kernel,
        out_shape=(shape((HEADS, rows, CPAD)), shape((CPAD, width))),
        in_specs=[VM, HBM, VM, VM] + [pl.BlockSpec(memory_space=pl.ANY)] * 5,
        out_specs=(VM, VM),
        scratch_shapes=[weight] * 3 + [dma((3,))],
        compiler_params=params(50),
        cost_estimate=pl.CostEstimate(flops=2 * 10**9, bytes_accessed=8 * 2**20, transcendentals=0),
        name="fold",
    )(win, enc_w, latent_init, scale, wout, enc_idx, bias, dec_idx, ends)
    square = shape((width, width))
    latent, normed, pw0, pw1, pw2 = pl.pallas_call(
        encode_kernel,
        out_shape=(shape((rows, width)),) * 2 + (square,) * 3,
        in_specs=[SM] * 2 + [VM] * 7 + [HBM] * 2,
        out_specs=(VM,) * 5,
        scratch_shapes=[
            pltpu.VMEM((points + 2 * BG, CPAD), F32),
            pltpu.VMEM((CPAD, BG), F32),
            pltpu.VMEM((slots * 16, CPAD), F32),
            pltpu.VMEM((slots * 16, CPAD), F32),
            pltpu.VMEM((HEADS, rows, CPAD), BF),
            weight,
            dma((4,)),
        ],
        compiler_params=params(44),
        name="encode",
    )(ends, enc_idx, grid_near, grid, grid_far, qt, bias, av, latent_init, enc_w, proc_w)
    normed_far = swap_far(normed)
    normed_near = swap_near(normed)
    q, num, den, top, aq, bo, co, pw3, dw1, dw2 = pl.pallas_call(
        project_kernel,
        out_shape=(shape((rows, width)),)
        + (shape((rows, width), F32),) * 3
        + (shape((CPAD, width)), shape((width, CPAD)), shape((CPAD, CPAD)))
        + (square,) * 3,
        in_specs=[VM] * 7 + [HBM] * 2,
        out_specs=(VM,) * 10,
        scratch_shapes=[pltpu.VMEM((rows, width), BF)] * 2 + [weight] * 2 + [dma((5,))],
        compiler_params=params(36),
        cost_estimate=pl.CostEstimate(flops=3 * 10**9, bytes_accessed=12 * 2**20, transcendentals=0),
        name="project",
    )(normed, win, wout, scale, pw0, pw1, pw2, proc_w, dec_w)
    half_scratch = [
        pltpu.VMEM((rows // 2, WIN - rows // 2), F32),
        pltpu.VMEM((rows // 2, width), BF),
    ]
    wide = shape((WIN, width))
    mesh_outer, keys, values = pl.pallas_call(
        window_outer_kernel,
        out_shape=(shape((BL, width)), wide, wide),
        in_specs=[SM] + [VM] * 10,
        out_specs=(VM,) * 3,
        scratch_shapes=half_scratch,
        compiler_params=params(24),
        name="window_outer",
    )(ends, q, num, den, top, normed_near, normed_far, latent, pw1, pw2, pw3)
    mesh_far = swap_far(mesh_outer)
    mesh_inner = pl.pallas_call(
        window_inner_kernel,
        out_shape=shape((BL, width)),
        in_specs=[SM] + [VM] * 8,
        out_specs=VM,
        scratch_shapes=half_scratch,
        compiler_params=params(24),
        cost_estimate=pl.CostEstimate(flops=3 * 10**9, bytes_accessed=12 * 2**20, transcendentals=0),
        name="window_inner",
    )(ends, q, num, den, top, keys, values, latent, pw3)
    mesh_near = swap_near(mesh_inner)
    mesh_far = pl.pallas_call(
        pass_kernel,
        out_shape=shape((BL, width)),
        in_specs=[pl.BlockSpec(memory_space=pl.ANY)],
        out_specs=pl.BlockSpec(memory_space=pl.ANY),
        input_output_aliases={0: 0},
        compiler_params=params(16),
        name="pass",
    )(mesh_far)
    nodes = rows + 2 * BL
    dq, dk, dv = pl.pallas_call(
        prepare_kernel,
        out_shape=(
            shape((points * 8, 128), F32),
            shape((rows * 8, 128), F32),
            shape((rows * 8, 128), F32),
        ),
        in_specs=[SM] + [VM] * 6,
        out_specs=(VM,) * 3,
        compiler_params=params(24),
        cost_estimate=pl.CostEstimate(flops=10**6, bytes_accessed=2**16, transcendentals=0),
        name="prepare",
    )(ends, mesh_inner, mesh_outer, grid, aq, dw1, dw2)
    out = pl.pallas_call(
        decode_kernel,
        out_shape=shape((channels, points)),
        in_specs=[SM] * 2 + [VM] * 10,
        out_specs=VM,
        scratch_shapes=[
            pltpu.VMEM((nodes * 8, 128), F32),
            pltpu.VMEM((nodes * 8, 128), F32),
            pltpu.VMEM((3, CHUNK * 4, 256), BF),
            pltpu.VMEM((3, CHUNK * 4, 256), F32),
            pltpu.VMEM((points * 8, 128), F32),
        ],
        compiler_params=params(32),
        name="decode",
    )(ends, dec_idx, mesh_far, mesh_near, dk, dv, dq, grid, bo, co, dw1, dw2)
    return out.T


def solution(mesh):
    both = ("wide", "narrow")
    placed = (
        P(both, None),
        P(both, None),
        P(both, None),
        P(both),
        P(both, None),
        P(),
        P(),
        P(),
        P(),
        P(),
        P(),
    )
    return jax.shard_map(
        on_device,
        mesh=mesh,
        in_specs=placed,
        out_specs=P(both, None),
        check_vma=False,
    )
```

```python
import math

import jax
import jax.numpy as jnp
from jax import lax
from jax.experimental import pallas as pl
from jax.experimental.pallas import tpu as pltpu
from jax.sharding import PartitionSpec as P

WIN = 512
BG = 1024
BL = 128
HEADS = 16
SIZE = 64
PAIRS = HEADS // 2
CPAD = 128
LOG2E = math.log2(math.e)
NEG = -1e30
BF = jnp.bfloat16
F32 = jnp.float32

VM = pl.BlockSpec(memory_space=pltpu.VMEM)
SM = pl.BlockSpec(memory_space=pltpu.SMEM)
HBM = pl.BlockSpec(memory_space=pltpu.HBM)


def dot(a, b):
    return jnp.dot(a, b, preferred_element_type=F32)


def dot_t(a, b):
    return lax.dot_general(a, b, (((1,), (1,)), ((), ())), preferred_element_type=F32)


def low_half(shape):
    return lax.broadcasted_iota(jnp.int32, shape, len(shape) - 1) < SIZE


def sides(core, near, far):
    return jnp.where(core == 0, far, near), jnp.where(core == 0, near, far)


def params(mib):
    return pltpu.CompilerParams(vmem_limit_bytes=mib * 2**20)


def fetch(source, rows, buffers, sems):
    copies = [
        pltpu.make_async_copy(source.at[row], buf, sems.at[at])
        for row, buf, at in zip(rows, buffers, range(len(rows)))
    ]
    for copy in copies:
        copy.start()
    return copies


def lane_scale(scale, row):
    low = low_half((1, 128))
    factor = LOG2E / math.sqrt(SIZE)
    return jnp.concatenate(
        [
            jnp.where(low, scale[row, 2 * pair] * factor, scale[row, 2 * pair + 1] * factor)
            for pair in range(PAIRS)
        ],
        axis=1,
    )


def fold_kernel(w_in, w_out, enc_w, lat, scale, *others):
    qt, av, win, wout, wide, w0, w1, w2, sems = others[-9:]
    got = fetch(enc_w, (1, 0, 2), (w1, w0, w2), sems)
    wide[...] = jnp.zeros_like(wide)
    for given, padded in ((w_in, win), (w_out, wout)):
        wide[0 : given.shape[0], :] = given[...].astype(F32)
        padded[...] = wide[...].astype(BF)
    got[0].wait()
    ak = dot(win[...], w1[...]).astype(BF)
    got[1].wait()
    q = (dot(lat[...], w0[...]) * lane_scale(scale, 0)).astype(BF)
    low = low_half((1, 128))
    for pair in range(PAIRS):
        at = slice(pair * 128, pair * 128 + 128)
        keys = ak[:, at]
        both = q[:, at]
        zero = jnp.zeros_like(both)
        qt[2 * pair] = dot_t(jnp.where(low, both, zero), keys).astype(BF)
        qt[2 * pair + 1] = dot_t(jnp.where(low, zero, both), keys).astype(BF)
    got[2].wait()
    av[...] = dot(win[...], w2[...]).astype(BF)


def encode_kernel(
    ends, idx, near, own, far, qt, bias, av, lat, enc_w, proc_w,
    latent, normed, pw0, pw1, pw2,
    grid, wide, ge0, ge1, z, w3, sems,
):
    got = fetch(enc_w, (3,), (w3,), sems.at[pl.ds(0, 1)])
    later = fetch(proc_w, (0, 1, 2), (pw0, pw1, pw2), sems.at[pl.ds(1, 3)])
    rows = lat.shape[0]
    groups = rows // 16
    reach = near.shape[1]
    wide[...] = jnp.zeros_like(wide)
    for begin in (0, own.shape[1] + reach):
        given = sides(ends[2], near[...], far[...])[begin > 0]
        wide[0 : given.shape[0], :] = given.astype(F32)
        for part in range(0, reach, 512):
            grid[begin + part : begin + part + 512, :] = wide[:, part : part + 512].T
    for part in range(0, own.shape[1], 512):
        grid[reach + part : reach + part + 512, :] = own[:, part : part + 512].astype(F32).T
    row = lax.broadcasted_iota(jnp.int32, (256, 256), 0)
    col = lax.broadcasted_iota(jnp.int32, (256, 256), 1)
    diag = jnp.where(row % 16 == col % 16, 0.0, NEG)

    def collect(number, ge):
        base = number * 16
        for slot in range(16):
            for node in range(16):
                edge = slot * 16 + node
                ge[pl.ds(edge, 1), :] = grid[pl.ds(idx[base + (slot * rows + node)], 1), :]

    def attend(number, ge):
        points = ge[...].astype(BF)
        these = slice(number * 16, number * 16 + 16)
        queries = qt[:, these, :].reshape(256, CPAD)
        score = dot_t(queries, points) + (diag + bias[number : number + 1, :])
        expo = jnp.exp2(score - jnp.max(score, axis=1, keepdims=True)).astype(BF)
        mixed = dot(expo, jnp.concatenate([points, jnp.ones_like(points)], axis=1))
        mixed = mixed[:, :CPAD] * (1.0 / mixed[:, CPAD:])
        z[:, these, :] = mixed.reshape(16, 16, CPAD).astype(BF)

    buffers = (ge0, ge1)
    collect(0, ge0)
    for number in range(groups):
        attend(number, buffers[number % 2])
        if number + 1 < groups:
            collect(number + 1, buffers[(number + 1) % 2])
    low = low_half((1, 128))
    parts = []
    for pair in range(PAIRS):
        values = av[:, pair * 128 : pair * 128 + 128]
        zero = jnp.zeros_like(values)
        parts.append(
            dot(z[2 * pair], jnp.where(low, values, zero))
            + dot(z[2 * pair + 1], jnp.where(low, zero, values))
        )
    encoded = jnp.concatenate(parts, axis=1).astype(BF)
    got[0].wait()
    rounded = (lat[...].astype(F32) + dot(encoded, w3[...])).astype(BF)
    latent[...] = rounded
    wide = rounded.astype(F32)
    center = wide - jnp.mean(wide, axis=1, keepdims=True)
    spread = jnp.mean(center * center, axis=1, keepdims=True)
    normed[...] = (center * lax.rsqrt(spread + 1e-05)).astype(BF)
    for copy in later:
        copy.wait()


def attend_pair(both, keys, values, bias):
    low = low_half((1, 128))
    zero = jnp.zeros_like(both)
    rows = both.shape[0]
    stacked = jnp.concatenate([jnp.where(low, both, zero), jnp.where(low, zero, both)], axis=0)
    score = dot_t(stacked, keys)
    if bias is not None:
        score = (score.reshape(2, rows, -1) + bias[None]).reshape(2 * rows, -1)
    highest = jnp.max(score, axis=1, keepdims=True)
    expo = jnp.exp2(score - highest).astype(BF)
    total = dot(expo, jnp.concatenate([values, jnp.ones_like(values)], axis=1))
    highest = jnp.broadcast_to(highest, (2 * rows, 128))
    return (
        jnp.where(low, total[:rows, :128], total[rows:, :128]),
        jnp.where(low, total[:rows, 128:], total[rows:, 128:]),
        jnp.where(low, highest[:rows], highest[rows:]),
    )


def project_kernel(
    normed, win, wout, scale, wq, wk, wv, proc_w, dec_w,
    q, num, den, top, aq, bo, co, pw3, dw1, dw2, k, v, dw0, dw3, sems,
):
    got = fetch(dec_w, (0, 3), (dw0, dw3), sems.at[pl.ds(0, 2)])
    later = fetch(proc_w, (3,), (pw3,), sems.at[pl.ds(2, 1)])
    later += fetch(dec_w, (1, 2), (dw1, dw2), sems.at[pl.ds(3, 2)])
    rows = normed[...]
    q[...] = (dot(rows, wq[...]) * lane_scale(scale, 1)).astype(BF)
    k[...] = dot(rows, wk[...]).astype(BF)
    v[...] = dot(rows, wv[...]).astype(BF)
    for pair in range(PAIRS):
        at = slice(pair * 128, pair * 128 + 128)
        num[:, at], den[:, at], top[:, at] = attend_pair(q[:, at], k[:, at], v[:, at], None)
    co[...] = dot_t(wout[...], win[...]).astype(BF)
    got[0].wait()
    aq[...] = (dot(win[...], dw0[...]) * lane_scale(scale, 2)).astype(BF)
    got[1].wait()
    bo[...] = dot_t(dw3[...], wout[...]).astype(BF)
    for copy in later:
        copy.wait()


def window_half(side, ends, q, keys, values, num, den, top, latent, wo, bias, mixed, out):
    half, span = bias.shape
    row = lax.broadcasted_iota(jnp.int32, (half, span), 0)
    col = lax.broadcasted_iota(jnp.int32, (half, span), 1)
    begin = pl.multiple_of(side * half, half)
    place = col + begin
    place = jnp.where(place < WIN // 2, place, place + 2 * half)
    far = place - begin - row
    inside = (far >= 0) & (far <= WIN) & (place >= ends[0]) & (place < ends[1])
    bias[...] = jnp.where(inside, 0.0, NEG)
    these = pl.ds(begin, half)
    band = pl.ds(begin, span)
    for pair in range(PAIRS):
        at = slice(pair * 128, pair * 128 + 128)
        more, weight, highest = attend_pair(
            q[these, at], keys[band, at], values[band, at], bias[...]
        )
        own = top[these, at]
        joint = jnp.maximum(own, highest)
        own = jnp.exp2(own - joint)
        other = jnp.exp2(highest - joint)
        mixed[:, at] = (
            (num[these, at] * own + more * other) / (den[these, at] * own + weight * other)
        ).astype(BF)
    out[...] = (latent[these, :].astype(F32) + dot(mixed[...], wo[...])).astype(BF)


def window_outer_kernel(
    ends, q, num, den, top, near, far, latent, wk, wv, wo, outer, keys, values, bias, mixed
):
    halo = jnp.concatenate(sides(ends[2], near[...], far[...]), axis=0)
    keys[...] = dot(halo, wk[...]).astype(BF)
    values[...] = dot(halo, wv[...]).astype(BF)
    window_half(
        ends[2], ends, q, keys, values, num, den, top, latent, wo, bias, mixed, outer
    )


def window_inner_kernel(
    ends, q, num, den, top, keys, values, latent, wo, inner, bias, mixed
):
    window_half(
        1 - ends[2], ends, q, keys, values, num, den, top, latent, wo, bias, mixed, inner
    )


CHUNK = 128


def to_tiles(rows, weight, tiles, begin):
    count = rows.shape[0]
    for two in range(4):
        wide = dot(rows, weight[:, two * 256 : two * 256 + 256])
        for block in (2 * two, 2 * two + 1):
            tiles[pl.ds(begin * 8 + block, count, stride=8), :] = wide[
                :, block % 2 * 128 : block % 2 * 128 + 128
            ]


def prepare_kernel(ends, inner, outer, state, aq, wk, wv, q, k, v):
    own = jnp.concatenate(sides(ends[2], inner[...], outer[...]), axis=0)
    to_tiles(own, wk, k, 0)
    to_tiles(own, wv, v, 0)
    points = state.shape[1]
    for first in range(0, points, 512):
        to_tiles(state[:, first : first + 512].astype(F32).T.astype(BF), aq, q, first)


def decode_kernel(
    ends, idx, far, near, ko, vo, q, grid, bo, co, wk, wv, out, kf, vf, prod, wts, dec
):
    points = grid.shape[1]
    side = near.shape[0]
    halo = jnp.concatenate(sides(ends[2], near[...], far[...]), axis=0)
    for weight, tiles, own in ((wk, kf, ko), (wv, vf, vo)):
        tiles[side * 8 : side * 8 + own.shape[0], :] = own[...]
        for two in range(4):
            wide = dot(halo, weight[:, two * 256 : two * 256 + 256])
            for block in (2 * two, 2 * two + 1):
                both = wide[:, block % 2 * 128 : block % 2 * 128 + 128]
                tiles[pl.ds(block, side, stride=8), :] = both[:side]
                tiles[pl.ds(side * 8 + own.shape[0] + block, side, stride=8), :] = both[side:]
    head_row = lax.broadcasted_iota(jnp.int32, (256, 256), 0) // SIZE
    head_col = lax.broadcasted_iota(jnp.int32, (256, 256), 1) // SIZE
    ones = jnp.where(head_row == head_col, 1.0, 0.0).astype(BF)
    sub = 128

    def one_chunk(number, carry):
        first = pl.multiple_of(number * CHUNK, CHUNK)

        def tile_of(tiles, edge, at):
            return tiles[pl.ds(pl.multiple_of(idx[edge * points + first + at], 8), 8), :]

        for quad in range(0, CHUNK, 4):
            mine = [
                q[pl.ds(pl.multiple_of((first + quad + at) * 8, 8), 8), :] for at in range(4)
            ]
            for edge in range(3):
                terms = [mine[at] * tile_of(kf, edge, quad + at) for at in range(4)]
                place = slice(quad * 4, quad * 4 + 16)
                prod[edge, place, 0:128] = jnp.concatenate([terms[0], terms[2]], axis=0).astype(BF)
                prod[edge, place, 128:256] = jnp.concatenate([terms[1], terms[3]], axis=0).astype(BF)
        for begin in range(0, CHUNK * 4, sub):
            score = dot(prod[:, begin : begin + sub, :].reshape(3 * sub, 256), ones)
            score = [score[edge * sub : edge * sub + sub] for edge in range(3)]
            highest = jnp.maximum(jnp.maximum(score[0], score[1]), score[2])
            expo = [jnp.exp2(part - highest) for part in score]
            inverse = 1.0 / (expo[0] + expo[1] + expo[2])
            for edge in range(3):
                wts[edge, begin : begin + sub, :] = expo[edge] * inverse
        for at in range(CHUNK):
            top = at // 4 * 16 + (at % 4) // 2 * 8
            lane = at % 2 * 128
            total = None
            for edge in range(3):
                term = wts[edge, top : top + 8, lane : lane + 128] * tile_of(vf, edge, at)
                total = term if total is None else total + term
            dec[pl.ds(pl.multiple_of((first + at) * 8, 8), 8), :] = total
        return carry

    lax.fori_loop(0, points // CHUNK, one_chunk, 0)
    block = 256
    for first in range(0, points, block):
        wide = jnp.concatenate(
            [dec[pl.ds(first * 8 + part, block, stride=8), :] for part in range(8)], axis=1
        ).astype(BF)
        result = dot(wide, bo[...]).T + dot(co[...], grid[:, first : first + block])
        out[:, first : first + block] = result[: out.shape[0], :].astype(BF)


def pass_kernel(given, same):
    pass


def shape(dims, kind=BF):
    return jax.ShapeDtypeStruct(dims, kind)


def swap_near(inner):
    return lax.ppermute(inner, "narrow", [(0, 1), (1, 0)])


def swap_far(outer):
    axes = ("wide", "narrow")
    pairs = []
    for i in range(1, lax.axis_size(axes) - 1, 2):
        pairs += [(i, i + 1), (i + 1, i)]
    return lax.ppermute(outer, axes, pairs)


def on_device(
    grid_state,
    latent_init,
    enc_src,
    enc_count,
    dec_src,
    w_in,
    enc_w,
    proc_w,
    dec_w,
    w_out,
    logit_scale,
):
    points, channels = grid_state.shape
    rows, width = latent_init.shape
    slots = enc_src.shape[1]
    place = lax.axis_index(("wide", "narrow"))
    total = rows * lax.axis_size(("wide", "narrow"))
    weight = pltpu.VMEM((width, width), BF)
    dma = pltpu.SemaphoreType.DMA

    grid = jnp.pad(grid_state.T, ((0, CPAD - channels), (0, 0)))
    core = lax.axis_index("narrow")
    channel_rows = grid_state.T
    grid_far = swap_far(lax.dynamic_slice_in_dim(channel_rows, core * (points - BG), BG, 1))
    grid_near = swap_near(
        lax.dynamic_slice_in_dim(channel_rows, (1 - core) * (points - BG), BG, 1)
    )
    enc_idx = jnp.clip(enc_src.T, 0, points + 2 * BG - 1).reshape(-1)
    live = jnp.arange(slots, dtype=jnp.int32)[:, None] < enc_count[None, :]
    bias = jnp.where(live, 0.0, NEG).astype(F32)
    bias = bias.reshape(slots, rows // 16, 16).transpose(1, 0, 2).reshape(rows // 16, slots * 16)
    dec_idx = jnp.clip(dec_src.T - (place * rows - BL), 0, rows + 2 * BL - 1).reshape(-1) * 8
    ends = jnp.stack([WIN // 2 - place * rows, total + WIN // 2 - place * rows, core])

    padded = shape((CPAD, width))
    qt, av, win, wout = pl.pallas_call(
        fold_kernel,
        out_shape=(shape((HEADS, rows, CPAD)), padded, padded, padded),
        in_specs=[VM, VM, HBM, VM, SM] + [pl.BlockSpec(memory_space=pl.ANY)] * 5,
        out_specs=(VM,) * 4,
        scratch_shapes=[pltpu.VMEM((CPAD, width), F32)] + [weight] * 3 + [dma((3,))],
        compiler_params=params(50),
        cost_estimate=pl.CostEstimate(flops=2 * 10**9, bytes_accessed=8 * 2**20, transcendentals=0),
        name="fold",
    )(w_in, w_out.T, enc_w, latent_init, logit_scale, enc_idx, bias, dec_idx, ends, grid)
    square = shape((width, width))
    latent, normed, pw0, pw1, pw2 = pl.pallas_call(
        encode_kernel,
        out_shape=(shape((rows, width)),) * 2 + (square,) * 3,
        in_specs=[SM] * 2 + [VM] * 7 + [HBM] * 2,
        out_specs=(VM,) * 5,
        scratch_shapes=[
            pltpu.VMEM((points + 2 * BG, CPAD), F32),
            pltpu.VMEM((CPAD, BG), F32),
            pltpu.VMEM((slots * 16, CPAD), F32),
            pltpu.VMEM((slots * 16, CPAD), F32),
            pltpu.VMEM((HEADS, rows, CPAD), BF),
            weight,
            dma((4,)),
        ],
        compiler_params=params(44),
        name="encode",
    )(ends, enc_idx, grid_near, grid, grid_far, qt, bias, av, latent_init, enc_w, proc_w)
    normed_far = swap_far(normed)
    normed_near = swap_near(normed)
    q, num, den, top, aq, bo, co, pw3, dw1, dw2 = pl.pallas_call(
        project_kernel,
        out_shape=(shape((rows, width)),)
        + (shape((rows, width), F32),) * 3
        + (shape((CPAD, width)), shape((width, CPAD)), shape((CPAD, CPAD)))
        + (square,) * 3,
        in_specs=[VM] * 3 + [SM] + [VM] * 3 + [HBM] * 2,
        out_specs=(VM,) * 10,
        scratch_shapes=[pltpu.VMEM((rows, width), BF)] * 2 + [weight] * 2 + [dma((5,))],
        compiler_params=params(36),
        cost_estimate=pl.CostEstimate(flops=3 * 10**9, bytes_accessed=12 * 2**20, transcendentals=0),
        name="project",
    )(normed, win, wout, logit_scale, pw0, pw1, pw2, proc_w, dec_w)
    half_scratch = [
        pltpu.VMEM((rows // 2, WIN - rows // 2), F32),
        pltpu.VMEM((rows // 2, width), BF),
    ]
    wide = shape((WIN, width))
    mesh_outer, keys, values = pl.pallas_call(
        window_outer_kernel,
        out_shape=(shape((BL, width)), wide, wide),
        in_specs=[SM] + [VM] * 10,
        out_specs=(VM,) * 3,
        scratch_shapes=half_scratch,
        compiler_params=params(24),
        name="window_outer",
    )(ends, q, num, den, top, normed_near, normed_far, latent, pw1, pw2, pw3)
    mesh_far = swap_far(mesh_outer)
    mesh_inner = pl.pallas_call(
        window_inner_kernel,
        out_shape=shape((BL, width)),
        in_specs=[SM] + [VM] * 8,
        out_specs=VM,
        scratch_shapes=half_scratch,
        compiler_params=params(24),
        cost_estimate=pl.CostEstimate(flops=3 * 10**9, bytes_accessed=12 * 2**20, transcendentals=0),
        name="window_inner",
    )(ends, q, num, den, top, keys, values, latent, pw3)
    mesh_near = swap_near(mesh_inner)
    mesh_far = pl.pallas_call(
        pass_kernel,
        out_shape=shape((BL, width)),
        in_specs=[pl.BlockSpec(memory_space=pl.ANY)],
        out_specs=pl.BlockSpec(memory_space=pl.ANY),
        input_output_aliases={0: 0},
        compiler_params=params(16),
        name="pass",
    )(mesh_far)
    nodes = rows + 2 * BL
    dq, dk, dv = pl.pallas_call(
        prepare_kernel,
        out_shape=(
            shape((points * 8, 128), F32),
            shape((rows * 8, 128), F32),
            shape((rows * 8, 128), F32),
        ),
        in_specs=[SM] + [VM] * 6,
        out_specs=(VM,) * 3,
        compiler_params=params(24),
        cost_estimate=pl.CostEstimate(flops=10**6, bytes_accessed=2**16, transcendentals=0),
        name="prepare",
    )(ends, mesh_inner, mesh_outer, grid, aq, dw1, dw2)
    out = pl.pallas_call(
        decode_kernel,
        out_shape=shape((channels, points)),
        in_specs=[SM] * 2 + [VM] * 10,
        out_specs=VM,
        scratch_shapes=[
            pltpu.VMEM((nodes * 8, 128), F32),
            pltpu.VMEM((nodes * 8, 128), F32),
            pltpu.VMEM((3, CHUNK * 4, 256), BF),
            pltpu.VMEM((3, CHUNK * 4, 256), F32),
            pltpu.VMEM((points * 8, 128), F32),
        ],
        compiler_params=params(32),
        name="decode",
    )(ends, dec_idx, mesh_far, mesh_near, dk, dv, dq, grid, bo, co, dw1, dw2)
    return out.T


def solution(mesh):
    both = ("wide", "narrow")
    placed = (
        P(both, None),
        P(both, None),
        P(both, None),
        P(both),
        P(both, None),
        P(),
        P(),
        P(),
        P(),
        P(),
        P(),
    )
    return jax.shard_map(
        on_device,
        mesh=mesh,
        in_specs=placed,
        out_specs=P(both, None),
        check_vma=False,
    )
```

```python
import math

import jax
import jax.numpy as jnp
from jax import lax
from jax.experimental import pallas as pl
from jax.experimental.pallas import tpu as pltpu
from jax.sharding import PartitionSpec as P

WIN = 512
BG = 1024
BL = 128
HEADS = 16
SIZE = 64
PAIRS = HEADS // 2
CPAD = 128
LOG2E = math.log2(math.e)
NEG = -1e30
BF = jnp.bfloat16
F32 = jnp.float32

VM = pl.BlockSpec(memory_space=pltpu.VMEM)
SM = pl.BlockSpec(memory_space=pltpu.SMEM)
HBM = pl.BlockSpec(memory_space=pltpu.HBM)


def dot(a, b):
    return jnp.dot(a, b, preferred_element_type=F32)


def dot_t(a, b):
    return lax.dot_general(a, b, (((1,), (1,)), ((), ())), preferred_element_type=F32)


def low_half(shape):
    return lax.broadcasted_iota(jnp.int32, shape, len(shape) - 1) < SIZE


def sides(core, near, far):
    return jnp.where(core == 0, far, near), jnp.where(core == 0, near, far)


def params(mib):
    return pltpu.CompilerParams(vmem_limit_bytes=mib * 2**20)


def fetch(source, rows, buffers, sems):
    copies = [
        pltpu.make_async_copy(source.at[row], buf, sems.at[at])
        for row, buf, at in zip(rows, buffers, range(len(rows)))
    ]
    for copy in copies:
        copy.start()
    return copies


def fold_kernel(w_in, w_out, state, enc_w, lat, scale, *others):
    qt, av, win, wout, grid, wide, w0, w1, w2, sems = others[-10:]
    got = fetch(enc_w, (1, 0, 2), (w1, w0, w2), sems)
    wide[...] = jnp.zeros_like(wide)
    for given, padded in ((w_in, win), (w_out, wout)):
        wide[0 : given.shape[0], :] = given[...].astype(F32)
        padded[...] = wide[...].astype(BF)
    reach = wide.shape[1]
    for begin in range(0, state.shape[1], reach):
        wide[0 : state.shape[0], :] = state[:, begin : begin + reach].astype(F32)
        grid[:, begin : begin + reach] = wide[...].astype(BF)
    got[0].wait()
    ak = dot(win[...], w1[...]).astype(BF)
    got[1].wait()
    q = (dot(lat[...], w0[...]) * scale[0:1, :]).astype(BF)
    low = low_half((1, 128))
    for pair in range(PAIRS):
        at = slice(pair * 128, pair * 128 + 128)
        keys = ak[:, at]
        both = q[:, at]
        zero = jnp.zeros_like(both)
        qt[2 * pair] = dot_t(jnp.where(low, both, zero), keys).astype(BF)
        qt[2 * pair + 1] = dot_t(jnp.where(low, zero, both), keys).astype(BF)
    got[2].wait()
    av[...] = dot(win[...], w2[...]).astype(BF)


def encode_kernel(
    ends, idx, near, own, far, qt, bias, av, lat, enc_w, proc_w,
    latent, normed, pw0, pw1, pw2,
    grid, wide, ge0, ge1, z, w3, sems,
):
    got = fetch(enc_w, (3,), (w3,), sems.at[pl.ds(0, 1)])
    later = fetch(proc_w, (0, 1, 2), (pw0, pw1, pw2), sems.at[pl.ds(1, 3)])
    rows = lat.shape[0]
    groups = rows // 16
    reach = near.shape[1]
    wide[...] = jnp.zeros_like(wide)
    for begin in (0, own.shape[1] + reach):
        given = sides(ends[2], near[...], far[...])[begin > 0]
        wide[0 : given.shape[0], :] = given.astype(F32)
        for part in range(0, reach, 512):
            grid[begin + part : begin + part + 512, :] = wide[:, part : part + 512].T
    for part in range(0, own.shape[1], 512):
        grid[reach + part : reach + part + 512, :] = own[:, part : part + 512].astype(F32).T
    row = lax.broadcasted_iota(jnp.int32, (256, 256), 0)
    col = lax.broadcasted_iota(jnp.int32, (256, 256), 1)
    diag = jnp.where(row % 16 == col % 16, 0.0, NEG)

    def collect(number, ge):
        base = number * 16
        for slot in range(16):
            for node in range(16):
                edge = slot * 16 + node
                ge[pl.ds(edge, 1), :] = grid[pl.ds(idx[base + (slot * rows + node)], 1), :]

    def attend(number, ge):
        points = ge[...].astype(BF)
        these = slice(number * 16, number * 16 + 16)
        queries = qt[:, these, :].reshape(256, CPAD)
        score = dot_t(queries, points) + (diag + bias[number : number + 1, :])
        expo = jnp.exp2(score - jnp.max(score, axis=1, keepdims=True)).astype(BF)
        mixed = dot(expo, jnp.concatenate([points, jnp.ones_like(points)], axis=1))
        mixed = mixed[:, :CPAD] * (1.0 / mixed[:, CPAD:])
        z[:, these, :] = mixed.reshape(16, 16, CPAD).astype(BF)

    buffers = (ge0, ge1)
    collect(0, ge0)
    for number in range(groups):
        attend(number, buffers[number % 2])
        if number + 1 < groups:
            collect(number + 1, buffers[(number + 1) % 2])
    low = low_half((1, 128))
    parts = []
    for pair in range(PAIRS):
        values = av[:, pair * 128 : pair * 128 + 128]
        zero = jnp.zeros_like(values)
        parts.append(
            dot(z[2 * pair], jnp.where(low, values, zero))
            + dot(z[2 * pair + 1], jnp.where(low, zero, values))
        )
    encoded = jnp.concatenate(parts, axis=1).astype(BF)
    got[0].wait()
    rounded = (lat[...].astype(F32) + dot(encoded, w3[...])).astype(BF)
    latent[...] = rounded
    wide = rounded.astype(F32)
    center = wide - jnp.mean(wide, axis=1, keepdims=True)
    spread = jnp.mean(center * center, axis=1, keepdims=True)
    normed[...] = (center * lax.rsqrt(spread + 1e-05)).astype(BF)
    for copy in later:
        copy.wait()


def attend_pair(both, keys, values, bias):
    low = low_half((1, 128))
    zero = jnp.zeros_like(both)
    rows = both.shape[0]
    stacked = jnp.concatenate([jnp.where(low, both, zero), jnp.where(low, zero, both)], axis=0)
    score = dot_t(stacked, keys)
    if bias is not None:
        score = (score.reshape(2, rows, -1) + bias[None]).reshape(2 * rows, -1)
    highest = jnp.max(score, axis=1, keepdims=True)
    expo = jnp.exp2(score - highest).astype(BF)
    total = dot(expo, jnp.concatenate([values, jnp.ones_like(values)], axis=1))
    highest = jnp.broadcast_to(highest, (2 * rows, 128))
    return (
        jnp.where(low, total[:rows, :128], total[rows:, :128]),
        jnp.where(low, total[:rows, 128:], total[rows:, 128:]),
        jnp.where(low, highest[:rows], highest[rows:]),
    )


def project_kernel(
    normed, win, wout, scale, wq, wk, wv, proc_w, dec_w,
    q, num, den, top, aq, bo, co, pw3, dw1, dw2, k, v, dw0, dw3, sems,
):
    got = fetch(dec_w, (0, 3), (dw0, dw3), sems.at[pl.ds(0, 2)])
    later = fetch(proc_w, (3,), (pw3,), sems.at[pl.ds(2, 1)])
    later += fetch(dec_w, (1, 2), (dw1, dw2), sems.at[pl.ds(3, 2)])
    rows = normed[...]
    q[...] = (dot(rows, wq[...]) * scale[1:2, :]).astype(BF)
    k[...] = dot(rows, wk[...]).astype(BF)
    v[...] = dot(rows, wv[...]).astype(BF)
    for pair in range(PAIRS):
        at = slice(pair * 128, pair * 128 + 128)
        num[:, at], den[:, at], top[:, at] = attend_pair(q[:, at], k[:, at], v[:, at], None)
    co[...] = dot_t(wout[...], win[...]).astype(BF)
    got[0].wait()
    aq[...] = (dot(win[...], dw0[...]) * scale[2:3, :]).astype(BF)
    got[1].wait()
    bo[...] = dot_t(dw3[...], wout[...]).astype(BF)
    for copy in later:
        copy.wait()


def window_half(side, ends, q, keys, values, num, den, top, latent, wo, bias, mixed, out):
    half, span = bias.shape
    row = lax.broadcasted_iota(jnp.int32, (half, span), 0)
    col = lax.broadcasted_iota(jnp.int32, (half, span), 1)
    begin = pl.multiple_of(side * half, half)
    place = col + begin
    place = jnp.where(place < WIN // 2, place, place + 2 * half)
    far = place - begin - row
    inside = (far >= 0) & (far <= WIN) & (place >= ends[0]) & (place < ends[1])
    bias[...] = jnp.where(inside, 0.0, NEG)
    these = pl.ds(begin, half)
    band = pl.ds(begin, span)
    for pair in range(PAIRS):
        at = slice(pair * 128, pair * 128 + 128)
        more, weight, highest = attend_pair(
            q[these, at], keys[band, at], values[band, at], bias[...]
        )
        own = top[these, at]
        joint = jnp.maximum(own, highest)
        own = jnp.exp2(own - joint)
        other = jnp.exp2(highest - joint)
        mixed[:, at] = (
            (num[these, at] * own + more * other) / (den[these, at] * own + weight * other)
        ).astype(BF)
    out[...] = (latent[these, :].astype(F32) + dot(mixed[...], wo[...])).astype(BF)


def window_outer_kernel(
    ends, q, num, den, top, near, far, latent, wk, wv, wo, outer, keys, values, bias, mixed
):
    halo = jnp.concatenate(sides(ends[2], near[...], far[...]), axis=0)
    keys[...] = dot(halo, wk[...]).astype(BF)
    values[...] = dot(halo, wv[...]).astype(BF)
    window_half(
        ends[2], ends, q, keys, values, num, den, top, latent, wo, bias, mixed, outer
    )


def window_inner_kernel(
    ends, q, num, den, top, keys, values, latent, wo, inner, bias, mixed
):
    window_half(
        1 - ends[2], ends, q, keys, values, num, den, top, latent, wo, bias, mixed, inner
    )


CHUNK = 128


def to_tiles(rows, weight, tiles, begin):
    count = rows.shape[0]
    for two in range(4):
        wide = dot(rows, weight[:, two * 256 : two * 256 + 256])
        for block in (2 * two, 2 * two + 1):
            tiles[pl.ds(begin * 8 + block, count, stride=8), :] = wide[
                :, block % 2 * 128 : block % 2 * 128 + 128
            ]


def prepare_kernel(ends, inner, outer, state, aq, wk, wv, q, k, v):
    own = jnp.concatenate(sides(ends[2], inner[...], outer[...]), axis=0)
    to_tiles(own, wk, k, 0)
    to_tiles(own, wv, v, 0)
    points = state.shape[1]
    for first in range(0, points, 512):
        to_tiles(state[:, first : first + 512].astype(F32).T.astype(BF), aq, q, first)


def decode_kernel(
    ends, idx, far, near, ko, vo, q, grid, bo, co, wk, wv, out, kf, vf, prod, wts, dec
):
    points = grid.shape[1]
    side = near.shape[0]
    halo = jnp.concatenate(sides(ends[2], near[...], far[...]), axis=0)
    for weight, tiles, own in ((wk, kf, ko), (wv, vf, vo)):
        tiles[side * 8 : side * 8 + own.shape[0], :] = own[...]
        for two in range(4):
            wide = dot(halo, weight[:, two * 256 : two * 256 + 256])
            for block in (2 * two, 2 * two + 1):
                both = wide[:, block % 2 * 128 : block % 2 * 128 + 128]
                tiles[pl.ds(block, side, stride=8), :] = both[:side]
                tiles[pl.ds(side * 8 + own.shape[0] + block, side, stride=8), :] = both[side:]
    head_row = lax.broadcasted_iota(jnp.int32, (256, 256), 0) // SIZE
    head_col = lax.broadcasted_iota(jnp.int32, (256, 256), 1) // SIZE
    ones = jnp.where(head_row == head_col, 1.0, 0.0).astype(BF)
    sub = 128

    def one_chunk(number, carry):
        first = pl.multiple_of(number * CHUNK, CHUNK)

        def tile_of(tiles, edge, at):
            return tiles[pl.ds(pl.multiple_of(idx[edge * points + first + at], 8), 8), :]

        for quad in range(0, CHUNK, 4):
            mine = [
                q[pl.ds(pl.multiple_of((first + quad + at) * 8, 8), 8), :] for at in range(4)
            ]
            for edge in range(3):
                terms = [mine[at] * tile_of(kf, edge, quad + at) for at in range(4)]
                place = slice(quad * 4, quad * 4 + 16)
                prod[edge, place, 0:128] = jnp.concatenate([terms[0], terms[2]], axis=0).astype(BF)
                prod[edge, place, 128:256] = jnp.concatenate([terms[1], terms[3]], axis=0).astype(BF)
        for begin in range(0, CHUNK * 4, sub):
            score = dot(prod[:, begin : begin + sub, :].reshape(3 * sub, 256), ones)
            score = [score[edge * sub : edge * sub + sub] for edge in range(3)]
            highest = jnp.maximum(jnp.maximum(score[0], score[1]), score[2])
            expo = [jnp.exp2(part - highest) for part in score]
            inverse = 1.0 / (expo[0] + expo[1] + expo[2])
            for edge in range(3):
                wts[edge, begin : begin + sub, :] = expo[edge] * inverse
        for at in range(CHUNK):
            top = at // 4 * 16 + (at % 4) // 2 * 8
            lane = at % 2 * 128
            total = None
            for edge in range(3):
                term = wts[edge, top : top + 8, lane : lane + 128] * tile_of(vf, edge, at)
                total = term if total is None else total + term
            dec[pl.ds(pl.multiple_of((first + at) * 8, 8), 8), :] = total
        return carry

    lax.fori_loop(0, points // CHUNK, one_chunk, 0)
    block = 256
    for first in range(0, points, block):
        wide = jnp.concatenate(
            [dec[pl.ds(first * 8 + part, block, stride=8), :] for part in range(8)], axis=1
        ).astype(BF)
        result = dot(wide, bo[...]).T + dot(co[...], grid[:, first : first + block])
        out[:, first : first + block] = result[: out.shape[0], :].astype(BF)


def pass_kernel(given, same):
    pass


def shape(dims, kind=BF):
    return jax.ShapeDtypeStruct(dims, kind)


def swap_near(inner):
    return lax.ppermute(inner, "narrow", [(0, 1), (1, 0)])


def swap_far(outer):
    axes = ("wide", "narrow")
    pairs = []
    for i in range(1, lax.axis_size(axes) - 1, 2):
        pairs += [(i, i + 1), (i + 1, i)]
    return lax.ppermute(outer, axes, pairs)


def on_device(
    grid_state,
    latent_init,
    enc_src,
    enc_count,
    dec_src,
    w_in,
    enc_w,
    proc_w,
    dec_w,
    w_out,
    logit_scale,
):
    points, channels = grid_state.shape
    rows, width = latent_init.shape
    slots = enc_src.shape[1]
    place = lax.axis_index(("wide", "narrow"))
    total = rows * lax.axis_size(("wide", "narrow"))
    weight = pltpu.VMEM((width, width), BF)
    dma = pltpu.SemaphoreType.DMA

    core = lax.axis_index("narrow")
    channel_rows = grid_state.T
    grid_far = swap_far(lax.dynamic_slice_in_dim(channel_rows, core * (points - BG), BG, 1))
    grid_near = swap_near(
        lax.dynamic_slice_in_dim(channel_rows, (1 - core) * (points - BG), BG, 1)
    )
    scale = jnp.repeat(logit_scale * (LOG2E / math.sqrt(SIZE)), SIZE, axis=1)
    enc_idx = jnp.clip(enc_src.T, 0, points + 2 * BG - 1).reshape(-1)
    live = jnp.arange(slots, dtype=jnp.int32)[:, None] < enc_count[None, :]
    bias = jnp.where(live, 0.0, NEG).astype(F32)
    bias = bias.reshape(slots, rows // 16, 16).transpose(1, 0, 2).reshape(rows // 16, slots * 16)
    dec_idx = jnp.clip(dec_src.T - (place * rows - BL), 0, rows + 2 * BL - 1).reshape(-1) * 8
    ends = jnp.stack([WIN // 2 - place * rows, total + WIN // 2 - place * rows, core])

    padded = shape((CPAD, width))
    qt, av, win, wout, grid = pl.pallas_call(
        fold_kernel,
        out_shape=(shape((HEADS, rows, CPAD)), padded, padded, padded, shape((CPAD, points))),
        in_specs=[VM, VM, VM, HBM, VM, VM] + [pl.BlockSpec(memory_space=pl.ANY)] * 4,
        out_specs=(VM,) * 5,
        scratch_shapes=[pltpu.VMEM((CPAD, width), F32)] + [weight] * 3 + [dma((3,))],
        compiler_params=params(50),
        cost_estimate=pl.CostEstimate(flops=2 * 10**9, bytes_accessed=8 * 2**20, transcendentals=0),
        name="fold",
    )(w_in, w_out.T, grid_state.T, enc_w, latent_init, scale, enc_idx, bias, dec_idx, ends)
    square = shape((width, width))
    latent, normed, pw0, pw1, pw2 = pl.pallas_call(
        encode_kernel,
        out_shape=(shape((rows, width)),) * 2 + (square,) * 3,
        in_specs=[SM] * 2 + [VM] * 7 + [HBM] * 2,
        out_specs=(VM,) * 5,
        scratch_shapes=[
            pltpu.VMEM((points + 2 * BG, CPAD), F32),
            pltpu.VMEM((CPAD, BG), F32),
            pltpu.VMEM((slots * 16, CPAD), F32),
            pltpu.VMEM((slots * 16, CPAD), F32),
            pltpu.VMEM((HEADS, rows, CPAD), BF),
            weight,
            dma((4,)),
        ],
        compiler_params=params(44),
        name="encode",
    )(ends, enc_idx, grid_near, grid, grid_far, qt, bias, av, latent_init, enc_w, proc_w)
    normed_far = swap_far(normed)
    normed_near = swap_near(normed)
    q, num, den, top, aq, bo, co, pw3, dw1, dw2 = pl.pallas_call(
        project_kernel,
        out_shape=(shape((rows, width)),)
        + (shape((rows, width), F32),) * 3
        + (shape((CPAD, width)), shape((width, CPAD)), shape((CPAD, CPAD)))
        + (square,) * 3,
        in_specs=[VM] * 7 + [HBM] * 2,
        out_specs=(VM,) * 10,
        scratch_shapes=[pltpu.VMEM((rows, width), BF)] * 2 + [weight] * 2 + [dma((5,))],
        compiler_params=params(36),
        cost_estimate=pl.CostEstimate(flops=3 * 10**9, bytes_accessed=12 * 2**20, transcendentals=0),
        name="project",
    )(normed, win, wout, scale, pw0, pw1, pw2, proc_w, dec_w)
    half_scratch = [
        pltpu.VMEM((rows // 2, WIN - rows // 2), F32),
        pltpu.VMEM((rows // 2, width), BF),
    ]
    wide = shape((WIN, width))
    mesh_outer, keys, values = pl.pallas_call(
        window_outer_kernel,
        out_shape=(shape((BL, width)), wide, wide),
        in_specs=[SM] + [VM] * 10,
        out_specs=(VM,) * 3,
        scratch_shapes=half_scratch,
        compiler_params=params(24),
        name="window_outer",
    )(ends, q, num, den, top, normed_near, normed_far, latent, pw1, pw2, pw3)
    mesh_far = swap_far(mesh_outer)
    mesh_inner = pl.pallas_call(
        window_inner_kernel,
        out_shape=shape((BL, width)),
        in_specs=[SM] + [VM] * 8,
        out_specs=VM,
        scratch_shapes=half_scratch,
        compiler_params=params(24),
        cost_estimate=pl.CostEstimate(flops=3 * 10**9, bytes_accessed=12 * 2**20, transcendentals=0),
        name="window_inner",
    )(ends, q, num, den, top, keys, values, latent, pw3)
    mesh_near = swap_near(mesh_inner)
    mesh_far = pl.pallas_call(
        pass_kernel,
        out_shape=shape((BL, width)),
        in_specs=[pl.BlockSpec(memory_space=pl.ANY)],
        out_specs=pl.BlockSpec(memory_space=pl.ANY),
        input_output_aliases={0: 0},
        compiler_params=params(16),
        name="pass",
    )(mesh_far)
    nodes = rows + 2 * BL
    dq, dk, dv = pl.pallas_call(
        prepare_kernel,
        out_shape=(
            shape((points * 8, 128), F32),
            shape((rows * 8, 128), F32),
            shape((rows * 8, 128), F32),
        ),
        in_specs=[SM] + [VM] * 6,
        out_specs=(VM,) * 3,
        compiler_params=params(24),
        cost_estimate=pl.CostEstimate(flops=10**6, bytes_accessed=2**16, transcendentals=0),
        name="prepare",
    )(ends, mesh_inner, mesh_outer, grid, aq, dw1, dw2)
    out = pl.pallas_call(
        decode_kernel,
        out_shape=shape((channels, points)),
        in_specs=[SM] * 2 + [VM] * 10,
        out_specs=VM,
        scratch_shapes=[
            pltpu.VMEM((nodes * 8, 128), F32),
            pltpu.VMEM((nodes * 8, 128), F32),
            pltpu.VMEM((3, CHUNK * 4, 256), BF),
            pltpu.VMEM((3, CHUNK * 4, 256), F32),
            pltpu.VMEM((points * 8, 128), F32),
        ],
        compiler_params=params(32),
        name="decode",
    )(ends, dec_idx, mesh_far, mesh_near, dk, dv, dq, grid, bo, co, dw1, dw2)
    return out.T


def solution(mesh):
    both = ("wide", "narrow")
    placed = (
        P(both, None),
        P(both, None),
        P(both, None),
        P(both),
        P(both, None),
        P(),
        P(),
        P(),
        P(),
        P(),
        P(),
    )
    return jax.shard_map(
        on_device,
        mesh=mesh,
        in_specs=placed,
        out_specs=P(both, None),
        check_vma=False,
    )
```
